128 devices in a mesh: section: 2 (over core), dp: 8 (over z, y_lo), tensor: 8 (over y_hi, x).
Axes of the slice: x: 4, y: 4 (y_hi: 2, y_lo: 2; y = y_hi * 2 + y_lo), z: 4, core: 2. Of those that a mesh axis runs over, the one named last changes fastest.
Arguments:
- inputs: bfloat16 [2, 1, 1024, 1024], P(None, None, 'dp'), may hold values from -6 to 6
- cotangent: bfloat16 [2, 1, 1024, 1024], P(None, None, 'dp'), may hold values from -6 to 6
- query_key_value_weight: bfloat16 [2, 1024, 3, 1024], P('section', 'dp', None, 'tensor'), may hold values from -0.1875 to 0.1875
- attention_out_weight: bfloat16 [2, 1024, 1024], P('section', 'tensor', 'dp'), may hold values from -0.5 to 0.5
- up_weight: bfloat16 [2, 1024, 4096], P('section', 'dp', 'tensor'), may hold values from -0.1875 to 0.1875
- down_weight: bfloat16 [2, 4096, 1024], P('section', 'tensor', 'dp'), may hold values from -0.09375 to 0.09375
- ln_gain: bfloat16 [2, 2, 1024], P('section', None, 'dp'), may hold values from 0.099609375 to 1.8984375
- ln_bias: bfloat16 [2, 2, 1024], P('section', None, 'dp'), may hold values from -3 to 3
- in_bias: bfloat16 [2, 2, 1024], P('section', None, 'tensor'), may hold values from -3 to 3
- output_biases: bfloat16 [2, 2, 1024], P('section', None, 'dp'), may hold values from -3 to 3
- expand_bias: bfloat16 [2, 4096], P('section', 'tensor'), may hold values from -3 to 3
Outputs:
- activations: bfloat16 [2, 2, 1, 1024, 1024], P('section', None, None, 'dp')
- input_grads: bfloat16 [2, 2, 1, 1024, 1024], P('section', None, None, 'dp')
- grad_qkv: float32 [2, 1024, 3, 1024], P('section', 'dp', None, 'tensor')
- grad_out: float32 [2, 1024, 1024], P('section', 'tensor', 'dp')
- grad_up: float32 [2, 1024, 4096], P('section', 'dp', 'tensor')
- grad_down: float32 [2, 4096, 1024], P('section', 'tensor', 'dp')
- grad_ln_gain: float32 [2, 2, 1024], P('section', None, 'dp')
- grad_ln_bias: float32 [2, 2, 1024], P('section', None, 'dp')
- grad_in_bias: float32 [2, 2, 1024], P('section', None, 'tensor')
- grad_out_bias: float32 [2, 2, 1024], P('section', None, 'dp')
- grad_up_bias: float32 [2, 4096], P('section', 'tensor')
The draws below stay inside these ranges and needn't reach their ends.
All inputs are finite; a program needn't handle non-finite values.
Results may differ from the reference program's by a relative error of at most 0.02.
Values may be sent and summed in bfloat16 or wider, within the bound.
No kernel may reach another device: no remote copies, remote signals or barrier semaphores. Data moves between devices by JAX's collectives and lax.ppermute only.
A program may use at most 128 MiB of HBM per device.

```python
import math
import jax
import jax.numpy as jnp
from jax import lax

D = 1024
H = 16
FF = 4096
HD = 64
LAYERS = 2
MICRO = 2
SEQ_LEN = 1024
SEQS = 1


def block_levels(rng, extent, split, smallest, high):
    def one(axis_at, shards_of):
        steps = jax.random.uniform(jax.random.fold_in(jax.random.fold_in(rng, 6), axis_at), (shards_of,), jnp.float32, smallest / len(split), high / len(split))
        return jnp.repeat(jnp.exp(steps), extent[axis_at] // shards_of).reshape((-1,) + (1,) * (len(extent) - axis_at - 1))

    loudness = one(*split[0])
    for cut in split[1:]:
        loudness = loudness * one(*cut)
    return loudness


def gaussian(stream_key, extent, scale, most, pieces=(), held_as=jnp.bfloat16):
    result = scale * jax.random.normal(stream_key, extent, jnp.float32)
    if pieces:
        result = result * block_levels(stream_key, extent, pieces, -0.22, 0.18)
    return jnp.clip(result, -most, most).astype(held_as)


def setup_inputs(seed: int = 0) -> dict:
    arg_keys = jax.random.split(jax.random.key(seed), 12)
    return {
        "inputs": gaussian(arg_keys[0], (MICRO, SEQS, SEQ_LEN, D), 1.0, 6.0, ((2, 8),)),
        "cotangent": gaussian(arg_keys[1], (MICRO, SEQS, SEQ_LEN, D), 1.0, 6.0, ((2, 8),)),
        "query_key_value_weight": gaussian(arg_keys[2], (LAYERS, D, 3, D), D ** -0.5, 0.1875, ((0, 2), (1, 8), (3, 8))),
        "attention_out_weight": gaussian(arg_keys[3], (LAYERS, D, D), (D // 8) ** -0.5, 0.5, ((0, 2), (1, 8), (2, 8))),
        "up_weight": gaussian(arg_keys[4], (LAYERS, D, FF), D ** -0.5, 0.1875, ((0, 2), (1, 8), (2, 8))),
        "down_weight": gaussian(arg_keys[5], (LAYERS, FF, D), FF ** -0.5, 0.09375, ((0, 2), (1, 8), (2, 8))),
        "ln_gain": jnp.clip(1.0 + 0.18 * jax.random.normal(arg_keys[6], (LAYERS, 2, D), jnp.float32), 0.099609375, 1.8984375).astype(jnp.bfloat16),
        "ln_bias": gaussian(arg_keys[7], (LAYERS, 2, D), 0.5, 3.0, ((0, 2), (2, 8))),
        "in_bias": gaussian(arg_keys[8], (LAYERS, 2, D), 0.5, 3.0, ((0, 2), (2, 8))),
        "output_biases": gaussian(arg_keys[9], (LAYERS, 2, D), 0.5, 3.0, ((0, 2), (2, 8))),
        "expand_bias": gaussian(arg_keys[10], (LAYERS, FF), 0.5, 3.0, ((0, 2), (1, 8))),
    }


EPSILON = 1e-05
MASKED = -1e+30

@jax.custom_vjp
def low(v):
    return lax.optimization_barrier(v.astype(jnp.bfloat16)).astype(jnp.float32)

@jax.custom_vjp
def lower_gradient(v):
    return v

def low_keep(v):
    return (low(v), None)

def low_pass(kept, grad):
    return (grad,)

def back_keep(v):
    return (v, None)

def back_low(kept, grad):
    return (low(grad),)
low.defvjp(low_keep, low_pass)
lower_gradient.defvjp(back_keep, back_low)

def layer_norm(layer_entry, norm_gain, norm_shift):
    row_mean = lax.optimization_barrier(jnp.mean(layer_entry, axis=-1, keepdims=True))
    centred = layer_entry - row_mean
    variance = lax.optimization_barrier(jnp.mean(centred * centred, axis=-1, keepdims=True))
    return centred * lax.rsqrt(variance + EPSILON) * norm_gain + norm_shift

def gelu_tanh(argument):
    return 0.5 * argument * (1.0 + jnp.tanh(0.7978845608028654 * (argument + 0.044715 * argument * argument * argument)))

def matrix_product(form, left_side, right_side):
    return jnp.einsum(form, left_side, right_side, precision=lax.Precision.HIGHEST)

def layer_apply(layer_entry, query_key_value_weight, attention_out_weight, up_weight, down_weight, ln_gain, ln_bias, in_bias, output_biases, expand_bias):
    seq_count, length, width = layer_entry.shape
    first_normalized = low(layer_norm(layer_entry, ln_gain[0], ln_bias[0]))
    projected_rows = matrix_product('zya,apc->zypc', first_normalized, query_key_value_weight)
    queries = low(lower_gradient(projected_rows[:, :, 0] + in_bias[0]))
    key_rows = low(lower_gradient(projected_rows[:, :, 1]))
    value_rows = low(lower_gradient(projected_rows[:, :, 2] + in_bias[1]))
    query_heads = queries.reshape(seq_count, length, H, HD)
    key_heads = key_rows.reshape(seq_count, length, H, HD)
    value_heads = value_rows.reshape(seq_count, length, H, HD)
    raw_scores = matrix_product('sqhe,skhe->shqk', query_heads, key_heads) * (1.0 / math.sqrt(HD))
    scores = lower_gradient(raw_scores)
    query_pos = lax.broadcasted_iota(jnp.int32, (length, length), 0)
    key_pos = lax.broadcasted_iota(jnp.int32, (length, length), 1)
    scores = jnp.where((key_pos <= query_pos)[None, None], scores, MASKED)
    row_max = lax.optimization_barrier(jnp.max(scores, axis=-1, keepdims=True))
    exponent = jnp.exp(scores - row_max)
    probability = low(exponent / lax.optimization_barrier(jnp.sum(exponent, axis=-1, keepdims=True)))
    mixture = matrix_product('shqk,skhe->sqhe', probability, value_heads).reshape(seq_count, length, width)
    attention_result = low(lower_gradient(mixture))
    residual_middle = layer_entry + lower_gradient(matrix_product('ckq,qw->ckw', attention_result, attention_out_weight) + output_biases[0])
    second_normalized = low(layer_norm(residual_middle, ln_gain[1], ln_bias[1]))
    hidden_preactivation = lower_gradient(matrix_product('ugw,wo->ugo', second_normalized, up_weight) + expand_bias)
    activated_hidden = low(gelu_tanh(hidden_preactivation))
    layer_result = residual_middle + lower_gradient(matrix_product('gam,mq->gaq', activated_hidden, down_weight) + output_biases[1])
    return low(lower_gradient(layer_result))

def reference(inputs, cotangent, query_key_value_weight, attention_out_weight, up_weight, down_weight, ln_gain, ln_bias, in_bias, output_biases, expand_bias):
    params = (query_key_value_weight, attention_out_weight, up_weight, down_weight, ln_gain, ln_bias, in_bias, output_biases, expand_bias)
    lower = tuple((parameter[0].astype(jnp.float32) for parameter in params))
    higher = tuple((parameter[1].astype(jnp.float32) for parameter in params))
    lower_sums = tuple((jnp.zeros_like(parameter) for parameter in lower))
    higher_sums = tuple((jnp.zeros_like(parameter) for parameter in higher))
    lower_acts = []
    higher_acts = []
    lower_grads = []
    higher_grads = []
    for micro_index in range(MICRO):
        layer_entry = inputs[micro_index].astype(jnp.float32)
        middle_out, lower_back = jax.vjp(layer_apply, layer_entry, *lower)
        final_out, higher_back = jax.vjp(layer_apply, middle_out, *higher)
        higher_terms = higher_back(cotangent[micro_index].astype(jnp.float32))
        lower_terms = lower_back(higher_terms[0])
        lower_sums = tuple((summed + added for summed, added in zip(lower_sums, lower_terms[1:])))
        higher_sums = tuple((summed + added for summed, added in zip(higher_sums, higher_terms[1:])))
        lower_acts.append(middle_out)
        higher_acts.append(final_out)
        lower_grads.append(lower_terms[0])
        higher_grads.append(higher_terms[0])
    activations = jnp.stack([jnp.stack(lower_acts), jnp.stack(higher_acts)]).astype(jnp.bfloat16)
    input_grads = jnp.stack([jnp.stack(lower_grads), jnp.stack(higher_grads)]).astype(jnp.bfloat16)
    stacked = tuple((jnp.stack([left_sum, right_sum]) for left_sum, right_sum in zip(lower_sums, higher_sums)))
    return (activations, input_grads, stacked[0], stacked[1], stacked[2], stacked[3], stacked[4], stacked[5], stacked[6], stacked[7], stacked[8])
```

```python
import math

import jax
import jax.numpy as jnp
from jax import lax
from jax.sharding import Mesh, PartitionSpec as P

HD = 64
EPSILON = 1e-05
MASKED = -1e30
BF = jnp.bfloat16
F32 = jnp.float32
CHIPS = ("yh", "z", "yl")
TOKENS = ("z", "yl", "yh")


def swap_cores(v):
    return lax.ppermute(v, "s", [(0, 1), (1, 0)])


def spread(piece):
    copies = jnp.broadcast_to(piece, (16, *piece.shape))
    return lax.all_to_all(copies, CHIPS, 0, 0, tiled=True)


def sum_over_x(part):
    got = [
        lax.ppermute(part, "x", [(i, i ^ k) for i in range(4)]).astype(F32) for k in (1, 3, 2)
    ]
    return (part.astype(F32) + got[0]) + (got[2] + got[1])


def layer_norm(v, gain, shift):
    mean = jnp.mean(v, axis=-1, keepdims=True)
    centred = v - mean
    variance = jnp.mean(centred * centred, axis=-1, keepdims=True)
    return centred * lax.rsqrt(variance + EPSILON) * gain + shift


def layer_norm_back(v, gain, grad):
    mean = jnp.mean(v, axis=-1, keepdims=True)
    centred = v - mean
    variance = jnp.mean(centred * centred, axis=-1, keepdims=True)
    inverse = lax.rsqrt(variance + EPSILON)
    xhat = centred * inverse
    d = grad * gain
    back = inverse * (
        d - jnp.mean(d, axis=-1, keepdims=True) - xhat * jnp.mean(d * xhat, axis=-1, keepdims=True)
    )
    return back, jnp.sum(grad * xhat, axis=0), jnp.sum(grad, axis=0)


def gelu(u):
    return 0.5 * u * (1.0 + jnp.tanh(0.7978845608028654 * (u + 0.044715 * u * u * u)))


def gelu_slope(u):
    t = jnp.tanh(0.7978845608028654 * (u + 0.044715 * u * u * u))
    return 0.5 * (1.0 + t) + 0.5 * u * (1.0 - t * t) * 0.7978845608028654 * (
        1.0 + 3.0 * 0.044715 * u * u
    )


def ein(form, a, b):
    return jnp.einsum(form, a, b, preferred_element_type=F32)


def forward(x, wa, wf, par):
    ln, qb, vb, ub = par
    n1 = layer_norm(x, ln[0], ln[2]).astype(BF)
    proj = ein("cd,hdk->hck", n1, wa[:, :, :192])
    q = (proj[:, :, :64] + qb[:, None]).astype(BF)
    k = proj[:, :, 64:128].astype(BF)
    v = (proj[:, :, 128:] + vb[:, None]).astype(BF)
    kv = jnp.concatenate([k, v], axis=-1)
    kv = lax.all_to_all(jnp.broadcast_to(kv, (16, *kv.shape)), TOKENS, 0, 0, tiled=True)
    kv = jnp.moveaxis(kv, 0, 1).reshape(4, 1024, 128)
    scores = ein("hqe,hke->hqk", q, kv[:, :, :64]) * (1.0 / math.sqrt(HD))
    first = lax.axis_index(TOKENS) * 64
    qpos = first + lax.broadcasted_iota(jnp.int32, (64, 1024), 0)
    kpos = lax.broadcasted_iota(jnp.int32, (64, 1024), 1)
    scores = jnp.where(kpos <= qpos, scores, MASKED)
    top = jnp.max(scores, axis=-1, keepdims=True)
    e = jnp.exp(scores - top)
    p = e / jnp.sum(e, axis=-1, keepdims=True)
    att = ein("hqk,hke->hqe", p.astype(BF), kv[:, :, 64:]).astype(BF)
    part = ein("hce,hde->cd", att, wa[:, :, 192:]).astype(BF)
    mid = x + (sum_over_x(part) + ln[4])
    n2 = layer_norm(mid, ln[1], ln[3]).astype(BF)
    pre = ein("cd,hdf->hcf", n2, wf[:, :, :256]) + ub[:, None]
    act = gelu(pre).astype(BF)
    part = ein("hcf,hdf->cd", act, wf[:, :, 256:]).astype(BF)
    y = (mid + (sum_over_x(part) + ln[5])).astype(BF)
    return y, (x, n1, q, kv, p, att, mid, n2, pre, act)


def backward(g, saved, wa, wf, par):
    x, n1, q, kv, p, att, mid, n2, pre, act = saved
    ln = par[0]
    gl = g.astype(BF)
    gf_down = ein("cd,hcf->hdf", gl, act)
    ob1 = jnp.sum(g, axis=0)
    dact = ein("cd,hdf->hcf", gl, wf[:, :, 256:])
    dpre = (dact * gelu_slope(pre)).astype(BF)
    gub = jnp.sum(dpre.astype(F32), axis=1)
    gf_up = ein("cd,hcf->hdf", n2, dpre)
    part = ein("hcf,hdf->cd", dpre, wf[:, :, :256]).astype(BF)
    back, gg1, gs1 = layer_norm_back(mid, ln[1], sum_over_x(part))
    dmid = g + back
    bg = dmid.astype(BF)
    ob0 = jnp.sum(bg.astype(F32), axis=0)
    ga_out = ein("cd,hce->hde", bg, att)
    datt = ein("cd,hde->hce", bg, wa[:, :, 192:]).astype(BF)
    dp = ein("hqe,hke->hqk", datt, kv[:, :, 64:])
    ds = (p * (dp - jnp.sum(p * dp, axis=-1, keepdims=True))).astype(BF)
    dq = (ein("hqk,hke->hqe", ds, kv[:, :, :64]) * (1.0 / math.sqrt(HD))).astype(BF)
    dk = ein("hqk,hqe->hke", ds, q) * (1.0 / math.sqrt(HD))
    dv = ein("hqk,hqe->hke", p.astype(BF), datt)
    dkv = jnp.concatenate([dk, dv], axis=-1).astype(BF).reshape(4, 16, 64, 128)
    dkv = lax.all_to_all(jnp.moveaxis(dkv, 1, 0), TOKENS, 0, 0, tiled=True)
    dkv = jnp.sum(dkv.astype(F32), axis=0).astype(BF)
    dproj = jnp.concatenate([dq, dkv], axis=-1)
    gib = jnp.sum(dproj.astype(F32), axis=1)
    ga_qkv = ein("cd,hcj->hdj", n1, dproj)
    part = ein("hcj,hdj->cd", dproj, wa[:, :, :192]).astype(BF)
    back, gg0, gs0 = layer_norm_back(x, ln[0], sum_over_x(part))
    dx = (dmid + back).astype(BF)
    ga = jnp.concatenate([ga_qkv, ga_out], axis=-1).astype(BF)
    gf = jnp.concatenate([gf_up, gf_down], axis=-1).astype(BF)
    rows = jnp.stack([gg0, gg1, gs0, gs1, ob0, ob1])
    return dx, ga, gf, (rows, gib, gub)


def by_owner(rows, gib, gub, s):
    dpart = jnp.moveaxis(rows.reshape(6, 8, 128), 1, 0)
    def natural(v):
        pair = v.reshape(2, 2, -1)
        return jnp.where(s == 0, pair, pair[::-1])
    qb = natural(gib[:, :64])
    vb = natural(gib[:, 128:])
    ub = natural(gub)
    tpart = jnp.concatenate(
        [
            jnp.moveaxis(qb, 0, 1).reshape(2, 1, 128),
            jnp.moveaxis(vb, 0, 1).reshape(2, 1, 128),
            jnp.moveaxis(ub, 0, 1).reshape(2, 4, 128),
        ],
        axis=1,
    )
    both = jnp.concatenate(
        [
            jnp.broadcast_to(dpart[None], (2, 8, 6, 128)),
            jnp.broadcast_to(tpart[:, None], (2, 8, 6, 128)),
        ],
        axis=2,
    )
    return both.reshape(16, 6, 256).astype(BF)


def reduce_layer(ga, gf, small):
    ga, gf = ga.reshape(2, 16, 128, 256), gf.reshape(2, 16, 128, 512)
    mf = (gf[0].astype(F32) + swap_cores(gf[1]).astype(F32)).astype(BF)
    rf = jnp.sum(lax.all_to_all(mf, CHIPS, 0, 0, tiled=True).astype(F32), axis=0)
    ma = (ga[0].astype(F32) + swap_cores(ga[1]).astype(F32)).astype(BF)
    sm = (small.astype(F32) + swap_cores(small).astype(F32)).astype(BF)
    ma = jnp.concatenate([ma, sm, jnp.zeros((16, 10, 256), BF)], axis=1)
    ra = jnp.sum(lax.all_to_all(ma, CHIPS, 0, 0, tiled=True).astype(F32), axis=0)
    return jnp.concatenate([ra[:128], rf], axis=1), ra[128:134].reshape(12, 128)


def local(inputs, cotangent, wqkv, wout, wup, wdown, gain, shift, inb, outb, upb):
    s = lax.axis_index("s")
    yh = lax.axis_index("yh")
    attn = jnp.concatenate([wqkv[0], wout[0].T[:, None]], axis=1).reshape(128, 4, 2, 64)
    attn = jnp.moveaxis(attn, 2, 0).reshape(2, 128, 256)
    up = jnp.moveaxis(wup[0].reshape(128, 2, 256), 1, 0)
    down = jnp.moveaxis(wdown[0].T.reshape(128, 2, 256), 1, 0)
    small = jnp.concatenate([gain[0], shift[0], outb[0], inb[0], upb[0].reshape(4, 128)])
    small = jnp.broadcast_to(small.reshape(1, 2, 768), (2, 2, 768))
    own = jnp.concatenate([attn, up, down], axis=2)
    own = jnp.concatenate([own, small, jnp.zeros((2, 14, 768), BF)], axis=1)
    both = lax.all_to_all(own, "s", 0, 0, tiled=True)
    urgent = jnp.concatenate(
        [both[0, :128, :256], both[:, 128:130].reshape(12, 256), jnp.zeros((4, 256), BF)]
    )
    g0a = spread(urgent)
    g0f = spread(both[0, :128, 256:])
    g1 = spread(both[1, :128])

    def whole(mine):
        mine = mine.reshape(2, 1024, -1)
        return jnp.concatenate([mine, swap_cores(mine)])

    wa = [whole(g0a[:, :128]), whole(g1[:, :, :256])]
    wf = [whole(g0f), whole(g1[:, :, 256:])]
    par = g0a[:, 128:140].reshape(2, 8, 2, 12, 128).astype(F32)
    pars = []
    for l in range(2):
        ln = jnp.moveaxis(par[0, :, l, :6], 0, 1).reshape(6, 1024)
        def split(v):
            v = jnp.moveaxis(v.reshape(2, 2, -1), 1, 0)
            return jnp.where(s == 0, v, v[::-1]).reshape(4, -1)
        pars.append(
            (ln, split(par[:, 0, l, 6]), split(par[:, 0, l, 7]), split(par[:, 0, l, 8:12]))
        )
    def own_rows(v):
        return lax.dynamic_slice(v, (s, 0, yh * 64, 0), (1, 1, 64, 1024)).reshape(64, 1024)

    y0, saved0 = forward(own_rows(inputs).astype(F32), wa[0], wf[0], pars[0])
    y1, saved1 = forward(y0.astype(F32), wa[1], wf[1], pars[1])

    def collect(a, b):
        rows = jnp.broadcast_to(jnp.stack([a, b])[:, None], (2, 2, 64, 1024))
        rows = lax.all_to_all(rows.reshape(4, 64, 1024), ("s", "yh"), 0, 0, tiled=True)
        return rows.reshape(1, 2, 1, 128, 1024)

    acts = collect(y0, y1)
    d1, ga1, gf1, sm1 = backward(own_rows(cotangent).astype(F32), saved1, wa[1], wf[1], pars[1])
    r1, t1 = reduce_layer(ga1, gf1, by_owner(*sm1, s))
    d0, ga0, gf0, sm0 = backward(d1.astype(F32), saved0, wa[0], wf[0], pars[0])
    r0, t0 = reduce_layer(ga0, gf0, by_owner(*sm0, s))
    grads = collect(d0, d1)
    w = lax.all_to_all(jnp.stack([r0, r1]), "s", 0, 0, tiled=True)
    t = jnp.where(s == 0, t0, t1)
    at = jnp.moveaxis(w[:, :, :256].reshape(2, 128, 4, 64), 0, 2).reshape(128, 4, 128)
    gup = jnp.moveaxis(w[:, :, 256:512], 0, 1).reshape(1, 128, 512)
    gdown = jnp.moveaxis(w[:, :, 512:], 0, 1).reshape(128, 512).T
    return (
        acts,
        grads,
        at[None, :, :3],
        at[None, :, 3].swapaxes(1, 2),
        gup,
        gdown[None],
        t[None, 0:2],
        t[None, 2:4],
        t[None, 6:8],
        t[None, 4:6],
        t[8:12].reshape(1, 512),
    )


def solution(mesh):
    parts = Mesh(mesh.devices.reshape(2, 4, 2, 2, 4), ("s", "z", "yl", "yh", "x"))
    dp, tp = ("z", "yl"), ("yh", "x")
    return jax.shard_map(
        local,
        mesh=parts,
        in_specs=(
            P(None, None, dp, None),
            P(None, None, dp, None),
            P("s", dp, None, tp),
            P("s", tp, dp),
            P("s", dp, tp),
            P("s", tp, dp),
            P("s", None, dp),
            P("s", None, dp),
            P("s", None, tp),
            P("s", None, dp),
            P("s", tp),
        ),
        out_specs=(
            P("s", None, None, dp, None),
            P("s", None, None, dp, None),
            P("s", dp, None, tp),
            P("s", tp, dp),
            P("s", dp, tp),
            P("s", tp, dp),
            P("s", None, dp),
            P("s", None, dp),
            P("s", None, tp),
            P("s", None, dp),
            P("s", tp),
        ),
        check_vma=False,
    )
```

```python
import functools
import math

import jax
import jax.numpy as jnp
from jax import lax
from jax.experimental import pallas as pl
from jax.experimental.pallas import tpu as pltpu
from jax.sharding import Mesh, PartitionSpec as P

EPSILON = 1e-05
MASKED = -1e30
SCALE = 1.0 / math.sqrt(64)
BF = jnp.bfloat16
F32 = jnp.float32
CHIPS = ("z", "yl", "yh")
ROWS = 64
D = 1024


def sds(*shape, dtype=BF):
    return jax.ShapeDtypeStruct(shape, dtype)


def call(kernel, outs, ins, us=3):
    specs, arrays = [], []
    for item in ins:
        if isinstance(item, tuple):
            array, block, index = item
            if block is None:
                specs.append(pl.BlockSpec(memory_space=pltpu.SMEM))
            else:
                specs.append(pl.BlockSpec(block, functools.partial(lambda at, i: at, index)))
        else:
            array = item
            specs.append(
                pl.BlockSpec(
                    array.shape, functools.partial(lambda n, i: (0,) * n, array.ndim)
                )
            )
        arrays.append(array)
    out_specs = [
        pl.BlockSpec(o.shape, functools.partial(lambda n, i: (0,) * n, len(o.shape)))
        for o in outs
    ]
    return pl.pallas_call(
        kernel,
        grid=(1,),
        out_shape=outs,
        in_specs=specs,
        out_specs=out_specs,
        compiler_params=pltpu.CompilerParams(vmem_limit_bytes=48 * 1024 * 1024),
        cost_estimate=pl.CostEstimate(
            flops=0, bytes_accessed=us * 3_000_000, transcendentals=0
        ),
    )(*arrays)


def nn(a, b):
    return jnp.dot(a, b, preferred_element_type=F32)


def nt(a, b):
    return lax.dot_general(a, b, (((1,), (1,)), ((), ())), preferred_element_type=F32)


def tn(a, b):
    return lax.dot_general(a, b, (((0,), (0,)), ((), ())), preferred_element_type=F32)


def heads():
    return [(k, side, yh) for k, (side, yh) in enumerate([(0, 0), (0, 1), (1, 0), (1, 1)])]


def attn_tile(ref, yh):
    if len(ref.shape) == 5:
        return ref[0, :, yh, 0:128, :].reshape(D, 256)
    return ref[:, yh, 0:128, :].reshape(D, 256)


def ffn_tile(ref, yh, part):
    return ref[:, yh, 0:128, part * 256 : part * 256 + 256].reshape(D, 256)


def low_half(v):
    lane = lax.broadcasted_iota(jnp.int32, v.shape, 1)
    return jnp.where(lane < 64, v, 0.0)


def high_half(v):
    lane = lax.broadcasted_iota(jnp.int32, v.shape, 1)
    return jnp.where(lane >= 64, v, 0.0)


def mean_of(v):
    return jnp.sum(v, axis=-1, keepdims=True) * (1.0 / D)


def normal(v):
    centred = v - mean_of(v)
    inverse = lax.rsqrt(mean_of(centred * centred) + EPSILON)
    return centred * inverse, inverse


def layer_norm(v, gain, shift):
    return normal(v)[0] * gain + shift


def layer_norm_back(v, gain, grad):
    xhat, inverse = normal(v)
    d = grad * gain
    back = inverse * (d - mean_of(d) - xhat * mean_of(d * xhat))
    return (
        back,
        jnp.sum(grad * xhat, axis=0, keepdims=True),
        jnp.sum(grad, axis=0, keepdims=True),
    )


def gelu(u):
    return 0.5 * u * (1.0 + jnp.tanh(0.7978845608028654 * (u + 0.044715 * u * u * u)))


def gelu_slope(u):
    t = jnp.tanh(0.7978845608028654 * (u + 0.044715 * u * u * u))
    return 0.5 * (1.0 + t) + 0.5 * u * (1.0 - t * t) * (
        0.7978845608028654 * (1.0 + 3.0 * 0.044715 * u * u)
    )


def total(parts):
    a, b, c, d = [p[...].astype(F32) for p in parts]
    return (a + b) + (c + d)


def ln_row(lnp, layer, which, kind):
    return lnp[which, layer * 8 + 4 + kind : layer * 8 + 5 + kind, :]


def project(x, lnp, bias, wm, wo, layer, n1, q, kv):
    normed = layer_norm(x, ln_row(lnp, layer, 0, 0), ln_row(lnp, layer, 0, 1)).astype(BF)
    n1[...] = normed
    for k, side, yh in heads():
        tile = nn(normed, attn_tile((wm, wo)[side], yh))
        tile = tile + bias[yh, layer * 8 + side : layer * 8 + side + 1, :]
        q[k] = low_half(tile[:, 128:]).astype(BF)
        pair = tile[:, :128].astype(BF)
        for g in range(16):
            kv[g, kv.shape[1] - ROWS :, k * 128 : k * 128 + 128] = pair


def pack_kernel(qkv, out, up, down, gain, shift, inb, outb, upb, msg, ffn):
    wt = out[...].astype(F32).T
    dt = down[...].astype(F32).T
    inb_, gain_, shift_, outb_ = [r[...].astype(F32) for r in (inb, gain, shift, outb)]
    upb_ = upb[...].astype(F32)
    zero = jnp.zeros((1, 64), F32)
    def flat(v):
        return jnp.concatenate([v[0:1], v[1:2]], axis=1)
    rows = []
    for j in range(2):
        cols = slice(j * 64, j * 64 + 64)
        rows.append(jnp.concatenate([zero, inb_[1:2, cols], inb_[0:1, cols], zero], axis=1))
    ups = [upb_[:, :256], upb_[:, 256:]]
    tail = [flat(gain_), flat(shift_), flat(outb_), jnp.zeros((9, 256), F32)]
    for j in range(2):
        cols = slice(j * 64, j * 64 + 64)
        tile = jnp.concatenate(
            [
                qkv[1, :, cols].astype(F32),
                qkv[2, :, cols].astype(F32),
                qkv[0, :, cols].astype(F32),
                wt[:, cols],
            ],
            axis=1,
        ).astype(BF)
        small = jnp.concatenate([rows[j], rows[1 - j], ups[j], ups[1 - j], *tail]).astype(BF)
        for g in range(16):
            msg[j, g, 0:128, :] = tile
            msg[j, g, 128:144, :] = small
        ffn[j, :, 0:256] = up[:, j * 256 : j * 256 + 256]
        ffn[j, :, 256:512] = dt[:, j * 256 : j * 256 + 256].astype(BF)


def first_kernel(x, params, wm, wo, piece, n1, q, msg, lnp, bias):
    for layer in range(2):
        blocks = [params[layer, d, 0].astype(F32) for d in range(8)]
        for half in range(2):
            cols = slice(half * 128, half * 128 + 128)
            lnp[half, layer * 8 : layer * 8 + 8, :] = jnp.concatenate(
                [b[0:8, cols] for b in blocks], axis=1
            )
        for yh in range(2):
            bias[yh, layer * 8 : layer * 8 + 8, :] = params[layer, 0, yh].astype(F32)[0:8]
    project(x[...].astype(F32), lnp, bias, wm, wo, 0, n1, q, msg)
    rest = piece[...]
    for g in range(16):
        msg[g, 0:128, :] = rest


def next_kernel(mid, p0, p1, p2, p3, lnp, bias, wm, wo, y, n1, q, msg):
    out = (mid[...] + (total((p0, p1, p2, p3)) + ln_row(lnp, 0, 1, 2))).astype(BF)
    y[...] = out
    project(out.astype(F32), lnp, bias, wm, wo, 1, n1, q, msg)


def attend_kernel(first, q, kv, wm, wo, part, prob, att):
    length = 16 * ROWS
    qpos = first[0] + lax.broadcasted_iota(jnp.int32, (ROWS, length), 0)
    kpos = lax.broadcasted_iota(jnp.int32, (ROWS, length), 1)
    allowed = kpos <= qpos
    acc = None
    for k, side, yh in heads():
        pair = kv[:, :, k * 128 : k * 128 + 128].reshape(length, 128)
        scores = jnp.where(allowed, nt(q[k], pair) * SCALE, MASKED)
        e = jnp.exp(scores - jnp.max(scores, axis=-1, keepdims=True))
        p = e / jnp.sum(e, axis=-1, keepdims=True)
        prob[k] = p
        mixed = high_half(nn(p.astype(BF), pair)).astype(BF)
        att[k] = mixed
        term = nt(mixed, attn_tile((wm, wo)[side], yh)[:, 128:])
        acc = term if acc is None else acc + term
    part[...] = acc.astype(BF)


def feed(x, parts, lnp, bias, wm, wo, layer, part, mid, n2, pre, act):
    middle = x[...].astype(F32) + (total(parts) + ln_row(lnp, layer, 0, 2))
    mid[...] = middle
    normed = layer_norm(middle, ln_row(lnp, layer, 1, 0), ln_row(lnp, layer, 1, 1)).astype(BF)
    n2[...] = normed
    acc = None
    for k, side, yh in heads():
        w = (wm, wo)[side]
        u = nn(normed, ffn_tile(w, yh, 0))
        u = u + bias[yh, layer * 8 + 2 + side : layer * 8 + 3 + side, :]
        pre[k] = u
        a = gelu(u).astype(BF)
        act[k] = a
        term = nt(a, ffn_tile(w, yh, 1))
        acc = term if acc is None else acc + term
    part[...] = acc.astype(BF)


def feed_back(g, pre, wm, wo, dpre, part):
    acc = None
    for k, side, yh in heads():
        w = (wm, wo)[side]
        d = (nn(g, ffn_tile(w, yh, 1)) * gelu_slope(pre[k])).astype(BF)
        dpre[k] = d
        term = nt(d, ffn_tile(w, yh, 0))
        acc = term if acc is None else acc + term
    part[...] = acc.astype(BF)


def feed_kernel(x, p0, p1, p2, p3, lnp, bias, wm, wo, part, mid, n2, pre, act):
    feed(x, (p0, p1, p2, p3), lnp, bias, wm, wo, 0, part, mid, n2, pre, act)


def turn_kernel(x, p0, p1, p2, p3, lnp, bias, wm, wo, g, part, mid, n2, pre, act, dpre, back):
    feed(x, (p0, p1, p2, p3), lnp, bias, wm, wo, 1, part, mid, n2, pre, act)
    feed_back(g[...], pre, wm, wo, dpre, back)


def grad_ffn_kernel(n2, g, dpre, act, mine, other, sums, row):
    for k, side, yh in heads():
        out = (mine, other)[side]
        out[:, yh, :, 0:256] = tn(n2[...], dpre[k]).astype(BF).reshape(8, 128, 256)
        out[:, yh, :, 256:512] = tn(g[...], act[k]).astype(BF).reshape(8, 128, 256)
        sums[k : k + 1, :] = jnp.sum(dpre[k].astype(F32), axis=0, keepdims=True)
    row[...] = jnp.sum(g[...].astype(F32), axis=0, keepdims=True)


def attend_back(layer, g, mid, parts, lnp, wm, wo, prob, q, kv, dmid, bg, dq, dkv, rows):
    back, gg, gs = layer_norm_back(mid[...], ln_row(lnp, layer, 1, 0), total(parts))
    dm = g[...].astype(F32) + back
    dmid[...] = dm
    low = dm.astype(BF)
    bg[...] = low
    rows[0:1, :] = gg
    rows[1:2, :] = gs
    rows[2:3, :] = jnp.sum(low.astype(F32), axis=0, keepdims=True)
    at = dkv.shape[1] - ROWS
    for k, side, yh in heads():
        pair = kv[:, :, k * 128 : k * 128 + 128].reshape(16 * ROWS, 128)
        da = high_half(nn(low, attn_tile((wm, wo)[side], yh)[:, 128:])).astype(BF)
        p = prob[k]
        dp = nt(da, pair)
        ds = (p * (dp - jnp.sum(p * dp, axis=-1, keepdims=True))).astype(BF)
        dq[k] = low_half(nn(ds, pair) * SCALE).astype(BF)
        both = tn(ds, q[k]) * SCALE + tn(p.astype(BF), da)
        dkv[:, at:, k * 128 : k * 128 + 128] = both.astype(BF).reshape(16, ROWS, 128)


def attend_back_kernel(g, mid, p0, p1, p2, p3, lnp, wm, wo, prob, q, kv, dmid, bg, dq, dkv, rows):
    attend_back(1, g, mid, (p0, p1, p2, p3), lnp, wm, wo, prob, q, kv, dmid, bg, dq, dkv, rows)


def attend_back_first_kernel(
    g, mid, p0, p1, p2, p3, lnp, wm, wo, prob, q, kv, gm, gr, dmid, bg, dq, msg, rows
):
    attend_back(0, g, mid, (p0, p1, p2, p3), lnp, wm, wo, prob, q, kv, dmid, bg, dq, msg, rows)
    for i in range(8):
        for j in range(2):
            msg[2 * i + j, 0:128, :] = (gm[i, j].astype(F32) + gr[i, j].astype(F32)).astype(BF)


def project_back_kernel(dkv, dq, wm, wo, dproj, part, sums):
    pairs = jnp.sum(dkv[...].astype(F32), axis=0).astype(BF)
    acc = None
    for k, side, yh in heads():
        tile = jnp.concatenate([pairs[:, k * 128 : k * 128 + 128], dq[k]], axis=1)
        dproj[k] = tile
        sums[k : k + 1, :] = jnp.sum(tile.astype(F32), axis=0, keepdims=True)
        term = nt(tile, attn_tile((wm, wo)[side], yh))
        acc = term if acc is None else acc + term
    part[...] = acc.astype(BF)


def grad_attn_kernel(n1, bg, att, dproj, mine, other):
    for k, side, yh in heads():
        out = (mine, other)[side]
        first = tn(n1[...], dproj[k])
        second = tn(bg[...], att[k])
        out[:, yh, :, 0:128] = first[:, :128].astype(BF).reshape(8, 128, 128)
        out[:, yh, :, 128:] = (first[:, 128:] + second).astype(BF).reshape(8, 128, 128)


def hand_down_kernel(x, dmid, p0, p1, p2, p3, lnp, pre, wm, wo, dx, dpre, part, rows):
    back, gg, gs = layer_norm_back(
        x[...].astype(F32), ln_row(lnp, 1, 0, 0), total((p0, p1, p2, p3))
    )
    g = (dmid[...] + back).astype(BF)
    dx[...] = g
    rows[0:1, :] = gg
    rows[1:2, :] = gs
    feed_back(g, pre, wm, wo, dpre, part)


def last_kernel(
    x, dmid, p0, p1, p2, p3, lnp, gm, gr,
    r0, o0, a0, u0, h1, r1, o1, a1, u1, dx, msg,
):
    back, gg, gs = layer_norm_back(
        x[...].astype(F32), ln_row(lnp, 0, 0, 0), total((p0, p1, p2, p3))
    )
    dx[...] = (dmid[...] + back).astype(BF)
    lines = []
    for first, rows, ob, a, u in (
        ((gg, gs), r0, o0, a0, u0),
        ((h1[0:1, :], h1[1:2, :]), r1, o1, a1, u1),
    ):
        lines.append(
            (
                a[...],
                u[...],
                (
                    (first[0], rows[0:1, :]),
                    (first[1], rows[1:2, :]),
                    (rows[2:3, :], ob[...]),
                ),
            )
        )
    for d in range(8):
        cols = slice(d * 128, d * 128 + 128)
        for yh in range(2):
            block = []
            for a, u, pairs in lines:
                block += [a[yh : yh + 1], a[2 + yh : 3 + yh], u[yh : yh + 1], u[2 + yh : 3 + yh]]
                block += [jnp.concatenate([f[:, cols], s[:, cols]], axis=1) for f, s in pairs]
            block.append(jnp.zeros((2, 256), F32))
            g = 2 * d + yh
            msg[g, 0:128, :] = (gm[d, yh].astype(F32) + gr[d, yh].astype(F32)).astype(BF)
            msg[g, 128:144, :] = jnp.concatenate(block).astype(BF)


def combine_kernel(am, ar, fm, fr, msg):
    msg[0, :, 0:256] = (am[0].astype(F32) + ar[0].astype(F32)).astype(BF)
    msg[0, :, 256:768] = (fm[0].astype(F32) + fr[0].astype(F32)).astype(BF)


def settle_kernel(tail, l0, l1, out):
    t = jnp.sum(tail[...].astype(F32), axis=0)
    out[0, 0:128, 0:256] = t[0:128]
    out[1, 0:128, 0:256] = jnp.sum(l1[:, :, 0:256].astype(F32), axis=0)
    for j in range(2):
        cols = slice(256 + j * 256, 512 + j * 256)
        out[0, 0:128, cols] = jnp.sum(l0[:, 0:128, j * 256 : j * 256 + 256].astype(F32), axis=0)
        out[1, 0:128, cols] = jnp.sum(l1[:, :, cols].astype(F32), axis=0)
    small = t[128:144]
    pad = jnp.zeros((1, 256), F32)
    out[0, 128:136, 0:256] = jnp.concatenate([small[0:7], pad])
    out[1, 128:136, 0:256] = jnp.concatenate([small[7:14], pad])


def unpack_kernel(r, qkv, out, up, down, gain, shift, inb, outb, upb):
    a = [r[j, 0:128, 0:256] for j in range(2)]
    for i, at in enumerate((128, 0, 64)):
        qkv[i] = jnp.concatenate([t[:, at : at + 64] for t in a], axis=1)
    out[...] = jnp.concatenate([t[:, 192:256] for t in a], axis=1).T
    for j in range(2):
        up[:, j * 256 : j * 256 + 256] = r[j, 0:128, 256:512]
        down[j * 256 : j * 256 + 256, :] = r[j, 0:128, 512:768].T
    s0, s1 = r[0, 128:136, 0:256], r[1, 128:136, 0:256]
    for row, ref in ((4, gain), (5, shift), (6, outb)):
        t = s0[row : row + 1] + s1[row : row + 1]
        ref[0:1, :] = t[:, 0:128]
        ref[1:2, :] = t[:, 128:256]
    sides = [s0[0:1] + s1[1:2], s0[1:2] + s1[0:1]]
    inb[0:1, :] = jnp.concatenate([t[:, 128:192] for t in sides], axis=1)
    inb[1:2, :] = jnp.concatenate([t[:, 64:128] for t in sides], axis=1)
    upb[...] = jnp.concatenate([s0[2:3] + s1[3:4], s0[3:4] + s1[2:3]], axis=1)


def swap_cores(v):
    return lax.ppermute(v, "s", [(0, 1), (1, 0)])


def all_parts(part):
    got = [lax.ppermute(part, "x", [(i, i ^ k) for i in range(4)]) for k in (1, 3, 2)]
    return part, got[0], got[2], got[1]


def exchange(v, axes=CHIPS):
    return lax.all_to_all(v, axes, 0, 0, tiled=True)


def by_layer(mine, first, second):
    return jnp.where(mine == 0, first, second)


def whole_rows(s, yh, a, b):
    keep, send = by_layer(s, a, b), by_layer(s, b, a)
    got = swap_cores(send)
    rows = jnp.stack([by_layer(s, keep, got), by_layer(s, got, keep)])
    far = lax.ppermute(rows, "yh", [(0, 1), (1, 0)])
    return jnp.concatenate([by_layer(yh, rows, far), by_layer(yh, far, rows)], axis=1).reshape(
        1, 2, 1, 128, D
    )


def local(inputs, cotangent, wqkv, wout, wup, wdown, gain, shift, inb, outb, upb):
    s, yh = lax.axis_index("s"), lax.axis_index("yh")
    first = (lax.axis_index(CHIPS) * ROWS).astype(jnp.int32).reshape(1)

    def own_rows(v):
        return lax.dynamic_slice(v, (s, 0, yh * ROWS, 0), (1, 1, ROWS, D)).reshape(ROWS, D)

    x, cot = own_rows(inputs), own_rows(cotangent)
    msg, ffn = call(
        pack_kernel,
        [sds(2, 16, 144, 256), sds(2, 128, 512)],
        [
            jnp.moveaxis(wqkv[0], 1, 0), wout[0], wup[0], wdown[0],
            gain[0], shift[0], inb[0], outb[0], upb,
        ],
    )
    u = exchange(msg.reshape(32, 144, 256), ("s", *CHIPS)).reshape(2, 16, 144, 256)
    got = swap_cores(by_layer(s, ffn[1], ffn[0]))
    piece0, piece1 = by_layer(s, ffn[0], got), by_layer(s, got, ffn[1])
    u = u.reshape(2, 8, 2, 144, 256)
    am = [(u, (1, 8, 2, 144, 256), (l, 0, 0, 0, 0)) for l in range(2)]
    ao = [swap_cores(u[l]) for l in range(2)]
    kinds = dict(n1=sds(ROWS, D), q=sds(4, ROWS, 128))
    n10, q0, msg, lnp, bias = call(
        first_kernel,
        [kinds["n1"], kinds["q"], sds(16, 192, 512), sds(2, 16, D, dtype=F32), sds(2, 16, 256, dtype=F32)],
        [x, (u, (2, 8, 2, 16, 256), (0, 0, 0, 8, 0)), am[0], ao[0], piece0],
    )
    got0 = exchange(msg)
    kv0 = (got0, (16, ROWS, 512), (0, 2, 0))
    f0 = (got0.reshape(8, 2, 192, 512), (8, 2, 128, 512), (0, 0, 0, 0))
    f0o = (swap_cores(got0).reshape(8, 2, 192, 512), (8, 2, 128, 512), (0, 0, 0, 0))
    attend_outs = [sds(ROWS, D), sds(4, ROWS, D, dtype=F32), sds(4, ROWS, 128)]
    feed_outs = [
        sds(ROWS, D), sds(ROWS, D, dtype=F32), sds(ROWS, D),
        sds(4, ROWS, 256, dtype=F32), sds(4, ROWS, 256),
    ]
    part, prob0, att0 = call(attend_kernel, attend_outs, [(first, None, None), q0, kv0, am[0], ao[0]])
    f1 = exchange(jnp.broadcast_to(piece1, (16, 128, 512))).reshape(8, 2, 128, 512)
    f1o = swap_cores(f1)
    part, mid0, n20, pre0, act0 = call(
        feed_kernel, feed_outs, [x, *all_parts(part), lnp, bias, f0, f0o]
    )
    y0, n11, q1, msg = call(
        next_kernel,
        [sds(ROWS, D), kinds["n1"], kinds["q"], sds(16, ROWS, 512)],
        [mid0, *all_parts(part), lnp, bias, am[1], ao[1]],
    )
    kv1 = exchange(msg)
    part, prob1, att1 = call(attend_kernel, attend_outs, [(first, None, None), q1, kv1, am[1], ao[1]])
    part, mid1, n21, pre1, act1, dpre1, back = call(
        turn_kernel,
        feed_outs + [sds(4, ROWS, 256), sds(ROWS, D)],
        [y0, *all_parts(part), lnp, bias, f1, f1o, cot],
    )
    backs = all_parts(back)
    a, b, c, d = [p.astype(F32) for p in all_parts(part)]
    y1 = (mid1 + (((a + b) + (c + d)) + lnp[1, 14:15])).astype(BF)
    grad_ffn_outs = [
        sds(8, 2, 128, 512), sds(8, 2, 128, 512), sds(4, 256, dtype=F32), sds(1, D, dtype=F32)
    ]
    gfm1, gfo1, gub1, ob11 = call(grad_ffn_kernel, grad_ffn_outs, [n21, cot, dpre1, act1])
    gfr1 = swap_cores(gfo1)
    back_outs = [sds(ROWS, D, dtype=F32), sds(ROWS, D), sds(4, ROWS, 128)]
    rows_out = sds(8, D, dtype=F32)
    dmid1, bg1, dq1, dkv, rows1 = call(
        attend_back_kernel,
        back_outs + [sds(16, ROWS, 512), rows_out],
        [cot, mid1, *backs, lnp, am[1], ao[1], prob1, q1, kv1],
    )
    dkv = exchange(dkv)
    project_outs = [sds(4, ROWS, 256), sds(ROWS, D), sds(4, 256, dtype=F32)]
    dproj1, part, gib1 = call(project_back_kernel, project_outs, [dkv, dq1, am[1], ao[1]])
    backs = all_parts(part)
    grad_attn_outs = [sds(8, 2, 128, 256), sds(8, 2, 128, 256)]
    gam1, gao1 = call(grad_attn_kernel, grad_attn_outs, [n11, bg1, att1, dproj1])
    gar1 = swap_cores(gao1)
    dx1, dpre0, part, head1 = call(
        hand_down_kernel,
        [sds(ROWS, D), sds(4, ROWS, 256), sds(ROWS, D), rows_out],
        [y0, dmid1, *backs, lnp, pre0, f0, f0o],
    )
    backs = all_parts(part)
    gfm0, gfo0, gub0, ob10 = call(grad_ffn_kernel, grad_ffn_outs, [n20, dx1, dpre0, act0])
    gfr0 = swap_cores(gfo0)
    def flat(v):
        return v.reshape(16, 128, v.shape[-1])
    msg1 = pl.pallas_call(
        combine_kernel,
        grid=(16,),
        out_shape=sds(16, 128, 768),
        in_specs=[pl.BlockSpec((1, 128, w), lambda i: (i, 0, 0)) for w in (256, 256, 512, 512)],
        out_specs=pl.BlockSpec((1, 128, 768), lambda i: (i, 0, 0)),
        compiler_params=pltpu.CompilerParams(vmem_limit_bytes=32 * 1024 * 1024),
        cost_estimate=pl.CostEstimate(flops=0, bytes_accessed=9_000_000, transcendentals=0),
    )(flat(gam1), flat(gar1), flat(gfm1), flat(gfr1))
    l1 = exchange(msg1)
    dmid0, bg0, dq0, msg, rows0 = call(
        attend_back_first_kernel,
        back_outs + [sds(16, 192, 512), rows_out],
        [dx1, mid0, *backs, lnp, am[0], ao[0], prob0, q0, kv0, gfm0, gfr0],
    )
    l0 = exchange(msg)
    dproj0, part, gib0 = call(
        project_back_kernel, project_outs, [(l0, (16, ROWS, 512), (0, 2, 0)), dq0, am[0], ao[0]]
    )
    backs = all_parts(part)
    gam0, gao0 = call(grad_attn_kernel, grad_attn_outs, [n10, bg0, att0, dproj0])
    gar0 = swap_cores(gao0)
    dx0, msg = call(
        last_kernel,
        [sds(ROWS, D), sds(16, 144, 256)],
        [x, dmid0, *backs, lnp, gam0, gar0, rows0, ob10, gib0, gub0, head1, rows1, ob11, gib1, gub1],
    )
    tail = exchange(msg)
    acts = whole_rows(s, yh, y0, y1)
    grads = whole_rows(s, yh, dx0, dx1)
    (settled,) = call(settle_kernel, [sds(2, 144, 768, dtype=F32)], [tail, l0, l1])
    settled = exchange(settled, "s")
    f = functools.partial(sds, dtype=F32)
    gq, go, gu, gd, gg, gs, gi, gb, gub = call(
        unpack_kernel,
        [f(3, 128, 128), f(128, 128), f(128, 512), f(512, 128), f(2, 128), f(2, 128), f(2, 128), f(2, 128), f(1, 512)],
        [settled],
    )
    return (
        acts, grads, jnp.moveaxis(gq, 0, 1)[None], go[None], gu[None], gd[None],
        gg[None], gs[None], gi[None], gb[None], gub,
    )


def solution(mesh):
    parts = Mesh(mesh.devices.reshape(2, 4, 2, 2, 4), ("s", "z", "yl", "yh", "x"))
    dp, tp = ("z", "yl"), ("yh", "x")
    return jax.shard_map(
        local,
        mesh=parts,
        in_specs=(
            P(None, None, dp, None),
            P(None, None, dp, None),
            P("s", dp, None, tp),
            P("s", tp, dp),
            P("s", dp, tp),
            P("s", tp, dp),
            P("s", None, dp),
            P("s", None, dp),
            P("s", None, tp),
            P("s", None, dp),
            P("s", tp),
        ),
        out_specs=(
            P("s", None, None, dp, None),
            P("s", None, None, dp, None),
            P("s", dp, None, tp),
            P("s", tp, dp),
            P("s", dp, tp),
            P("s", tp, dp),
            P("s", None, dp),
            P("s", None, dp),
            P("s", None, tp),
            P("s", None, dp),
            P("s", tp),
        ),
        check_vma=False,
    )
```

```python
import functools
import math

import jax
import jax.numpy as jnp
from jax import lax
from jax.experimental import pallas as pl
from jax.experimental.pallas import tpu as pltpu
from jax.sharding import Mesh, PartitionSpec as P

EPSILON = 1e-05
MASKED = -1e30
SCALE = 1.0 / math.sqrt(64)
BF = jnp.bfloat16
F32 = jnp.float32
CHIPS = ("z", "yl", "yh")
ROWS = 64
D = 1024


def sds(*shape, dtype=BF):
    return jax.ShapeDtypeStruct(shape, dtype)


def call(kernel, outs, ins, us=3):
    specs, arrays = [], []
    for item in ins:
        if isinstance(item, tuple):
            array, block, index = item
            if block is None:
                specs.append(pl.BlockSpec(memory_space=pltpu.SMEM))
            else:
                specs.append(pl.BlockSpec(block, functools.partial(lambda at, i: at, index)))
        else:
            array = item
            specs.append(
                pl.BlockSpec(
                    array.shape, functools.partial(lambda n, i: (0,) * n, array.ndim)
                )
            )
        arrays.append(array)
    out_specs = [
        pl.BlockSpec(o.shape, functools.partial(lambda n, i: (0,) * n, len(o.shape)))
        for o in outs
    ]
    return pl.pallas_call(
        kernel,
        grid=(1,),
        out_shape=outs,
        in_specs=specs,
        out_specs=out_specs,
        compiler_params=pltpu.CompilerParams(vmem_limit_bytes=48 * 1024 * 1024),
        cost_estimate=pl.CostEstimate(
            flops=0, bytes_accessed=us * 3_000_000, transcendentals=0
        ),
    )(*arrays)


def nn(a, b):
    return jnp.dot(a, b, preferred_element_type=F32)


def nt(a, b):
    return lax.dot_general(a, b, (((1,), (1,)), ((), ())), preferred_element_type=F32)


def tn(a, b):
    return lax.dot_general(a, b, (((0,), (0,)), ((), ())), preferred_element_type=F32)


def heads():
    return [(k, side, yh) for k, (side, yh) in enumerate([(0, 0), (0, 1), (1, 0), (1, 1)])]


def attn_tile(ref, yh):
    return ref[:, yh, 0:128, :].reshape(D, 256)


def ffn_tile(ref, yh, part):
    return ref[:, yh, 0:128, part * 256 : part * 256 + 256].reshape(D, 256)


def low_half(v):
    lane = lax.broadcasted_iota(jnp.int32, v.shape, 1)
    return jnp.where(lane < 64, v, 0.0)


def high_half(v):
    lane = lax.broadcasted_iota(jnp.int32, v.shape, 1)
    return jnp.where(lane >= 64, v, 0.0)


def mean_of(v):
    return jnp.sum(v, axis=-1, keepdims=True) * (1.0 / D)


def normal(v):
    centred = v - mean_of(v)
    inverse = lax.rsqrt(mean_of(centred * centred) + EPSILON)
    return centred * inverse, inverse


def layer_norm(v, gain, shift):
    return normal(v)[0] * gain + shift


def layer_norm_back(v, gain, grad):
    xhat, inverse = normal(v)
    d = grad * gain
    back = inverse * (d - mean_of(d) - xhat * mean_of(d * xhat))
    return (
        back,
        jnp.sum(grad * xhat, axis=0, keepdims=True),
        jnp.sum(grad, axis=0, keepdims=True),
    )


def gelu(u):
    return 0.5 * u * (1.0 + jnp.tanh(0.7978845608028654 * (u + 0.044715 * u * u * u)))


def gelu_slope(u):
    t = jnp.tanh(0.7978845608028654 * (u + 0.044715 * u * u * u))
    return 0.5 * (1.0 + t) + 0.5 * u * (1.0 - t * t) * (
        0.7978845608028654 * (1.0 + 3.0 * 0.044715 * u * u)
    )


def total(parts):
    a, b, c, d = [p[...].astype(F32) for p in parts]
    return (a + b) + (c + d)


def ln_row(lnp, layer, which, kind):
    return lnp[which, layer * 8 + 4 + kind : layer * 8 + 5 + kind, :]


def project(x, lnp, bias, wm, wo, layer, n1, q, kv):
    normed = layer_norm(x, ln_row(lnp, layer, 0, 0), ln_row(lnp, layer, 0, 1)).astype(BF)
    n1[...] = normed
    for k, side, yh in heads():
        tile = nn(normed, attn_tile((wm, wo)[side], yh))
        tile = tile + bias[yh, layer * 8 + side : layer * 8 + side + 1, :]
        q[k] = low_half(tile[:, 128:]).astype(BF)
        pair = tile[:, :128].astype(BF)
        for g in range(16):
            kv[g, kv.shape[1] - ROWS :, k * 128 : k * 128 + 128] = pair


def pack_kernel(core, qkv, out, up, down, gain, shift, inb, outb, upb, keep, send):
    wt = out[...].astype(F32).T
    dt = down[...].astype(F32).T
    inb_, gain_, shift_, outb_ = [r[...].astype(F32) for r in (inb, gain, shift, outb)]
    upb_ = upb[...].astype(F32)
    zero = jnp.zeros((1, 64), F32)
    def flat(v):
        return jnp.concatenate([v[0:1], v[1:2]], axis=1)
    rows = []
    for j in range(2):
        cols = slice(j * 64, j * 64 + 64)
        rows.append(jnp.concatenate([zero, inb_[1:2, cols], inb_[0:1, cols], zero], axis=1))
    ups = [upb_[:, :256], upb_[:, 256:]]
    rest = [flat(gain_), flat(shift_), flat(outb_), jnp.zeros((9, 256), F32)]
    halves = []
    for j in range(2):
        cols = slice(j * 64, j * 64 + 64)
        wide = slice(j * 256, j * 256 + 256)
        halves.append(
            (
                up[:, wide].astype(F32),
                dt[:, wide],
                jnp.concatenate([qkv[i, :, cols].astype(F32) for i in (1, 2, 0)] + [wt[:, cols]], axis=1),
                jnp.concatenate([rows[j], rows[1 - j], ups[j], ups[1 - j], *rest]),
            )
        )
    first = core[0] == 0
    for ref, pair in ((keep, halves), (send, halves[::-1])):
        values = [jnp.where(first, a, b).astype(BF) for a, b in zip(*pair)]
        ref[0:128, 0:256] = values[0]
        ref[0:128, 256:512] = values[1]
        ref[0:128, 512:768] = values[2]
        ref[128:144, 512:768] = values[3]


def spread_kernel(core, keep, got, msg, ffn0, ffn1, attn1):
    first = core[0] == 0
    k, o = keep[...], got[...]
    lower, upper = jnp.where(first, k, o), jnp.where(first, o, k)
    small = jnp.concatenate(
        [v[128:144, 512:768].astype(F32)[0:8] for v in (lower, upper)]
    ).astype(BF)
    tile = lower[0:128, 512:768]
    for g in range(16):
        msg[g, 0:128, :] = tile
        msg[g, 128:144, :] = small
    ffn0[...] = lower[0:128, 0:512]
    ffn1[...] = upper[0:128, 0:512]
    attn1[...] = upper[0:128, 512:768]


def first_kernel(x, params, wm, wo, piece, n1, q, msg, lnp, bias):
    for layer in range(2):
        part = slice(layer * 8, layer * 8 + 8)
        blocks = [params[d, 0].astype(F32)[part] for d in range(8)]
        for half in range(2):
            cols = slice(half * 128, half * 128 + 128)
            lnp[half, part, :] = jnp.concatenate([b[:, cols] for b in blocks], axis=1)
        for yh in range(2):
            bias[yh, part, :] = params[0, yh].astype(F32)[part]
    project(x[...].astype(F32), lnp, bias, wm, wo, 0, n1, q, msg)
    rest = piece[...]
    for g in range(16):
        msg[g, 0:128, :] = rest


def next_kernel(mid, p0, p1, p2, p3, lnp, bias, wm, wo, y, n1, q, msg):
    out = (mid[...] + (total((p0, p1, p2, p3)) + ln_row(lnp, 0, 1, 2))).astype(BF)
    y[...] = out
    project(out.astype(F32), lnp, bias, wm, wo, 1, n1, q, msg)


def attend_kernel(first, q, kv, wm, wo, part, prob, att):
    length = 16 * ROWS
    qpos = first[0] + lax.broadcasted_iota(jnp.int32, (ROWS, length), 0)
    kpos = lax.broadcasted_iota(jnp.int32, (ROWS, length), 1)
    allowed = kpos <= qpos
    acc = None
    for k, side, yh in heads():
        pair = kv[:, :, k * 128 : k * 128 + 128].reshape(length, 128)
        scores = jnp.where(allowed, nt(q[k], pair) * SCALE, MASKED)
        e = jnp.exp(scores - jnp.max(scores, axis=-1, keepdims=True))
        p = e / jnp.sum(e, axis=-1, keepdims=True)
        prob[k] = p
        mixed = high_half(nn(p.astype(BF), pair)).astype(BF)
        att[k] = mixed
        term = nt(mixed, attn_tile((wm, wo)[side], yh)[:, 128:])
        acc = term if acc is None else acc + term
    part[...] = acc.astype(BF)


def feed(x, parts, lnp, bias, wm, wo, layer, part, mid, n2, pre, act):
    middle = x[...].astype(F32) + (total(parts) + ln_row(lnp, layer, 0, 2))
    mid[...] = middle
    normed = layer_norm(middle, ln_row(lnp, layer, 1, 0), ln_row(lnp, layer, 1, 1)).astype(BF)
    n2[...] = normed
    acc = None
    for k, side, yh in heads():
        w = (wm, wo)[side]
        u = nn(normed, ffn_tile(w, yh, 0))
        u = u + bias[yh, layer * 8 + 2 + side : layer * 8 + 3 + side, :]
        pre[k] = u
        a = gelu(u).astype(BF)
        act[k] = a
        term = nt(a, ffn_tile(w, yh, 1))
        acc = term if acc is None else acc + term
    part[...] = acc.astype(BF)


def feed_back(g, pre, wm, wo, dpre, part):
    acc = None
    for k, side, yh in heads():
        w = (wm, wo)[side]
        d = (nn(g, ffn_tile(w, yh, 1)) * gelu_slope(pre[k])).astype(BF)
        dpre[k] = d
        term = nt(d, ffn_tile(w, yh, 0))
        acc = term if acc is None else acc + term
    part[...] = acc.astype(BF)


def feed_kernel(x, p0, p1, p2, p3, lnp, bias, wm, wo, part, mid, n2, pre, act):
    feed(x, (p0, p1, p2, p3), lnp, bias, wm, wo, 0, part, mid, n2, pre, act)


def turn_kernel(x, p0, p1, p2, p3, lnp, bias, wm, wo, g, part, mid, n2, pre, act, dpre, back):
    feed(x, (p0, p1, p2, p3), lnp, bias, wm, wo, 1, part, mid, n2, pre, act)
    feed_back(g[...], pre, wm, wo, dpre, back)


def grad_ffn_kernel(n2, g, dpre, act, mine, other, sums, row):
    for k, side, yh in heads():
        out = (mine, other)[side]
        out[:, yh, :, 0:256] = tn(n2[...], dpre[k]).astype(BF).reshape(8, 128, 256)
        out[:, yh, :, 256:512] = tn(g[...], act[k]).astype(BF).reshape(8, 128, 256)
        sums[k : k + 1, :] = jnp.sum(dpre[k].astype(F32), axis=0, keepdims=True)
    row[...] = jnp.sum(g[...].astype(F32), axis=0, keepdims=True)


def attend_back(layer, g, mid, parts, lnp, wm, wo, prob, q, kv, dmid, bg, dq, dkv, rows):
    back, gg, gs = layer_norm_back(mid[...], ln_row(lnp, layer, 1, 0), total(parts))
    dm = g[...].astype(F32) + back
    dmid[...] = dm
    low = dm.astype(BF)
    bg[...] = low
    rows[0:1, :] = gg
    rows[1:2, :] = gs
    rows[2:3, :] = jnp.sum(low.astype(F32), axis=0, keepdims=True)
    at = dkv.shape[1] - ROWS
    for k, side, yh in heads():
        pair = kv[:, :, k * 128 : k * 128 + 128].reshape(16 * ROWS, 128)
        da = high_half(nn(low, attn_tile((wm, wo)[side], yh)[:, 128:])).astype(BF)
        p = prob[k]
        dp = nt(da, pair)
        ds = (p * (dp - jnp.sum(p * dp, axis=-1, keepdims=True))).astype(BF)
        dq[k] = low_half(nn(ds, pair) * SCALE).astype(BF)
        both = tn(ds, q[k]) * SCALE + tn(p.astype(BF), da)
        dkv[:, at:, k * 128 : k * 128 + 128] = both.astype(BF).reshape(16, ROWS, 128)


def attend_back_kernel(g, mid, p0, p1, p2, p3, lnp, wm, wo, prob, q, kv, dmid, bg, dq, dkv, rows):
    attend_back(1, g, mid, (p0, p1, p2, p3), lnp, wm, wo, prob, q, kv, dmid, bg, dq, dkv, rows)


def attend_back_first_kernel(
    g, mid, p0, p1, p2, p3, lnp, wm, wo, prob, q, kv, gm, gr, dmid, bg, dq, msg, rows
):
    attend_back(0, g, mid, (p0, p1, p2, p3), lnp, wm, wo, prob, q, kv, dmid, bg, dq, msg, rows)
    for i in range(8):
        for j in range(2):
            msg[2 * i + j, 0:128, :] = (gm[i, j].astype(F32) + gr[i, j].astype(F32)).astype(BF)


def project_back_kernel(dkv, dq, wm, wo, dproj, part, sums):
    pairs = jnp.sum(dkv[...].astype(F32), axis=0).astype(BF)
    acc = None
    for k, side, yh in heads():
        tile = jnp.concatenate([pairs[:, k * 128 : k * 128 + 128], dq[k]], axis=1)
        dproj[k] = tile
        sums[k : k + 1, :] = jnp.sum(tile.astype(F32), axis=0, keepdims=True)
        term = nt(tile, attn_tile((wm, wo)[side], yh))
        acc = term if acc is None else acc + term
    part[...] = acc.astype(BF)


def grad_attn_kernel(n1, bg, att, dproj, mine, other):
    for k, side, yh in heads():
        out = (mine, other)[side]
        first = tn(n1[...], dproj[k])
        second = tn(bg[...], att[k])
        out[:, yh, :, 0:128] = first[:, :128].astype(BF).reshape(8, 128, 128)
        out[:, yh, :, 128:] = (first[:, 128:] + second).astype(BF).reshape(8, 128, 128)


def hand_down_kernel(x, dmid, p0, p1, p2, p3, lnp, pre, wm, wo, dx, dpre, part, rows):
    back, gg, gs = layer_norm_back(
        x[...].astype(F32), ln_row(lnp, 1, 0, 0), total((p0, p1, p2, p3))
    )
    g = (dmid[...] + back).astype(BF)
    dx[...] = g
    rows[0:1, :] = gg
    rows[1:2, :] = gs
    feed_back(g, pre, wm, wo, dpre, part)


def last_kernel(
    x, dmid, p0, p1, p2, p3, lnp, gm, gr,
    r0, o0, a0, u0, h1, r1, o1, a1, u1, dx, msg,
):
    back, gg, gs = layer_norm_back(
        x[...].astype(F32), ln_row(lnp, 0, 0, 0), total((p0, p1, p2, p3))
    )
    dx[...] = (dmid[...] + back).astype(BF)
    lines = []
    for first, rows, ob, a, u in (
        ((gg, gs), r0, o0, a0, u0),
        ((h1[0:1, :], h1[1:2, :]), r1, o1, a1, u1),
    ):
        lines.append(
            (
                a[...],
                u[...],
                (
                    (first[0], rows[0:1, :]),
                    (first[1], rows[1:2, :]),
                    (rows[2:3, :], ob[...]),
                ),
            )
        )
    for d in range(8):
        cols = slice(d * 128, d * 128 + 128)
        for yh in range(2):
            block = []
            for a, u, pairs in lines:
                block += [a[yh : yh + 1], a[2 + yh : 3 + yh], u[yh : yh + 1], u[2 + yh : 3 + yh]]
                block += [jnp.concatenate([f[:, cols], s[:, cols]], axis=1) for f, s in pairs]
            block.append(jnp.zeros((2, 256), F32))
            g = 2 * d + yh
            msg[g, 0:128, :] = (gm[d, yh].astype(F32) + gr[d, yh].astype(F32)).astype(BF)
            msg[g, 128:144, :] = jnp.concatenate(block).astype(BF)


def combine_kernel(am, ar, fm, fr, msg):
    msg[0, :, 0:512] = (fm[0].astype(F32) + fr[0].astype(F32)).astype(BF)
    msg[0, :, 512:768] = (am[0].astype(F32) + ar[0].astype(F32)).astype(BF)


def settle_kernel(tail, l0, l1, out):
    t = jnp.sum(tail[...].astype(F32), axis=0)
    out[0, 0:128, 512:768] = t[0:128]
    for j in range(2):
        cols = slice(j * 256, j * 256 + 256)
        out[0, 0:128, cols] = jnp.sum(l0[:, 0:128, cols].astype(F32), axis=0)
    out[1, 0:128, :] = l1[...].astype(F32)
    small = t[128:144]
    pad = jnp.zeros((1, 256), F32)
    out[0, 128:136, 512:768] = jnp.concatenate([small[0:7], pad])
    out[1, 128:136, 512:768] = jnp.concatenate([small[7:14], pad])


def unpack_kernel(r, qkv, out, up, down, gain, shift, inb, outb, upb):
    a = [r[j, 0:128, 512:768] for j in range(2)]
    for i, at in enumerate((128, 0, 64)):
        qkv[i] = jnp.concatenate([t[:, at : at + 64] for t in a], axis=1)
    out[...] = jnp.concatenate([t[:, 192:256] for t in a], axis=1).T
    for j in range(2):
        up[:, j * 256 : j * 256 + 256] = r[j, 0:128, 0:256]
        down[j * 256 : j * 256 + 256, :] = r[j, 0:128, 256:512].T
    s0, s1 = r[0, 128:136, 512:768], r[1, 128:136, 512:768]
    for row, ref in ((4, gain), (5, shift), (6, outb)):
        t = s0[row : row + 1] + s1[row : row + 1]
        ref[0:1, :] = t[:, 0:128]
        ref[1:2, :] = t[:, 128:256]
    sides = [s0[0:1] + s1[1:2], s0[1:2] + s1[0:1]]
    inb[0:1, :] = jnp.concatenate([t[:, 128:192] for t in sides], axis=1)
    inb[1:2, :] = jnp.concatenate([t[:, 64:128] for t in sides], axis=1)
    upb[...] = jnp.concatenate([s0[2:3] + s1[3:4], s0[3:4] + s1[2:3]], axis=1)


def swap_cores(v):
    return lax.ppermute(v, "s", [(0, 1), (1, 0)])


def all_parts(part):
    got = [lax.ppermute(part, "x", [(i, i ^ k) for i in range(4)]) for k in (1, 3, 2)]
    return part, got[0], got[2], got[1]


def exchange(v, axes=CHIPS):
    return lax.all_to_all(v, axes, 0, 0, tiled=True)


def by_layer(mine, first, second):
    return jnp.where(mine == 0, first, second)


def whole_rows(s, yh, a, b):
    keep, send = by_layer(s, a, b), by_layer(s, b, a)
    got = swap_cores(send)
    rows = jnp.stack([by_layer(s, keep, got), by_layer(s, got, keep)])
    far = lax.ppermute(rows, "yh", [(0, 1), (1, 0)])
    return jnp.concatenate([by_layer(yh, rows, far), by_layer(yh, far, rows)], axis=1).reshape(
        1, 2, 1, 128, D
    )


def local(inputs, cotangent, wqkv, wout, wup, wdown, gain, shift, inb, outb, upb):
    s, yh = lax.axis_index("s"), lax.axis_index("yh")
    first = (lax.axis_index(CHIPS) * ROWS).astype(jnp.int32).reshape(1)

    def own_rows(v):
        return lax.dynamic_slice(v, (s, 0, yh * ROWS, 0), (1, 1, ROWS, D)).reshape(ROWS, D)

    x, cot = own_rows(inputs), own_rows(cotangent)
    core = (s.astype(jnp.int32).reshape(1), None, None)
    keep, send = call(
        pack_kernel,
        [sds(144, 768), sds(144, 768)],
        [
            core, jnp.moveaxis(wqkv[0], 1, 0), wout[0], wup[0], wdown[0],
            gain[0], shift[0], inb[0], outb[0], upb,
        ],
    )
    msg, piece0, ffn1, attn1 = call(
        spread_kernel,
        [sds(16, 144, 256), sds(128, 512), sds(128, 512), sds(128, 256)],
        [core, keep, swap_cores(send)],
    )
    a0 = exchange(msg).reshape(8, 2, 144, 256)
    a1 = lax.all_gather(attn1, CHIPS, axis=0, tiled=True).reshape(8, 2, 128, 256)
    f1 = lax.all_gather(ffn1, CHIPS, axis=0, tiled=True).reshape(8, 2, 128, 512)
    am, ao = [a0, a1], [swap_cores(a0), swap_cores(a1)]
    f1o = swap_cores(f1)
    kinds = dict(n1=sds(ROWS, D), q=sds(4, ROWS, 128))
    n10, q0, msg, lnp, bias = call(
        first_kernel,
        [kinds["n1"], kinds["q"], sds(16, 192, 512), sds(2, 16, D, dtype=F32), sds(2, 16, 256, dtype=F32)],
        [x, (a0, (8, 2, 16, 256), (0, 0, 8, 0)), am[0], ao[0], piece0],
    )
    got0 = exchange(msg)
    kv0 = (got0, (16, ROWS, 512), (0, 2, 0))
    f0 = (got0.reshape(8, 2, 192, 512), (8, 2, 128, 512), (0, 0, 0, 0))
    f0o = (swap_cores(got0).reshape(8, 2, 192, 512), (8, 2, 128, 512), (0, 0, 0, 0))
    attend_outs = [sds(ROWS, D), sds(4, ROWS, D, dtype=F32), sds(4, ROWS, 128)]
    feed_outs = [
        sds(ROWS, D), sds(ROWS, D, dtype=F32), sds(ROWS, D),
        sds(4, ROWS, 256, dtype=F32), sds(4, ROWS, 256),
    ]
    part, prob0, att0 = call(attend_kernel, attend_outs, [(first, None, None), q0, kv0, am[0], ao[0]])
    part, mid0, n20, pre0, act0 = call(
        feed_kernel, feed_outs, [x, *all_parts(part), lnp, bias, f0, f0o]
    )
    y0, n11, q1, msg = call(
        next_kernel,
        [sds(ROWS, D), kinds["n1"], kinds["q"], sds(16, ROWS, 512)],
        [mid0, *all_parts(part), lnp, bias, am[1], ao[1]],
    )
    kv1 = exchange(msg)
    part, prob1, att1 = call(attend_kernel, attend_outs, [(first, None, None), q1, kv1, am[1], ao[1]])
    part, mid1, n21, pre1, act1, dpre1, back = call(
        turn_kernel,
        feed_outs + [sds(4, ROWS, 256), sds(ROWS, D)],
        [y0, *all_parts(part), lnp, bias, f1, f1o, cot],
    )
    backs = all_parts(back)
    a, b, c, d = [p.astype(F32) for p in all_parts(part)]
    y1 = (mid1 + (((a + b) + (c + d)) + lnp[1, 14:15])).astype(BF)
    grad_ffn_outs = [
        sds(8, 2, 128, 512), sds(8, 2, 128, 512), sds(4, 256, dtype=F32), sds(1, D, dtype=F32)
    ]
    gfm1, gfo1, gub1, ob11 = call(grad_ffn_kernel, grad_ffn_outs, [n21, cot, dpre1, act1])
    gfr1 = swap_cores(gfo1)
    back_outs = [sds(ROWS, D, dtype=F32), sds(ROWS, D), sds(4, ROWS, 128)]
    rows_out = sds(8, D, dtype=F32)
    dmid1, bg1, dq1, dkv, rows1 = call(
        attend_back_kernel,
        back_outs + [sds(16, ROWS, 512), rows_out],
        [cot, mid1, *backs, lnp, am[1], ao[1], prob1, q1, kv1],
    )
    dkv = exchange(dkv)
    project_outs = [sds(4, ROWS, 256), sds(ROWS, D), sds(4, 256, dtype=F32)]
    dproj1, part, gib1 = call(project_back_kernel, project_outs, [dkv, dq1, am[1], ao[1]])
    backs = all_parts(part)
    grad_attn_outs = [sds(8, 2, 128, 256), sds(8, 2, 128, 256)]
    gam1, gao1 = call(grad_attn_kernel, grad_attn_outs, [n11, bg1, att1, dproj1])
    gar1 = swap_cores(gao1)
    dx1, dpre0, part, head1 = call(
        hand_down_kernel,
        [sds(ROWS, D), sds(4, ROWS, 256), sds(ROWS, D), rows_out],
        [y0, dmid1, *backs, lnp, pre0, f0, f0o],
    )
    backs = all_parts(part)
    gfm0, gfo0, gub0, ob10 = call(grad_ffn_kernel, grad_ffn_outs, [n20, dx1, dpre0, act0])
    gfr0 = swap_cores(gfo0)
    def flat(v):
        return v.reshape(16, 128, v.shape[-1])
    msg1 = pl.pallas_call(
        combine_kernel,
        grid=(16,),
        out_shape=sds(16, 128, 768),
        in_specs=[pl.BlockSpec((1, 128, w), lambda i: (i, 0, 0)) for w in (256, 256, 512, 512)],
        out_specs=pl.BlockSpec((1, 128, 768), lambda i: (i, 0, 0)),
        compiler_params=pltpu.CompilerParams(vmem_limit_bytes=32 * 1024 * 1024),
        cost_estimate=pl.CostEstimate(flops=0, bytes_accessed=9_000_000, transcendentals=0),
    )(flat(gam1), flat(gar1), flat(gfm1), flat(gfr1))
    l1 = lax.psum_scatter(msg1.reshape(2048, 768), CHIPS, scatter_dimension=0, tiled=True)
    dmid0, bg0, dq0, msg, rows0 = call(
        attend_back_first_kernel,
        back_outs + [sds(16, 192, 512), rows_out],
        [dx1, mid0, *backs, lnp, am[0], ao[0], prob0, q0, kv0, gfm0, gfr0],
    )
    l0 = exchange(msg)
    dproj0, part, gib0 = call(
        project_back_kernel, project_outs, [(l0, (16, ROWS, 512), (0, 2, 0)), dq0, am[0], ao[0]]
    )
    backs = all_parts(part)
    gam0, gao0 = call(grad_attn_kernel, grad_attn_outs, [n10, bg0, att0, dproj0])
    gar0 = swap_cores(gao0)
    dx0, msg = call(
        last_kernel,
        [sds(ROWS, D), sds(16, 144, 256)],
        [x, dmid0, *backs, lnp, gam0, gar0, rows0, ob10, gib0, gub0, head1, rows1, ob11, gib1, gub1],
    )
    tail = exchange(msg)
    acts = whole_rows(s, yh, y0, y1)
    grads = whole_rows(s, yh, dx0, dx1)
    (settled,) = call(settle_kernel, [sds(2, 144, 768, dtype=F32)], [tail, l0, l1])
    settled = exchange(settled, "s")
    f = functools.partial(sds, dtype=F32)
    gq, go, gu, gd, gg, gs, gi, gb, gub = call(
        unpack_kernel,
        [f(3, 128, 128), f(128, 128), f(128, 512), f(512, 128), f(2, 128), f(2, 128), f(2, 128), f(2, 128), f(1, 512)],
        [settled],
    )
    return (
        acts, grads, jnp.moveaxis(gq, 0, 1)[None], go[None], gu[None], gd[None],
        gg[None], gs[None], gi[None], gb[None], gub,
    )


def solution(mesh):
    parts = Mesh(mesh.devices.reshape(2, 4, 2, 2, 4), ("s", "z", "yl", "yh", "x"))
    dp, tp = ("z", "yl"), ("yh", "x")
    return jax.shard_map(
        local,
        mesh=parts,
        in_specs=(
            P(None, None, dp, None),
            P(None, None, dp, None),
            P("s", dp, None, tp),
            P("s", tp, dp),
            P("s", dp, tp),
            P("s", tp, dp),
            P("s", None, dp),
            P("s", None, dp),
            P("s", None, tp),
            P("s", None, dp),
            P("s", tp),
        ),
        out_specs=(
            P("s", None, None, dp, None),
            P("s", None, None, dp, None),
            P("s", dp, None, tp),
            P("s", tp, dp),
            P("s", dp, tp),
            P("s", tp, dp),
            P("s", None, dp),
            P("s", None, dp),
            P("s", None, tp),
            P("s", None, dp),
            P("s", tp),
        ),
        check_vma=False,
    )
```

```python
import functools
import math

import jax
import jax.numpy as jnp
from jax import lax
from jax.experimental import pallas as pl
from jax.experimental.pallas import tpu as pltpu
from jax.sharding import Mesh, PartitionSpec as P

EPSILON = 1e-05
MASKED = -1e30
SCALE = 1.0 / math.sqrt(64)
BF = jnp.bfloat16
F32 = jnp.float32
CHIPS = ("z", "yl", "yh")
ROWS = 64
D = 1024


def sds(*shape, dtype=BF):
    return jax.ShapeDtypeStruct(shape, dtype)


def call(kernel, outs, ins, us=3, through=()):
    specs, arrays = [], []
    for item in ins:
        if isinstance(item, tuple):
            array, block, index = item
            if block is None:
                specs.append(pl.BlockSpec(memory_space=pltpu.SMEM))
            else:
                specs.append(pl.BlockSpec(block, functools.partial(lambda at, i: at, index)))
        else:
            array = item
            specs.append(
                pl.BlockSpec(
                    array.shape, functools.partial(lambda n, i: (0,) * n, array.ndim)
                )
            )
        arrays.append(array)
    out_specs = [
        pl.BlockSpec(o.shape, functools.partial(lambda n, i: (0,) * n, len(o.shape)))
        for o in outs
    ]
    n, m, k = len(ins), len(outs), len(through)

    def body(*refs):
        kernel(*refs[:n], *refs[n + k : n + k + m])

    return pl.pallas_call(
        body,
        grid=(1,),
        out_shape=list(outs) + [sds(*t.shape, dtype=t.dtype) for t in through],
        in_specs=specs + [pl.BlockSpec(memory_space=pl.ANY)] * k,
        out_specs=out_specs + [pl.BlockSpec(memory_space=pl.ANY)] * k,
        input_output_aliases={n + i: m + i for i in range(k)},
        compiler_params=pltpu.CompilerParams(vmem_limit_bytes=48 * 1024 * 1024),
        cost_estimate=pl.CostEstimate(
            flops=0, bytes_accessed=us * 3_000_000, transcendentals=0
        ),
    )(*arrays, *through)


def nn(a, b):
    return jnp.dot(a, b, preferred_element_type=F32)


def nt(a, b):
    return lax.dot_general(a, b, (((1,), (1,)), ((), ())), preferred_element_type=F32)


def tn(a, b):
    return lax.dot_general(a, b, (((0,), (0,)), ((), ())), preferred_element_type=F32)


def heads():
    return [(k, side, yh) for k, (side, yh) in enumerate([(0, 0), (0, 1), (1, 0), (1, 1)])]


def attn_tile(ref, yh):
    if len(ref.shape) == 5:
        return ref[0, :, yh, 0:128, :].reshape(D, 256)
    return ref[:, yh, 0:128, :].reshape(D, 256)


def ffn_tile(ref, yh, part):
    return ref[:, yh, 0:128, part * 256 : part * 256 + 256].reshape(D, 256)


def low_half(v):
    lane = lax.broadcasted_iota(jnp.int32, v.shape, 1)
    return jnp.where(lane < 64, v, 0.0)


def high_half(v):
    lane = lax.broadcasted_iota(jnp.int32, v.shape, 1)
    return jnp.where(lane >= 64, v, 0.0)


def mean_of(v):
    return jnp.sum(v, axis=-1, keepdims=True) * (1.0 / D)


def normal(v):
    centred = v - mean_of(v)
    inverse = lax.rsqrt(mean_of(centred * centred) + EPSILON)
    return centred * inverse, inverse


def layer_norm(v, gain, shift):
    return normal(v)[0] * gain + shift


def layer_norm_back(v, gain, grad):
    xhat, inverse = normal(v)
    d = grad * gain
    back = inverse * (d - mean_of(d) - xhat * mean_of(d * xhat))
    return (
        back,
        jnp.sum(grad * xhat, axis=0, keepdims=True),
        jnp.sum(grad, axis=0, keepdims=True),
    )


def gelu(u):
    return 0.5 * u * (1.0 + jnp.tanh(0.7978845608028654 * (u + 0.044715 * u * u * u)))


def gelu_slope(u):
    t = jnp.tanh(0.7978845608028654 * (u + 0.044715 * u * u * u))
    return 0.5 * (1.0 + t) + 0.5 * u * (1.0 - t * t) * (
        0.7978845608028654 * (1.0 + 3.0 * 0.044715 * u * u)
    )


def total(parts):
    a, b, c, d = [p[...].astype(F32) for p in parts]
    return (a + b) + (c + d)


def ln_row(lnp, layer, which, kind):
    return lnp[which, layer * 8 + 4 + kind : layer * 8 + 5 + kind, :]


def project(x, lnp, bias, wm, wo, layer, n1, q, kv):
    normed = layer_norm(x, ln_row(lnp, layer, 0, 0), ln_row(lnp, layer, 0, 1)).astype(BF)
    n1[...] = normed
    for k, side, yh in heads():
        tile = nn(normed, attn_tile((wm, wo)[side], yh))
        tile = tile + bias[yh, layer * 8 + side : layer * 8 + side + 1, :]
        q[k] = low_half(tile[:, 128:]).astype(BF)
        pair = tile[:, :128].astype(BF)
        for g in range(16):
            kv[g, kv.shape[1] - ROWS :, k * 128 : k * 128 + 128] = pair


def pack_kernel(*refs):
    sources, (msg, ffn), held, sem = refs[:9], refs[9:11], refs[11:20], refs[20]
    copies = [
        pltpu.make_async_copy(a, b, sem.at[i]) for i, (a, b) in enumerate(zip(sources, held))
    ]
    for c in copies:
        c.start()
    for c in copies:
        c.wait()
    pack(*held, msg, ffn)


def pack(qkv, out, up, down, gain, shift, inb, outb, upb, msg, ffn):
    wt = out[...].astype(F32).T
    dt = down[...].astype(F32).T
    inb_, gain_, shift_, outb_ = [r[...].astype(F32) for r in (inb, gain, shift, outb)]
    upb_ = upb[...].astype(F32)
    zero = jnp.zeros((1, 64), F32)
    def flat(v):
        return jnp.concatenate([v[0:1], v[1:2]], axis=1)
    rows = []
    for j in range(2):
        cols = slice(j * 64, j * 64 + 64)
        rows.append(jnp.concatenate([zero, inb_[1:2, cols], inb_[0:1, cols], zero], axis=1))
    ups = [upb_[:, :256], upb_[:, 256:]]
    tail = [flat(gain_), flat(shift_), flat(outb_), jnp.zeros((9, 256), F32)]
    for j in range(2):
        cols = slice(j * 64, j * 64 + 64)
        tile = jnp.concatenate(
            [
                qkv[1, :, cols].astype(F32),
                qkv[2, :, cols].astype(F32),
                qkv[0, :, cols].astype(F32),
                wt[:, cols],
            ],
            axis=1,
        ).astype(BF)
        small = jnp.concatenate([rows[j], rows[1 - j], ups[j], ups[1 - j], *tail]).astype(BF)
        for g in range(16):
            msg[j, g, 0:128, :] = tile
            msg[j, g, 128:144, :] = small
        ffn[j, :, 0:256] = up[:, j * 256 : j * 256 + 256]
        ffn[j, :, 256:512] = dt[:, j * 256 : j * 256 + 256].astype(BF)


def first_kernel(x, params, wm, wo, piece, n1, q, msg, lnp, bias):
    for layer in range(2):
        blocks = [params[layer, d, 0].astype(F32) for d in range(8)]
        for half in range(2):
            cols = slice(half * 128, half * 128 + 128)
            lnp[half, layer * 8 : layer * 8 + 8, :] = jnp.concatenate(
                [b[0:8, cols] for b in blocks], axis=1
            )
        for yh in range(2):
            bias[yh, layer * 8 : layer * 8 + 8, :] = params[layer, 0, yh].astype(F32)[0:8]
    project(x[...].astype(F32), lnp, bias, wm, wo, 0, n1, q, msg)
    rest = piece[...]
    for g in range(16):
        msg[g, 0:128, :] = rest


def next_kernel(mid, p0, p1, p2, p3, lnp, bias, wm, wo, y, n1, q, msg):
    out = (mid[...] + (total((p0, p1, p2, p3)) + ln_row(lnp, 0, 1, 2))).astype(BF)
    y[...] = out
    project(out.astype(F32), lnp, bias, wm, wo, 1, n1, q, msg)


def attend_spread_kernel(first, q, kv, wm, wo, piece, part, prob, att, copies):
    attend_kernel(first, q, kv, wm, wo, part, prob, att)
    rest = piece[...]
    for g in range(16):
        copies[g] = rest


def attend_kernel(first, q, kv, wm, wo, part, prob, att):
    length = 16 * ROWS
    qpos = first[0] + lax.broadcasted_iota(jnp.int32, (ROWS, length), 0)
    kpos = lax.broadcasted_iota(jnp.int32, (ROWS, length), 1)
    allowed = kpos <= qpos
    acc = None
    for k, side, yh in heads():
        pair = kv[:, :, k * 128 : k * 128 + 128].reshape(length, 128)
        scores = jnp.where(allowed, nt(q[k], pair) * SCALE, MASKED)
        e = jnp.exp(scores - jnp.max(scores, axis=-1, keepdims=True))
        p = e / jnp.sum(e, axis=-1, keepdims=True)
        prob[k] = p
        mixed = high_half(nn(p.astype(BF), pair)).astype(BF)
        att[k] = mixed
        term = nt(mixed, attn_tile((wm, wo)[side], yh)[:, 128:])
        acc = term if acc is None else acc + term
    part[...] = acc.astype(BF)


def feed(x, parts, lnp, bias, wm, wo, layer, part, mid, n2, pre, act):
    middle = x[...].astype(F32) + (total(parts) + ln_row(lnp, layer, 0, 2))
    mid[...] = middle
    normed = layer_norm(middle, ln_row(lnp, layer, 1, 0), ln_row(lnp, layer, 1, 1)).astype(BF)
    n2[...] = normed
    acc = None
    for k, side, yh in heads():
        w = (wm, wo)[side]
        u = nn(normed, ffn_tile(w, yh, 0))
        u = u + bias[yh, layer * 8 + 2 + side : layer * 8 + 3 + side, :]
        pre[k] = u
        a = gelu(u).astype(BF)
        act[k] = a
        term = nt(a, ffn_tile(w, yh, 1))
        acc = term if acc is None else acc + term
    part[...] = acc.astype(BF)


def feed_back(g, pre, wm, wo, dpre, part):
    acc = None
    for k, side, yh in heads():
        w = (wm, wo)[side]
        d = (nn(g, ffn_tile(w, yh, 1)) * gelu_slope(pre[k])).astype(BF)
        dpre[k] = d
        term = nt(d, ffn_tile(w, yh, 0))
        acc = term if acc is None else acc + term
    part[...] = acc.astype(BF)


def feed_kernel(x, p0, p1, p2, p3, lnp, bias, wm, wo, part, mid, n2, pre, act):
    feed(x, (p0, p1, p2, p3), lnp, bias, wm, wo, 0, part, mid, n2, pre, act)


def turn_kernel(x, p0, p1, p2, p3, lnp, bias, wm, wo, g, part, mid, n2, pre, act, dpre, back):
    feed(x, (p0, p1, p2, p3), lnp, bias, wm, wo, 1, part, mid, n2, pre, act)
    feed_back(g[...], pre, wm, wo, dpre, back)


def grad_ffn_kernel(n2, g, dpre, act, mine, other, sums, row):
    for k, side, yh in heads():
        out = (mine, other)[side]
        out[:, yh, :, 0:256] = tn(n2[...], dpre[k]).astype(BF).reshape(8, 128, 256)
        out[:, yh, :, 256:512] = tn(g[...], act[k]).astype(BF).reshape(8, 128, 256)
        sums[k : k + 1, :] = jnp.sum(dpre[k].astype(F32), axis=0, keepdims=True)
    row[...] = jnp.sum(g[...].astype(F32), axis=0, keepdims=True)


def attend_back(layer, g, mid, parts, lnp, wm, wo, prob, q, kv, dmid, bg, dq, dkv, rows):
    back, gg, gs = layer_norm_back(mid[...], ln_row(lnp, layer, 1, 0), total(parts))
    dm = g[...].astype(F32) + back
    dmid[...] = dm
    low = dm.astype(BF)
    bg[...] = low
    rows[0:1, :] = gg
    rows[1:2, :] = gs
    rows[2:3, :] = jnp.sum(low.astype(F32), axis=0, keepdims=True)
    at = dkv.shape[1] - ROWS
    for k, side, yh in heads():
        pair = kv[:, :, k * 128 : k * 128 + 128].reshape(16 * ROWS, 128)
        da = high_half(nn(low, attn_tile((wm, wo)[side], yh)[:, 128:])).astype(BF)
        p = prob[k]
        dp = nt(da, pair)
        ds = (p * (dp - jnp.sum(p * dp, axis=-1, keepdims=True))).astype(BF)
        dq[k] = low_half(nn(ds, pair) * SCALE).astype(BF)
        both = tn(ds, q[k]) * SCALE + tn(p.astype(BF), da)
        dkv[:, at:, k * 128 : k * 128 + 128] = both.astype(BF).reshape(16, ROWS, 128)


def add_into(msg, gm, gr):
    for i in range(8):
        for j in range(2):
            msg[2 * i + j, 0:128, :] = (gm[i, j].astype(F32) + gr[i, j].astype(F32)).astype(BF)


def attend_back_kernel(
    g, mid, p0, p1, p2, p3, lnp, wm, wo, prob, q, kv, gm, gr, dmid, bg, dq, dkv, rows, msg
):
    attend_back(1, g, mid, (p0, p1, p2, p3), lnp, wm, wo, prob, q, kv, dmid, bg, dq, dkv, rows)
    add_into(msg, gm, gr)


def attend_back_first_kernel(
    g, mid, p0, p1, p2, p3, lnp, wm, wo, prob, q, kv, gm, gr, dmid, bg, dq, msg, rows
):
    attend_back(0, g, mid, (p0, p1, p2, p3), lnp, wm, wo, prob, q, kv, dmid, bg, dq, msg, rows)
    add_into(msg, gm, gr)


def project_back_kernel(dkv, dq, wm, wo, dproj, part, sums):
    pairs = jnp.sum(dkv[...].astype(F32), axis=0).astype(BF)
    acc = None
    for k, side, yh in heads():
        tile = jnp.concatenate([pairs[:, k * 128 : k * 128 + 128], dq[k]], axis=1)
        dproj[k] = tile
        sums[k : k + 1, :] = jnp.sum(tile.astype(F32), axis=0, keepdims=True)
        term = nt(tile, attn_tile((wm, wo)[side], yh))
        acc = term if acc is None else acc + term
    part[...] = acc.astype(BF)


def grad_attn_kernel(n1, bg, att, dproj, mine, other):
    for k, side, yh in heads():
        out = (mine, other)[side]
        first = tn(n1[...], dproj[k])
        second = tn(bg[...], att[k])
        out[:, yh, :, 0:128] = first[:, :128].astype(BF).reshape(8, 128, 128)
        out[:, yh, :, 128:] = (first[:, 128:] + second).astype(BF).reshape(8, 128, 128)


def hand_down_kernel(x, dmid, p0, p1, p2, p3, lnp, pre, wm, wo, dx, dpre, part, rows):
    back, gg, gs = layer_norm_back(
        x[...].astype(F32), ln_row(lnp, 1, 0, 0), total((p0, p1, p2, p3))
    )
    g = (dmid[...] + back).astype(BF)
    dx[...] = g
    rows[0:1, :] = gg
    rows[1:2, :] = gs
    feed_back(g, pre, wm, wo, dpre, part)


def last_kernel(
    x, dmid, p0, p1, p2, p3, lnp, gm0, gr0, gm1, gr1,
    r0, o0, a0, u0, h1, r1, o1, a1, u1, dx, msg,
):
    back, gg, gs = layer_norm_back(
        x[...].astype(F32), ln_row(lnp, 0, 0, 0), total((p0, p1, p2, p3))
    )
    dx[...] = (dmid[...] + back).astype(BF)
    lines = []
    for first, rows, ob, a, u in (
        ((gg, gs), r0, o0, a0, u0),
        ((h1[0:1, :], h1[1:2, :]), r1, o1, a1, u1),
    ):
        lines.append(
            (
                a[...],
                u[...],
                (
                    (first[0], rows[0:1, :]),
                    (first[1], rows[1:2, :]),
                    (rows[2:3, :], ob[...]),
                ),
            )
        )
    for d in range(8):
        cols = slice(d * 128, d * 128 + 128)
        for yh in range(2):
            block = []
            for a, u, pairs in lines:
                block += [a[yh : yh + 1], a[2 + yh : 3 + yh], u[yh : yh + 1], u[2 + yh : 3 + yh]]
                block += [jnp.concatenate([f[:, cols], s[:, cols]], axis=1) for f, s in pairs]
            block.append(jnp.zeros((2, 256), F32))
            g = 2 * d + yh
            for at, gm, gr in ((0, gm0, gr0), (256, gm1, gr1)):
                both = gm[d, yh].astype(F32) + gr[d, yh].astype(F32)
                msg[g, 0:128, at : at + 256] = both.astype(BF)
            msg[g, 128:144, 0:256] = jnp.concatenate(block).astype(BF)
            msg[g, 128:144, 256:512] = jnp.zeros((16, 256), BF)


def settle_kernel(core, l0, l1, keep, send):
    first = core[0] == 0
    for j in range(2):
        cols = slice(j * 256, j * 256 + 256)
        a = jnp.sum(l0[:, 0:128, cols].astype(F32), axis=0)
        b = jnp.sum(l1[:, 0:128, cols].astype(F32), axis=0)
        keep[:, cols] = jnp.where(first, a, b)
        send[:, cols] = jnp.where(first, b, a)


def settle_tail_kernel(core, tail, keep, send):
    first = core[0] == 0
    t = jnp.sum(tail[...].astype(F32), axis=0)
    a, b = t[0:128, 0:256], t[0:128, 256:512]
    small = t[128:144, 0:256]
    pad = jnp.zeros((1, 256), F32)
    c, d = jnp.concatenate([small[0:7], pad]), jnp.concatenate([small[7:14], pad])
    keep[0:128, :] = jnp.where(first, a, b)
    send[0:128, :] = jnp.where(first, b, a)
    keep[128:136, :] = jnp.where(first, c, d)
    send[128:136, :] = jnp.where(first, d, c)


def unpack_kernel(
    core, fk, fg, ak, ag, qkv, out, up, down, gain, shift, inb, outb, upb
):
    first = core[0] == 0

    def ordered(k, g):
        return jnp.where(first, k, g), jnp.where(first, g, k)

    a = ordered(ak[0:128, :], ag[0:128, :])
    for i, at in enumerate((128, 0, 64)):
        qkv[i] = jnp.concatenate([t[:, at : at + 64] for t in a], axis=1)
    out[...] = jnp.concatenate([t[:, 192:256] for t in a], axis=1).T
    ups = ordered(fk[:, 0:256], fg[:, 0:256])
    downs = ordered(fk[:, 256:512], fg[:, 256:512])
    for j in range(2):
        up[:, j * 256 : j * 256 + 256] = ups[j]
        down[j * 256 : j * 256 + 256, :] = downs[j].T
    s0, s1 = ordered(ak[128:136, :], ag[128:136, :])
    for row, ref in ((4, gain), (5, shift), (6, outb)):
        t = s0[row : row + 1] + s1[row : row + 1]
        ref[0:1, :] = t[:, 0:128]
        ref[1:2, :] = t[:, 128:256]
    sides = [s0[0:1] + s1[1:2], s0[1:2] + s1[0:1]]
    inb[0:1, :] = jnp.concatenate([t[:, 128:192] for t in sides], axis=1)
    inb[1:2, :] = jnp.concatenate([t[:, 64:128] for t in sides], axis=1)
    upb[...] = jnp.concatenate([s0[2:3] + s1[3:4], s0[3:4] + s1[2:3]], axis=1)


def swap_cores(v):
    return lax.ppermute(v, "s", [(0, 1), (1, 0)])


def all_parts(part):
    got = [lax.ppermute(part, "x", [(i, i ^ k) for i in range(4)]) for k in (1, 3, 2)]
    return part, got[0], got[2], got[1]


def exchange(v, axes=CHIPS):
    return lax.all_to_all(v, axes, 0, 0, tiled=True)


def by_layer(mine, first, second):
    return jnp.where(mine == 0, first, second)


def whole_rows(s, yh, a, b):
    keep, send = by_layer(s, a, b), by_layer(s, b, a)
    got = swap_cores(send)
    rows = jnp.stack([by_layer(s, keep, got), by_layer(s, got, keep)])
    far = lax.ppermute(rows, "yh", [(0, 1), (1, 0)])
    return jnp.concatenate([by_layer(yh, rows, far), by_layer(yh, far, rows)], axis=1).reshape(
        1, 2, 1, 128, D
    )


def local(inputs, cotangent, wqkv, wout, wup, wdown, gain, shift, inb, outb, upb):
    s, yh = lax.axis_index("s"), lax.axis_index("yh")
    first = (lax.axis_index(CHIPS) * ROWS).astype(jnp.int32).reshape(1)

    def own_rows(v):
        return lax.dynamic_slice(v, (s, 0, yh * ROWS, 0), (1, 1, ROWS, D)).reshape(ROWS, D)

    x, cot = own_rows(inputs), own_rows(cotangent)
    core = (s.astype(jnp.int32).reshape(1), None, None)
    weights = [
        jnp.moveaxis(wqkv[0], 1, 0), wout[0], wup[0], wdown[0],
        gain[0], shift[0], inb[0], outb[0], upb,
    ]
    msg, ffn = pl.pallas_call(
        pack_kernel,
        out_shape=[sds(2, 16, 144, 256), sds(2, 128, 512)],
        in_specs=[pl.BlockSpec(memory_space=pl.ANY)] * 9,
        out_specs=[pl.BlockSpec(memory_space=pltpu.VMEM)] * 2,
        scratch_shapes=[pltpu.VMEM(w.shape, BF) for w in weights]
        + [pltpu.SemaphoreType.DMA((9,))],
        compiler_params=pltpu.CompilerParams(vmem_limit_bytes=48 * 1024 * 1024),
    )(*weights)
    u = exchange(msg.reshape(32, 144, 256), ("s", *CHIPS)).reshape(2, 16, 144, 256)
    got = swap_cores(by_layer(s, ffn[1], ffn[0]))
    piece0, piece1 = by_layer(s, ffn[0], got), by_layer(s, got, ffn[1])
    u = u.reshape(2, 8, 2, 144, 256)
    am = [(u, (1, 8, 2, 144, 256), (l, 0, 0, 0, 0)) for l in range(2)]
    ao = [swap_cores(u[l]) for l in range(2)]
    kinds = dict(n1=sds(ROWS, D), q=sds(4, ROWS, 128))
    n10, q0, msg, lnp, bias = call(
        first_kernel,
        [kinds["n1"], kinds["q"], sds(16, 192, 512), sds(2, 16, D, dtype=F32), sds(2, 16, 256, dtype=F32)],
        [x, (u, (2, 8, 2, 16, 256), (0, 0, 0, 8, 0)), am[0], ao[0], piece0],
    )
    got0 = exchange(msg)
    kv0 = (got0, (16, ROWS, 512), (0, 2, 0))
    f0 = (got0.reshape(8, 2, 192, 512), (8, 2, 128, 512), (0, 0, 0, 0))
    f0o = (swap_cores(got0).reshape(8, 2, 192, 512), (8, 2, 128, 512), (0, 0, 0, 0))
    attend_outs = [sds(ROWS, D), sds(4, ROWS, D, dtype=F32), sds(4, ROWS, 128)]
    feed_outs = [
        sds(ROWS, D), sds(ROWS, D, dtype=F32), sds(ROWS, D),
        sds(4, ROWS, 256, dtype=F32), sds(4, ROWS, 256),
    ]
    part, prob0, att0, copies = call(
        attend_spread_kernel,
        attend_outs + [sds(16, 128, 512)],
        [(first, None, None), q0, kv0, am[0], ao[0], piece1],
    )
    f1 = exchange(copies)
    part, mid0, n20, pre0, act0 = call(
        feed_kernel, feed_outs, [x, *all_parts(part), lnp, bias, f0, f0o]
    )
    y0, n11, q1, msg, f1 = call(
        next_kernel,
        [sds(ROWS, D), kinds["n1"], kinds["q"], sds(16, ROWS, 512)],
        [mid0, *all_parts(part), lnp, bias, am[1], ao[1]],
        through=[f1],
    )
    f1 = f1.reshape(8, 2, 128, 512)
    f1o = swap_cores(f1)
    kv1 = exchange(msg)
    part, prob1, att1 = call(attend_kernel, attend_outs, [(first, None, None), q1, kv1, am[1], ao[1]])
    part, mid1, n21, pre1, act1, dpre1, back = call(
        turn_kernel,
        feed_outs + [sds(4, ROWS, 256), sds(ROWS, D)],
        [y0, *all_parts(part), lnp, bias, f1, f1o, cot],
    )
    backs = all_parts(back)
    a, b, c, d = [p.astype(F32) for p in all_parts(part)]
    y1 = (mid1 + (((a + b) + (c + d)) + lnp[1, 14:15])).astype(BF)
    grad_ffn_outs = [
        sds(8, 2, 128, 512), sds(8, 2, 128, 512), sds(4, 256, dtype=F32), sds(1, D, dtype=F32)
    ]
    gfm1, gfo1, gub1, ob11 = call(grad_ffn_kernel, grad_ffn_outs, [n21, cot, dpre1, act1])
    gfr1 = swap_cores(gfo1)
    back_outs = [sds(ROWS, D, dtype=F32), sds(ROWS, D), sds(4, ROWS, 128)]
    rows_out = sds(8, D, dtype=F32)
    dmid1, bg1, dq1, dkv, rows1, l1 = call(
        attend_back_kernel,
        back_outs + [sds(16, ROWS, 512), rows_out, sds(16, 128, 512)],
        [cot, mid1, *backs, lnp, am[1], ao[1], prob1, q1, kv1, gfm1, gfr1],
    )
    dkv = exchange(dkv)
    project_outs = [sds(4, ROWS, 256), sds(ROWS, D), sds(4, 256, dtype=F32)]
    dproj1, part, gib1, l1 = call(
        project_back_kernel, project_outs, [dkv, dq1, am[1], ao[1]], through=[l1]
    )
    l1 = exchange(l1)
    backs = all_parts(part)
    grad_attn_outs = [sds(8, 2, 128, 256), sds(8, 2, 128, 256)]
    gam1, gao1 = call(grad_attn_kernel, grad_attn_outs, [n11, bg1, att1, dproj1])
    gar1 = swap_cores(gao1)
    dx1, dpre0, part, head1 = call(
        hand_down_kernel,
        [sds(ROWS, D), sds(4, ROWS, 256), sds(ROWS, D), rows_out],
        [y0, dmid1, *backs, lnp, pre0, f0, f0o],
    )
    backs = all_parts(part)
    gfm0, gfo0, gub0, ob10 = call(grad_ffn_kernel, grad_ffn_outs, [n20, dx1, dpre0, act0])
    gfr0 = swap_cores(gfo0)
    dmid0, bg0, dq0, msg, rows0, l1 = call(
        attend_back_first_kernel,
        back_outs + [sds(16, 192, 512), rows_out],
        [dx1, mid0, *backs, lnp, am[0], ao[0], prob0, q0, kv0, gfm0, gfr0],
        through=[l1],
    )
    l0 = exchange(msg)
    dproj0, part, gib0 = call(
        project_back_kernel, project_outs, [(l0, (16, ROWS, 512), (0, 2, 0)), dq0, am[0], ao[0]]
    )
    backs = all_parts(part)
    gam0, gao0 = call(grad_attn_kernel, grad_attn_outs, [n10, bg0, att0, dproj0])
    gar0 = swap_cores(gao0)
    dx0, msg = call(
        last_kernel,
        [sds(ROWS, D), sds(16, 144, 512)],
        [x, dmid0, *backs, lnp, gam0, gar0, gam1, gar1, rows0, ob10, gib0, gub0, head1, rows1, ob11, gib1, gub1],
    )
    tail = exchange(msg)
    acts = whole_rows(s, yh, y0, y1)
    grads = whole_rows(s, yh, dx0, dx1)
    f = functools.partial(sds, dtype=F32)
    fk, send = call(
        settle_kernel,
        [f(128, 512), f(128, 512)],
        [core, (l0, (16, 128, 512), (0, 0, 0)), l1],
    )
    fg = swap_cores(send)
    ak, send = call(settle_tail_kernel, [f(136, 256), f(136, 256)], [core, tail])
    gq, go, gu, gd, gg, gs, gi, gb, gub = call(
        unpack_kernel,
        [f(3, 128, 128), f(128, 128), f(128, 512), f(512, 128), f(2, 128), f(2, 128), f(2, 128), f(2, 128), f(1, 512)],
        [core, fk, fg, ak, swap_cores(send)],
    )
    return (
        acts, grads, jnp.moveaxis(gq, 0, 1)[None], go[None], gu[None], gd[None],
        gg[None], gs[None], gi[None], gb[None], gub,
    )


def solution(mesh):
    parts = Mesh(mesh.devices.reshape(2, 4, 2, 2, 4), ("s", "z", "yl", "yh", "x"))
    dp, tp = ("z", "yl"), ("yh", "x")
    return jax.shard_map(
        local,
        mesh=parts,
        in_specs=(
            P(None, None, dp, None),
            P(None, None, dp, None),
            P("s", dp, None, tp),
            P("s", tp, dp),
            P("s", dp, tp),
            P("s", tp, dp),
            P("s", None, dp),
            P("s", None, dp),
            P("s", None, tp),
            P("s", None, dp),
            P("s", tp),
        ),
        out_specs=(
            P("s", None, None, dp, None),
            P("s", None, None, dp, None),
            P("s", dp, None, tp),
            P("s", tp, dp),
            P("s", dp, tp),
            P("s", tp, dp),
            P("s", None, dp),
            P("s", None, dp),
            P("s", None, tp),
            P("s", None, dp),
            P("s", tp),
        ),
        check_vma=False,
    )
```

```python
import functools
import math

import jax
import jax.numpy as jnp
from jax import lax
from jax.experimental import pallas as pl
from jax.experimental.pallas import tpu as pltpu
from jax.sharding import Mesh, PartitionSpec as P

EPSILON = 1e-05
MASKED = -1e30
SCALE = 1.0 / math.sqrt(64)
BF = jnp.bfloat16
F32 = jnp.float32
CHIPS = ("z", "yl", "yh")
ROWS = 64
D = 1024


def sds(*shape, dtype=BF):
    return jax.ShapeDtypeStruct(shape, dtype)


def kept(*shape, dtype=BF):
    return ("kept", pltpu.HBM(shape, dtype))


def message(*shape):
    return pltpu.HBM(shape, BF)


def call(kernel, outs, ins, us=3, through=()):
    n, m, k = len(ins), len(outs), len(through)
    held = [i for i, o in enumerate(outs) if isinstance(o, tuple)]
    outs = [o[1] if isinstance(o, tuple) else o for o in outs]
    specs, arrays = [], []
    for item in ins:
        if isinstance(item, tuple):
            array, block, index = item
            if block is None:
                specs.append(pl.BlockSpec(memory_space=pltpu.SMEM))
            else:
                specs.append(
                    pl.BlockSpec(
                        block,
                        functools.partial(lambda at, i: at, index),
                        pipeline_mode=pl.Buffered(1),
                    )
                )
        else:
            array = item
            specs.append(
                pl.BlockSpec(
                    array.shape,
                    functools.partial(lambda n, i: (0,) * n, array.ndim),
                    pipeline_mode=pl.Buffered(1),
                )
            )
        arrays.append(array)
    out_specs = [
        pl.BlockSpec(o.shape, functools.partial(lambda n, i: (0,) * n, len(o.shape)))
        for o in outs
    ]

    def body(*refs):
        kernel(*refs[:n], *refs[n + k : n + k + m])

    results = pl.pallas_call(
        body,
        grid=(1,),
        out_shape=list(outs) + [pltpu.HBM(t.shape, t.dtype) for t in through],
        in_specs=specs + [pl.BlockSpec(memory_space=pl.ANY)] * k,
        out_specs=out_specs + [pl.BlockSpec(memory_space=pl.ANY)] * k,
        input_output_aliases={n + i: m + i for i in range(k)},
        compiler_params=pltpu.CompilerParams(vmem_limit_bytes=48 * 1024 * 1024),
        cost_estimate=pl.CostEstimate(
            flops=0, bytes_accessed=us * 3_000_000, transcendentals=0
        ),
    )(*arrays, *[pltpu.with_memory_space_constraint(t, pltpu.HBM) for t in through])
    return [
        pltpu.with_memory_space_constraint(r, pltpu.HBM) if i in held else r
        for i, r in enumerate(results)
    ]


def nn(a, b):
    return jnp.dot(a, b, preferred_element_type=F32)


def nt(a, b):
    return lax.dot_general(a, b, (((1,), (1,)), ((), ())), preferred_element_type=F32)


def tn(a, b):
    return lax.dot_general(a, b, (((0,), (0,)), ((), ())), preferred_element_type=F32)


def heads():
    return [(k, side, yh) for k, (side, yh) in enumerate([(0, 0), (0, 1), (1, 0), (1, 1)])]


def attn_tile(ref, yh):
    return ref[:, yh, 0:128, :].reshape(D, 256)


def ffn_tile(ref, yh, part):
    return ref[:, yh, 0:128, part * 256 : part * 256 + 256].reshape(D, 256)


def low_half(v):
    lane = lax.broadcasted_iota(jnp.int32, v.shape, 1)
    return jnp.where(lane < 64, v, 0.0)


def high_half(v):
    lane = lax.broadcasted_iota(jnp.int32, v.shape, 1)
    return jnp.where(lane >= 64, v, 0.0)


def mean_of(v):
    return jnp.sum(v, axis=-1, keepdims=True) * (1.0 / D)


def normal(v):
    centred = v - mean_of(v)
    inverse = lax.rsqrt(mean_of(centred * centred) + EPSILON)
    return centred * inverse, inverse


def layer_norm(v, gain, shift):
    return normal(v)[0] * gain + shift


def layer_norm_back(v, gain, grad):
    xhat, inverse = normal(v)
    d = grad * gain
    back = inverse * (d - mean_of(d) - xhat * mean_of(d * xhat))
    return (
        back,
        jnp.sum(grad * xhat, axis=0, keepdims=True),
        jnp.sum(grad, axis=0, keepdims=True),
    )


def gelu(u):
    return 0.5 * u * (1.0 + jnp.tanh(0.7978845608028654 * (u + 0.044715 * u * u * u)))


def gelu_slope(u):
    t = jnp.tanh(0.7978845608028654 * (u + 0.044715 * u * u * u))
    return 0.5 * (1.0 + t) + 0.5 * u * (1.0 - t * t) * (
        0.7978845608028654 * (1.0 + 3.0 * 0.044715 * u * u)
    )


def total(parts):
    a, b, c, d = [p[...].astype(F32) for p in parts]
    return (a + b) + (c + d)


def ln_row(lnp, layer, which, kind):
    return lnp[which, layer * 8 + 4 + kind : layer * 8 + 5 + kind, :]


def project(x, lnp, bias, wm, wo, layer, n1, q, kv):
    normed = layer_norm(x, ln_row(lnp, layer, 0, 0), ln_row(lnp, layer, 0, 1)).astype(BF)
    n1[...] = normed
    for k, side, yh in heads():
        tile = nn(normed, attn_tile((wm, wo)[side], yh))
        tile = tile + bias[yh, layer * 8 + side : layer * 8 + side + 1, :]
        q[k] = low_half(tile[:, 128:]).astype(BF)
        pair = tile[:, :128].astype(BF)
        for g in range(16):
            kv[g, kv.shape[1] - ROWS :, k * 128 : k * 128 + 128] = pair


def pack_kernel(core, *refs):
    sources, (keep, send), held, sem = refs[:9], refs[9:11], refs[11:20], refs[20]
    copies = [
        pltpu.make_async_copy(a, b, sem.at[i]) for i, (a, b) in enumerate(zip(sources, held))
    ]
    for c in copies:
        c.start()
    for c in copies:
        c.wait()
    pack(core, *held, keep, send)


def pack(core, qkv, out, up, down, gain, shift, inb, outb, upb, keep, send):
    wt = out[...].astype(F32).T
    dt = down[...].astype(F32).T
    inb_, gain_, shift_, outb_ = [r[...].astype(F32) for r in (inb, gain, shift, outb)]
    upb_ = upb[...].astype(F32)
    zero = jnp.zeros((1, 64), F32)
    def flat(v):
        return jnp.concatenate([v[0:1], v[1:2]], axis=1)
    rows = []
    for j in range(2):
        cols = slice(j * 64, j * 64 + 64)
        rows.append(jnp.concatenate([zero, inb_[1:2, cols], inb_[0:1, cols], zero], axis=1))
    ups = [upb_[:, :256], upb_[:, 256:]]
    rest = [flat(gain_), flat(shift_), flat(outb_), jnp.zeros((9, 256), F32)]
    halves = []
    for j in range(2):
        cols = slice(j * 64, j * 64 + 64)
        wide = slice(j * 256, j * 256 + 256)
        halves.append(
            (
                up[:, wide].astype(F32),
                dt[:, wide],
                jnp.concatenate([qkv[i, :, cols].astype(F32) for i in (1, 2, 0)] + [wt[:, cols]], axis=1),
                jnp.concatenate([rows[j], rows[1 - j], ups[j], ups[1 - j], *rest]),
            )
        )
    first = core[0] == 0
    for ref, pair in ((keep, halves), (send, halves[::-1])):
        values = [jnp.where(first, a, b).astype(BF) for a, b in zip(*pair)]
        ref[0:128, 0:256] = values[0]
        ref[0:128, 256:512] = values[1]
        ref[0:128, 512:768] = values[2]
        ref[128:144, 512:768] = values[3]


def spread_kernel(core, keep, got, msg, ffn0, ffn1):
    first = core[0] == 0
    k, o = keep[...], got[...]
    lower, upper = jnp.where(first, k, o), jnp.where(first, o, k)
    small = jnp.concatenate(
        [v[128:144, 512:768].astype(F32)[0:8] for v in (lower, upper)]
    ).astype(BF)
    tiles = lower[0:128, 512:768], upper[0:128, 512:768]
    for g in range(16):
        msg[g, 0:128, :] = tiles[0]
        msg[g, 128:256, :] = tiles[1]
        msg[g, 256:272, :] = small
    ffn0[...] = lower[0:128, 0:512]
    ffn1[...] = upper[0:128, 0:512]


def first_kernel(x, params, wm, wo, piece, n1, q, msg, lnp, bias):
    for layer in range(2):
        part = slice(layer * 8, layer * 8 + 8)
        blocks = [params[d, 0].astype(F32)[part] for d in range(8)]
        for half in range(2):
            cols = slice(half * 128, half * 128 + 128)
            lnp[half, part, :] = jnp.concatenate([b[:, cols] for b in blocks], axis=1)
        for yh in range(2):
            bias[yh, part, :] = params[0, yh].astype(F32)[part]
    project(x[...].astype(F32), lnp, bias, wm, wo, 0, n1, q, msg)
    rest = piece[...]
    for g in range(16):
        msg[g, 0:128, :] = rest


def next_kernel(mid, p0, p1, p2, p3, lnp, bias, wm, wo, y, n1, q, msg):
    out = (mid[...] + (total((p0, p1, p2, p3)) + ln_row(lnp, 0, 1, 2))).astype(BF)
    y[...] = out
    project(out.astype(F32), lnp, bias, wm, wo, 1, n1, q, msg)


def attend_spread_kernel(first, q, kv, wm, wo, piece, part, prob, att, copies):
    attend_kernel(first, q, kv, wm, wo, part, prob, att)
    rest = piece[...]
    for g in range(16):
        copies[g] = rest


def attend_kernel(first, q, kv, wm, wo, part, prob, att):
    length = 16 * ROWS
    qpos = first[0] + lax.broadcasted_iota(jnp.int32, (ROWS, length), 0)
    kpos = lax.broadcasted_iota(jnp.int32, (ROWS, length), 1)
    allowed = kpos <= qpos
    acc = None
    for k, side, yh in heads():
        pair = kv[:, :, k * 128 : k * 128 + 128].reshape(length, 128)
        scores = jnp.where(allowed, nt(q[k], pair) * SCALE, MASKED)
        e = jnp.exp(scores - jnp.max(scores, axis=-1, keepdims=True))
        p = e / jnp.sum(e, axis=-1, keepdims=True)
        prob[k] = p
        mixed = high_half(nn(p.astype(BF), pair)).astype(BF)
        att[k] = mixed
        term = nt(mixed, attn_tile((wm, wo)[side], yh)[:, 128:])
        acc = term if acc is None else acc + term
    part[...] = acc.astype(BF)


def feed(x, parts, lnp, bias, wm, wo, layer, part, mid, n2, pre, act):
    middle = x[...].astype(F32) + (total(parts) + ln_row(lnp, layer, 0, 2))
    mid[...] = middle
    normed = layer_norm(middle, ln_row(lnp, layer, 1, 0), ln_row(lnp, layer, 1, 1)).astype(BF)
    n2[...] = normed
    acc = None
    for k, side, yh in heads():
        w = (wm, wo)[side]
        u = nn(normed, ffn_tile(w, yh, 0))
        u = u + bias[yh, layer * 8 + 2 + side : layer * 8 + 3 + side, :]
        pre[k] = u
        a = gelu(u).astype(BF)
        act[k] = a
        term = nt(a, ffn_tile(w, yh, 1))
        acc = term if acc is None else acc + term
    part[...] = acc.astype(BF)


def feed_back(g, pre, wm, wo, dpre, part):
    acc = None
    for k, side, yh in heads():
        w = (wm, wo)[side]
        d = (nn(g, ffn_tile(w, yh, 1)) * gelu_slope(pre[k])).astype(BF)
        dpre[k] = d
        term = nt(d, ffn_tile(w, yh, 0))
        acc = term if acc is None else acc + term
    part[...] = acc.astype(BF)


def feed_kernel(x, p0, p1, p2, p3, lnp, bias, wm, wo, part, mid, n2, pre, act):
    feed(x, (p0, p1, p2, p3), lnp, bias, wm, wo, 0, part, mid, n2, pre, act)


def turn_kernel(x, p0, p1, p2, p3, lnp, bias, wm, wo, g, part, mid, n2, pre, act, dpre, back):
    feed(x, (p0, p1, p2, p3), lnp, bias, wm, wo, 1, part, mid, n2, pre, act)
    feed_back(g[...], pre, wm, wo, dpre, back)


def finish_kernel(mid, p0, p1, p2, p3, lnp, y):
    y[...] = (mid[...] + (total((p0, p1, p2, p3)) + ln_row(lnp, 1, 1, 2))).astype(BF)


def grad_ffn_kernel(n2, g, dpre, act, mine, other, sums, row):
    for k, side, yh in heads():
        out = (mine, other)[side]
        out[:, yh, :, 0:256] = tn(n2[...], dpre[k]).astype(BF).reshape(8, 128, 256)
        out[:, yh, :, 256:512] = tn(g[...], act[k]).astype(BF).reshape(8, 128, 256)
        sums[k : k + 1, :] = jnp.sum(dpre[k].astype(F32), axis=0, keepdims=True)
    row[...] = jnp.sum(g[...].astype(F32), axis=0, keepdims=True)


def attend_back(layer, g, mid, parts, lnp, wm, wo, prob, q, kv, dmid, bg, dq, dkv, rows):
    back, gg, gs = layer_norm_back(mid[...], ln_row(lnp, layer, 1, 0), total(parts))
    dm = g[...].astype(F32) + back
    dmid[...] = dm
    low = dm.astype(BF)
    bg[...] = low
    rows[0:1, :] = gg
    rows[1:2, :] = gs
    rows[2:3, :] = jnp.sum(low.astype(F32), axis=0, keepdims=True)
    at = dkv.shape[1] - ROWS
    for k, side, yh in heads():
        pair = kv[:, :, k * 128 : k * 128 + 128].reshape(16 * ROWS, 128)
        da = high_half(nn(low, attn_tile((wm, wo)[side], yh)[:, 128:])).astype(BF)
        p = prob[k]
        dp = nt(da, pair)
        ds = (p * (dp - jnp.sum(p * dp, axis=-1, keepdims=True))).astype(BF)
        dq[k] = low_half(nn(ds, pair) * SCALE).astype(BF)
        both = tn(ds, q[k]) * SCALE + tn(p.astype(BF), da)
        dkv[:, at:, k * 128 : k * 128 + 128] = both.astype(BF).reshape(16, ROWS, 128)


def attend_back_kernel(g, mid, p0, p1, p2, p3, lnp, wm, wo, prob, q, kv, dmid, bg, dq, dkv, rows):
    attend_back(1, g, mid, (p0, p1, p2, p3), lnp, wm, wo, prob, q, kv, dmid, bg, dq, dkv, rows)


def attend_back_first_kernel(
    g, mid, p0, p1, p2, p3, lnp, wm, wo, prob, q, kv, dmid, bg, dq, dkv, rows
):
    attend_back(0, g, mid, (p0, p1, p2, p3), lnp, wm, wo, prob, q, kv, dmid, bg, dq, dkv, rows)


def add_into(msg, at, gm, gr):
    for i in range(8):
        for j in range(2):
            both = gm[i, j].astype(F32) + gr[i, j].astype(F32)
            msg[2 * i + j, 0:128, at : at + gm.shape[3]] = both.astype(BF)


def add_kernel(gm, gr, msg):
    add_into(msg, 0, gm, gr)


def join_kernel(fm, fr, am, ar, msg):
    add_into(msg, 0, fm, fr)
    add_into(msg, 512, am, ar)


def mark_kernel(rows, out):
    out[...] = rows[0:1, 0:128]


def project_back_kernel(dkv, dq, wm, wo, dproj, part, sums):
    pairs = jnp.sum(dkv[...].astype(F32), axis=0).astype(BF)
    acc = None
    for k, side, yh in heads():
        tile = jnp.concatenate([pairs[:, k * 128 : k * 128 + 128], dq[k]], axis=1)
        dproj[k] = tile
        sums[k : k + 1, :] = jnp.sum(tile.astype(F32), axis=0, keepdims=True)
        term = nt(tile, attn_tile((wm, wo)[side], yh))
        acc = term if acc is None else acc + term
    part[...] = acc.astype(BF)


def grad_attn_kernel(n1, bg, att, dproj, mine, other):
    for k, side, yh in heads():
        out = (mine, other)[side]
        first = tn(n1[...], dproj[k])
        second = tn(bg[...], att[k])
        out[:, yh, :, 0:128] = first[:, :128].astype(BF).reshape(8, 128, 128)
        out[:, yh, :, 128:] = (first[:, 128:] + second).astype(BF).reshape(8, 128, 128)


def hand_down_kernel(x, dmid, p0, p1, p2, p3, lnp, pre, wm, wo, dx, dpre, part, rows):
    back, gg, gs = layer_norm_back(
        x[...].astype(F32), ln_row(lnp, 1, 0, 0), total((p0, p1, p2, p3))
    )
    g = (dmid[...] + back).astype(BF)
    dx[...] = g
    rows[0:1, :] = gg
    rows[1:2, :] = gs
    feed_back(g, pre, wm, wo, dpre, part)


def last_kernel(
    x, dmid, p0, p1, p2, p3, lnp, gm, gr,
    r0, o0, a0, u0, h1, r1, o1, a1, u1, dx, msg,
):
    back, gg, gs = layer_norm_back(
        x[...].astype(F32), ln_row(lnp, 0, 0, 0), total((p0, p1, p2, p3))
    )
    dx[...] = (dmid[...] + back).astype(BF)
    lines = []
    for first, rows, ob, a, u in (
        ((gg, gs), r0, o0, a0, u0),
        ((h1[0:1, :], h1[1:2, :]), r1, o1, a1, u1),
    ):
        lines.append(
            (
                a[...],
                u[...],
                (
                    (first[0], rows[0:1, :]),
                    (first[1], rows[1:2, :]),
                    (rows[2:3, :], ob[...]),
                ),
            )
        )
    for d in range(8):
        cols = slice(d * 128, d * 128 + 128)
        for yh in range(2):
            block = []
            for a, u, pairs in lines:
                block += [a[yh : yh + 1], a[2 + yh : 3 + yh], u[yh : yh + 1], u[2 + yh : 3 + yh]]
                block += [jnp.concatenate([f[:, cols], s[:, cols]], axis=1) for f, s in pairs]
            block.append(jnp.zeros((2, 256), F32))
            g = 2 * d + yh
            msg[g, 0:128, :] = (gm[d, yh].astype(F32) + gr[d, yh].astype(F32)).astype(BF)
            msg[g, 128:144, :] = jnp.concatenate(block).astype(BF)


def settle_kernel(core, l0, l1, keep, send, attn):
    first = core[0] == 0
    for j in range(2):
        cols = slice(j * 256, j * 256 + 256)
        a = jnp.sum(l0[:, :, cols].astype(F32), axis=0)
        b = jnp.sum(l1[:, :, cols].astype(F32), axis=0)
        keep[:, cols] = jnp.where(first, a, b)
        send[:, cols] = jnp.where(first, b, a)
    attn[...] = jnp.sum(l1[:, :, 512:768].astype(F32), axis=0)


def settle_tail_kernel(core, tail, attn, keep, send):
    first = core[0] == 0
    t = jnp.sum(tail[...].astype(F32), axis=0)
    a, b = t[0:128], attn[...]
    small = t[128:144]
    pad = jnp.zeros((1, 256), F32)
    c, d = jnp.concatenate([small[0:7], pad]), jnp.concatenate([small[7:14], pad])
    keep[0:128, :] = jnp.where(first, a, b)
    send[0:128, :] = jnp.where(first, b, a)
    keep[128:136, :] = jnp.where(first, c, d)
    send[128:136, :] = jnp.where(first, d, c)


def unpack_kernel(
    core, fk, fg, ak, ag, qkv, out, up, down, gain, shift, inb, outb, upb
):
    first = core[0] == 0

    def ordered(k, g):
        return jnp.where(first, k, g), jnp.where(first, g, k)

    a = ordered(ak[0:128, :], ag[0:128, :])
    for i, at in enumerate((128, 0, 64)):
        qkv[i] = jnp.concatenate([t[:, at : at + 64] for t in a], axis=1)
    out[...] = jnp.concatenate([t[:, 192:256] for t in a], axis=1).T
    ups = ordered(fk[:, 0:256], fg[:, 0:256])
    downs = ordered(fk[:, 256:512], fg[:, 256:512])
    for j in range(2):
        up[:, j * 256 : j * 256 + 256] = ups[j]
        down[j * 256 : j * 256 + 256, :] = downs[j].T
    s0, s1 = ordered(ak[128:136, :], ag[128:136, :])
    for row, ref in ((4, gain), (5, shift), (6, outb)):
        t = s0[row : row + 1] + s1[row : row + 1]
        ref[0:1, :] = t[:, 0:128]
        ref[1:2, :] = t[:, 128:256]
    sides = [s0[0:1] + s1[1:2], s0[1:2] + s1[0:1]]
    inb[0:1, :] = jnp.concatenate([t[:, 128:192] for t in sides], axis=1)
    inb[1:2, :] = jnp.concatenate([t[:, 64:128] for t in sides], axis=1)
    upb[...] = jnp.concatenate([s0[2:3] + s1[3:4], s0[3:4] + s1[2:3]], axis=1)


def swap_cores(v):
    return lax.ppermute(v, "s", [(0, 1), (1, 0)])


def all_parts(part):
    got = [lax.ppermute(part, "x", [(i, i ^ k) for i in range(4)]) for k in (1, 3, 2)]
    return part, got[0], got[2], got[1]


def exchange(v, axes=CHIPS):
    return lax.all_to_all(v, axes, 0, 0, tiled=True)


def by_layer(mine, first, second):
    return jnp.where(mine == 0, first, second)


def whole_rows(s, yh, a, b):
    keep, send = by_layer(s, a, b), by_layer(s, b, a)
    got = swap_cores(send)
    rows = jnp.stack([by_layer(s, keep, got), by_layer(s, got, keep)])
    far = lax.ppermute(rows, "yh", [(0, 1), (1, 0)])
    return jnp.concatenate([by_layer(yh, rows, far), by_layer(yh, far, rows)], axis=1).reshape(
        1, 2, 1, 128, D
    )


def local(inputs, cotangent, wqkv, wout, wup, wdown, gain, shift, inb, outb, upb):
    s, yh = lax.axis_index("s"), lax.axis_index("yh")
    first = (lax.axis_index(CHIPS) * ROWS).astype(jnp.int32).reshape(1)

    def own_rows(v):
        return lax.dynamic_slice(v, (s, 0, yh * ROWS, 0), (1, 1, ROWS, D)).reshape(ROWS, D)

    x, cot = own_rows(inputs), own_rows(cotangent)
    core = (s.astype(jnp.int32).reshape(1), None, None)
    weights = [
        jnp.moveaxis(wqkv[0], 1, 0), wout[0], wup[0], wdown[0],
        gain[0], shift[0], inb[0], outb[0], upb,
    ]
    keep, send = pl.pallas_call(
        pack_kernel,
        out_shape=[sds(144, 768), sds(144, 768)],
        in_specs=[pl.BlockSpec(memory_space=pltpu.SMEM)]
        + [pl.BlockSpec(memory_space=pl.ANY)] * 9,
        out_specs=[pl.BlockSpec(memory_space=pltpu.VMEM)] * 2,
        scratch_shapes=[pltpu.VMEM(w.shape, BF) for w in weights]
        + [pltpu.SemaphoreType.DMA((9,))],
        compiler_params=pltpu.CompilerParams(vmem_limit_bytes=48 * 1024 * 1024),
    )(core[0], *[pltpu.with_memory_space_constraint(w, pltpu.HBM) for w in weights])
    msg, piece0, piece1 = call(
        spread_kernel,
        [message(16, 272, 256), sds(128, 512), sds(128, 512)],
        [core, keep, swap_cores(send)],
    )
    u = exchange(msg).reshape(8, 2, 272, 256)
    uo = swap_cores(u)
    am = [(u, (8, 2, 128, 256), (0, 0, l, 0)) for l in range(2)]
    ao = [(uo, (8, 2, 128, 256), (0, 0, l, 0)) for l in range(2)]
    kinds = dict(n1=kept(ROWS, D), q=kept(4, ROWS, 128))
    n10, q0, msg, lnp, bias = call(
        first_kernel,
        [kinds["n1"], kinds["q"], message(16, 192, 512), kept(2, 16, D, dtype=F32), kept(2, 16, 256, dtype=F32)],
        [x, (u, (8, 2, 16, 256), (0, 0, 16, 0)), am[0], ao[0], piece0],
    )
    got0 = exchange(msg)
    kv0 = (got0, (16, ROWS, 512), (0, 2, 0))
    f0 = (got0.reshape(8, 2, 192, 512), (8, 2, 128, 512), (0, 0, 0, 0))
    f0o = (swap_cores(got0).reshape(8, 2, 192, 512), (8, 2, 128, 512), (0, 0, 0, 0))
    attend_outs = [sds(ROWS, D), kept(4, ROWS, D, dtype=F32), kept(4, ROWS, 128)]
    feed_outs = [
        sds(ROWS, D), kept(ROWS, D, dtype=F32), kept(ROWS, D),
        kept(4, ROWS, 256, dtype=F32), kept(4, ROWS, 256),
    ]
    part, prob0, att0, copies = call(
        attend_spread_kernel,
        attend_outs + [message(16, 128, 512)],
        [(first, None, None), q0, kv0, am[0], ao[0], piece1],
    )
    f1 = exchange(copies)
    part, mid0, n20, pre0, act0 = call(
        feed_kernel, feed_outs, [x, *all_parts(part), lnp, bias, f0, f0o]
    )
    y0, n11, q1, msg, f1 = call(
        next_kernel,
        [sds(ROWS, D), kinds["n1"], kinds["q"], message(16, ROWS, 512)],
        [mid0, *all_parts(part), lnp, bias, am[1], ao[1]],
        through=[f1],
    )
    f1 = f1.reshape(8, 2, 128, 512)
    f1o = swap_cores(f1)
    kv1 = exchange(msg)
    part, prob1, att1 = call(attend_kernel, attend_outs, [(first, None, None), q1, kv1, am[1], ao[1]])
    last_part, mid1, n21, pre1, act1, dpre1, back = call(
        turn_kernel,
        feed_outs + [kept(4, ROWS, 256), sds(ROWS, D)],
        [y0, *all_parts(part), lnp, bias, f1, f1o, cot],
    )
    backs = all_parts(back)
    grad_ffn_outs = [
        kept(8, 2, 128, 512), sds(8, 2, 128, 512), kept(4, 256, dtype=F32), kept(1, D, dtype=F32)
    ]
    gfm1, gfo1, gub1, ob11 = call(grad_ffn_kernel, grad_ffn_outs, [n21, cot, dpre1, act1])
    gfr1 = swap_cores(gfo1)
    back_outs = [kept(ROWS, D, dtype=F32), kept(ROWS, D), kept(4, ROWS, 128)]
    rows_out = kept(8, D, dtype=F32)
    dmid1, bg1, dq1, dkv, rows1 = call(
        attend_back_kernel,
        back_outs + [message(16, ROWS, 512), rows_out],
        [cot, mid1, *backs, lnp, am[1], ao[1], prob1, q1, kv1],
    )
    dkv = exchange(dkv)
    project_outs = [kept(4, ROWS, 256), sds(ROWS, D), kept(4, 256, dtype=F32)]
    dproj1, part, gib1 = call(project_back_kernel, project_outs, [dkv, dq1, am[1], ao[1]])
    backs = all_parts(part)
    grad_attn_outs = [kept(8, 2, 128, 256), sds(8, 2, 128, 256)]
    gam1, gao1 = call(grad_attn_kernel, grad_attn_outs, [n11, bg1, att1, dproj1])
    (l1,) = call(join_kernel, [message(16, 128, 768)], [gfm1, gfr1, gam1, swap_cores(gao1)])
    dx1, dpre0, part, head1, l1 = call(
        hand_down_kernel,
        [sds(ROWS, D), kept(4, ROWS, 256), sds(ROWS, D), rows_out],
        [y0, dmid1, *backs, lnp, pre0, f0, f0o],
        through=[l1],
    )
    l1 = exchange(l1)
    backs = all_parts(part)
    gfm0, gfo0, gub0, ob10 = call(grad_ffn_kernel, grad_ffn_outs, [n20, dx1, dpre0, act0])
    gfr0 = swap_cores(gfo0)
    dmid0, bg0, dq0, dkv, rows0, last_part = call(
        attend_back_first_kernel,
        back_outs + [message(16, ROWS, 512), rows_out],
        [dx1, mid0, *backs, lnp, am[0], ao[0], prob0, q0, kv0],
        through=[last_part],
    )
    (y1,) = call(finish_kernel, [sds(ROWS, D)], [mid1, *all_parts(last_part), lnp])
    _, dkv, l1, y1 = call(
        mark_kernel, [sds(1, 128, dtype=F32)], [rows0], through=[dkv, l1, y1]
    )
    dkv = exchange(dkv)
    (l0,) = call(add_kernel, [message(16, 128, 512)], [gfm0, gfr0])
    acts = whole_rows(s, yh, y0, y1)
    dproj0, part, gib0, l0, acts = call(
        project_back_kernel, project_outs, [dkv, dq0, am[0], ao[0]], through=[l0, acts]
    )
    l0 = exchange(l0)
    backs = all_parts(part)
    gam0, gao0 = call(grad_attn_kernel, grad_attn_outs, [n10, bg0, att0, dproj0])
    gar0 = swap_cores(gao0)
    dx0, msg, l0 = call(
        last_kernel,
        [sds(ROWS, D), message(16, 144, 256)],
        [x, dmid0, *backs, lnp, gam0, gar0, rows0, ob10, gib0, gub0, head1, rows1, ob11, gib1, gub1],
        through=[l0],
    )
    tail = exchange(msg)
    grads = whole_rows(s, yh, dx0, dx1)
    f = functools.partial(sds, dtype=F32)
    fk, send, at1 = call(settle_kernel, [f(128, 512), f(128, 512), f(128, 256)], [core, l0, l1])
    fg = swap_cores(send)
    ak, send = call(settle_tail_kernel, [f(136, 256), f(136, 256)], [core, tail, at1])
    gq, go, gu, gd, gg, gs, gi, gb, gub = call(
        unpack_kernel,
        [f(3, 128, 128), f(128, 128), f(128, 512), f(512, 128), f(2, 128), f(2, 128), f(2, 128), f(2, 128), f(1, 512)],
        [core, fk, fg, ak, swap_cores(send)],
    )
    return (
        acts, grads, jnp.moveaxis(gq, 0, 1)[None], go[None], gu[None], gd[None],
        gg[None], gs[None], gi[None], gb[None], gub,
    )


def solution(mesh):
    parts = Mesh(mesh.devices.reshape(2, 4, 2, 2, 4), ("s", "z", "yl", "yh", "x"))
    dp, tp = ("z", "yl"), ("yh", "x")
    return jax.shard_map(
        local,
        mesh=parts,
        in_specs=(
            P(None, None, dp, None),
            P(None, None, dp, None),
            P("s", dp, None, tp),
            P("s", tp, dp),
            P("s", dp, tp),
            P("s", tp, dp),
            P("s", None, dp),
            P("s", None, dp),
            P("s", None, tp),
            P("s", None, dp),
            P("s", tp),
        ),
        out_specs=(
            P("s", None, None, dp, None),
            P("s", None, None, dp, None),
            P("s", dp, None, tp),
            P("s", tp, dp),
            P("s", dp, tp),
            P("s", tp, dp),
            P("s", None, dp),
            P("s", None, dp),
            P("s", None, tp),
            P("s", None, dp),
            P("s", tp),
        ),
        check_vma=False,
    )
```

```python
import functools
import math

import jax
import jax.numpy as jnp
from jax import lax
from jax.experimental import pallas as pl
from jax.experimental.pallas import tpu as pltpu
from jax.sharding import Mesh, PartitionSpec as P

EPSILON = 1e-05
MASKED = -1e30
SCALE = 1.0 / math.sqrt(64)
BF = jnp.bfloat16
F32 = jnp.float32
CHIPS = ("z", "yl", "yh")
ROWS = 64
D = 1024


def sds(*shape, dtype=BF):
    return jax.ShapeDtypeStruct(shape, dtype)


def kept(*shape, dtype=BF):
    return ("kept", pltpu.HBM(shape, dtype))


def message(*shape):
    return pltpu.HBM(shape, BF)


def call(kernel, outs, ins, us=3, through=(), after=None):
    n, m, k = len(ins), len(outs), len(through)
    if after is not None:
        ins = [*ins, (after, (16 if after.dtype == BF else 8, 128), (0, 0))]
    e = len(ins)
    held = [i for i, o in enumerate(outs) if isinstance(o, tuple)]
    outs = [o[1] if isinstance(o, tuple) else o for o in outs]
    specs, arrays = [], []
    for item in ins:
        if isinstance(item, tuple):
            array, block, index = item
            if block is None:
                specs.append(pl.BlockSpec(memory_space=pltpu.SMEM))
            else:
                specs.append(
                    pl.BlockSpec(
                        block,
                        functools.partial(lambda at, i: at, index),
                        pipeline_mode=pl.Buffered(1),
                    )
                )
        else:
            array = item
            specs.append(
                pl.BlockSpec(
                    array.shape,
                    functools.partial(lambda n, i: (0,) * n, array.ndim),
                    pipeline_mode=pl.Buffered(1),
                )
            )
        arrays.append(array)
    out_specs = [
        pl.BlockSpec(o.shape, functools.partial(lambda n, i: (0,) * n, len(o.shape)))
        for o in outs
    ]

    def body(*refs):
        kernel(*refs[:n], *refs[e + k : e + k + m])

    results = pl.pallas_call(
        body,
        grid=(1,),
        out_shape=list(outs) + [pltpu.HBM(t.shape, t.dtype) for t in through],
        in_specs=specs + [pl.BlockSpec(memory_space=pl.ANY)] * k,
        out_specs=out_specs + [pl.BlockSpec(memory_space=pl.ANY)] * k,
        input_output_aliases={e + i: m + i for i in range(k)},
        compiler_params=pltpu.CompilerParams(vmem_limit_bytes=48 * 1024 * 1024),
        cost_estimate=pl.CostEstimate(
            flops=0, bytes_accessed=us * 3_000_000, transcendentals=0
        ),
    )(*arrays, *[pltpu.with_memory_space_constraint(t, pltpu.HBM) for t in through])
    return [
        pltpu.with_memory_space_constraint(r, pltpu.HBM) if i in held else r
        for i, r in enumerate(results)
    ]


def nn(a, b):
    return jnp.dot(a, b, preferred_element_type=F32)


def nt(a, b):
    return lax.dot_general(a, b, (((1,), (1,)), ((), ())), preferred_element_type=F32)


def tn(a, b):
    return lax.dot_general(a, b, (((0,), (0,)), ((), ())), preferred_element_type=F32)


def heads():
    return [(k, side, yh) for k, (side, yh) in enumerate([(0, 0), (0, 1), (1, 0), (1, 1)])]


def attn_tile(ref, yh):
    return ref[:, yh, 0:128, :].reshape(D, 256)


def ffn_tile(ref, yh, part):
    return ref[:, yh, 0:128, part * 256 : part * 256 + 256].reshape(D, 256)


def low_half(v):
    lane = lax.broadcasted_iota(jnp.int32, v.shape, 1)
    return jnp.where(lane < 64, v, 0.0)


def high_half(v):
    lane = lax.broadcasted_iota(jnp.int32, v.shape, 1)
    return jnp.where(lane >= 64, v, 0.0)


def mean_of(v):
    return jnp.sum(v, axis=-1, keepdims=True) * (1.0 / D)


def normal(v):
    centred = v - mean_of(v)
    inverse = lax.rsqrt(mean_of(centred * centred) + EPSILON)
    return centred * inverse, inverse


def layer_norm(v, gain, shift):
    return normal(v)[0] * gain + shift


def layer_norm_back(v, gain, grad):
    xhat, inverse = normal(v)
    d = grad * gain
    back = inverse * (d - mean_of(d) - xhat * mean_of(d * xhat))
    return (
        back,
        jnp.sum(grad * xhat, axis=0, keepdims=True),
        jnp.sum(grad, axis=0, keepdims=True),
    )


def gelu(u):
    return 0.5 * u * (1.0 + jnp.tanh(0.7978845608028654 * (u + 0.044715 * u * u * u)))


def gelu_slope(u):
    t = jnp.tanh(0.7978845608028654 * (u + 0.044715 * u * u * u))
    return 0.5 * (1.0 + t) + 0.5 * u * (1.0 - t * t) * (
        0.7978845608028654 * (1.0 + 3.0 * 0.044715 * u * u)
    )


def total(parts):
    a, b, c, d = [p[...].astype(F32) for p in parts]
    return (a + b) + (c + d)


def ln_row(lnp, layer, which, kind):
    return lnp[which, layer * 8 + 4 + kind : layer * 8 + 5 + kind, :]


def project(x, lnp, bias, wm, wo, layer, n1, q, kv):
    normed = layer_norm(x, ln_row(lnp, layer, 0, 0), ln_row(lnp, layer, 0, 1)).astype(BF)
    n1[...] = normed
    for k, side, yh in heads():
        tile = nn(normed, attn_tile((wm, wo)[side], yh))
        tile = tile + bias[yh, layer * 8 + side : layer * 8 + side + 1, :]
        q[k] = low_half(tile[:, 128:]).astype(BF)
        pair = tile[:, :128].astype(BF)
        for g in range(16):
            kv[g, kv.shape[1] - ROWS :, k * 128 : k * 128 + 128] = pair


def pack_kernel(core, *refs):
    sources, (keep, send), held, sem = refs[:9], refs[9:11], refs[11:20], refs[20]
    copies = [
        pltpu.make_async_copy(a, b, sem.at[i]) for i, (a, b) in enumerate(zip(sources, held))
    ]
    for c in copies:
        c.start()
    for c in copies:
        c.wait()
    pack(core, *held, keep, send)


def pack(core, qkv, out, up, down, gain, shift, inb, outb, upb, keep, send):
    wt = out[...].astype(F32).T
    dt = down[...].astype(F32).T
    inb_, gain_, shift_, outb_ = [r[...].astype(F32) for r in (inb, gain, shift, outb)]
    upb_ = upb[...].astype(F32)
    zero = jnp.zeros((1, 64), F32)
    def flat(v):
        return jnp.concatenate([v[0:1], v[1:2]], axis=1)
    rows = []
    for j in range(2):
        cols = slice(j * 64, j * 64 + 64)
        rows.append(jnp.concatenate([zero, inb_[1:2, cols], inb_[0:1, cols], zero], axis=1))
    ups = [upb_[:, :256], upb_[:, 256:]]
    rest = [flat(gain_), flat(shift_), flat(outb_), jnp.zeros((9, 256), F32)]
    halves = []
    for j in range(2):
        cols = slice(j * 64, j * 64 + 64)
        wide = slice(j * 256, j * 256 + 256)
        halves.append(
            (
                up[:, wide].astype(F32),
                dt[:, wide],
                jnp.concatenate([qkv[i, :, cols].astype(F32) for i in (1, 2, 0)] + [wt[:, cols]], axis=1),
                jnp.concatenate([rows[j], rows[1 - j], ups[j], ups[1 - j], *rest]),
            )
        )
    first = core[0] == 0
    for ref, pair in ((keep, halves), (send, halves[::-1])):
        values = [jnp.where(first, a, b).astype(BF) for a, b in zip(*pair)]
        ref[0:128, 0:256] = values[0]
        ref[0:128, 256:512] = values[1]
        ref[0:128, 512:768] = values[2]
        ref[128:144, 512:768] = values[3]


def spread_kernel(core, keep, got, msg, ffn0, ffn1):
    first = core[0] == 0
    k, o = keep[...], got[...]
    lower, upper = jnp.where(first, k, o), jnp.where(first, o, k)
    small = jnp.concatenate(
        [v[128:144, 512:768].astype(F32)[0:8] for v in (lower, upper)]
    ).astype(BF)
    tiles = lower[0:128, 512:768], upper[0:128, 512:768]
    for g in range(16):
        msg[g, 0:128, :] = tiles[0]
        msg[g, 128:256, :] = tiles[1]
        msg[g, 256:272, :] = small
    ffn0[...] = lower[0:128, 0:512]
    ffn1[...] = upper[0:128, 0:512]


def first_kernel(x, params, wm, wo, piece, n1, q, msg, lnp, bias):
    for layer in range(2):
        part = slice(layer * 8, layer * 8 + 8)
        blocks = [params[d, 0].astype(F32)[part] for d in range(8)]
        for half in range(2):
            cols = slice(half * 128, half * 128 + 128)
            lnp[half, part, :] = jnp.concatenate([b[:, cols] for b in blocks], axis=1)
        for yh in range(2):
            bias[yh, part, :] = params[0, yh].astype(F32)[part]
    project(x[...].astype(F32), lnp, bias, wm, wo, 0, n1, q, msg)
    rest = piece[...]
    for g in range(16):
        msg[g, 0:128, :] = rest


def next_kernel(mid, p0, p1, p2, p3, lnp, bias, wm, wo, y, n1, q, msg):
    out = (mid[...] + (total((p0, p1, p2, p3)) + ln_row(lnp, 0, 1, 2))).astype(BF)
    y[...] = out
    project(out.astype(F32), lnp, bias, wm, wo, 1, n1, q, msg)


def attend_spread_kernel(first, q, kv, wm, wo, piece, part, prob, att, copies):
    attend_kernel(first, q, kv, wm, wo, part, prob, att)
    rest = piece[...]
    for g in range(16):
        copies[g] = rest


def attend_kernel(first, q, kv, wm, wo, part, prob, att):
    length = 16 * ROWS
    qpos = first[0] + lax.broadcasted_iota(jnp.int32, (ROWS, length), 0)
    kpos = lax.broadcasted_iota(jnp.int32, (ROWS, length), 1)
    allowed = kpos <= qpos
    acc = None
    for k, side, yh in heads():
        pair = kv[:, :, k * 128 : k * 128 + 128].reshape(length, 128)
        scores = jnp.where(allowed, nt(q[k], pair) * SCALE, MASKED)
        e = jnp.exp(scores - jnp.max(scores, axis=-1, keepdims=True))
        p = e / jnp.sum(e, axis=-1, keepdims=True)
        prob[k] = p
        mixed = high_half(nn(p.astype(BF), pair)).astype(BF)
        att[k] = mixed
        term = nt(mixed, attn_tile((wm, wo)[side], yh)[:, 128:])
        acc = term if acc is None else acc + term
    part[...] = acc.astype(BF)


def feed(x, parts, lnp, bias, wm, wo, layer, part, mid, n2, pre, act):
    middle = x[...].astype(F32) + (total(parts) + ln_row(lnp, layer, 0, 2))
    mid[...] = middle
    normed = layer_norm(middle, ln_row(lnp, layer, 1, 0), ln_row(lnp, layer, 1, 1)).astype(BF)
    n2[...] = normed
    acc = None
    for k, side, yh in heads():
        w = (wm, wo)[side]
        u = nn(normed, ffn_tile(w, yh, 0))
        u = u + bias[yh, layer * 8 + 2 + side : layer * 8 + 3 + side, :]
        pre[k] = u
        a = gelu(u).astype(BF)
        act[k] = a
        term = nt(a, ffn_tile(w, yh, 1))
        acc = term if acc is None else acc + term
    part[...] = acc.astype(BF)


def feed_back(g, pre, wm, wo, dpre, part):
    acc = None
    for k, side, yh in heads():
        w = (wm, wo)[side]
        d = (nn(g, ffn_tile(w, yh, 1)) * gelu_slope(pre[k])).astype(BF)
        dpre[k] = d
        term = nt(d, ffn_tile(w, yh, 0))
        acc = term if acc is None else acc + term
    part[...] = acc.astype(BF)


def feed_kernel(x, p0, p1, p2, p3, lnp, bias, wm, wo, part, mid, n2, pre, act):
    feed(x, (p0, p1, p2, p3), lnp, bias, wm, wo, 0, part, mid, n2, pre, act)


def turn_kernel(x, p0, p1, p2, p3, lnp, bias, wm, wo, g, part, mid, n2, pre, act, dpre, back):
    feed(x, (p0, p1, p2, p3), lnp, bias, wm, wo, 1, part, mid, n2, pre, act)
    feed_back(g[...], pre, wm, wo, dpre, back)


def by_section(core, a, b, keep, send):
    first = core[0] == 0
    keep[...] = jnp.where(first, a, b)
    send[...] = jnp.where(first, b, a)


def finish_kernel(core, y0, mid, p0, p1, p2, p3, lnp, keep, send):
    y1 = (mid[...] + (total((p0, p1, p2, p3)) + ln_row(lnp, 1, 1, 2))).astype(BF)
    by_section(core, y0[...], y1, keep, send)


def pair_kernel(core, keep, got, rows):
    first = core[0] == 0
    k, g = keep[...], got[...]
    rows[0] = jnp.where(first, k, g)
    rows[1] = jnp.where(first, g, k)


def line_up_kernel(half, rows, far, out):
    first = half[0] == 0
    k, g = rows[...], far[...]
    out[:, 0:ROWS, :] = jnp.where(first, k, g)
    out[:, ROWS:, :] = jnp.where(first, g, k)


def grad_ffn_kernel(n2, g, dpre, act, mine, other, sums, row):
    for k, side, yh in heads():
        out = (mine, other)[side]
        out[:, yh, :, 0:256] = tn(n2[...], dpre[k]).astype(BF).reshape(8, 128, 256)
        out[:, yh, :, 256:512] = tn(g[...], act[k]).astype(BF).reshape(8, 128, 256)
        sums[k : k + 1, :] = jnp.sum(dpre[k].astype(F32), axis=0, keepdims=True)
    row[...] = jnp.sum(g[...].astype(F32), axis=0, keepdims=True)


def attend_back(layer, g, mid, parts, lnp, wm, wo, prob, q, kv, dmid, bg, dq, dkv, rows):
    back, gg, gs = layer_norm_back(mid[...], ln_row(lnp, layer, 1, 0), total(parts))
    dm = g[...].astype(F32) + back
    dmid[...] = dm
    low = dm.astype(BF)
    bg[...] = low
    rows[0:1, :] = gg
    rows[1:2, :] = gs
    rows[2:3, :] = jnp.sum(low.astype(F32), axis=0, keepdims=True)
    at = dkv.shape[1] - ROWS
    for k, side, yh in heads():
        pair = kv[:, :, k * 128 : k * 128 + 128].reshape(16 * ROWS, 128)
        da = high_half(nn(low, attn_tile((wm, wo)[side], yh)[:, 128:])).astype(BF)
        p = prob[k]
        dp = nt(da, pair)
        ds = (p * (dp - jnp.sum(p * dp, axis=-1, keepdims=True))).astype(BF)
        dq[k] = low_half(nn(ds, pair) * SCALE).astype(BF)
        both = tn(ds, q[k]) * SCALE + tn(p.astype(BF), da)
        dkv[:, at:, k * 128 : k * 128 + 128] = both.astype(BF).reshape(16, ROWS, 128)


def attend_back_kernel(g, mid, p0, p1, p2, p3, lnp, wm, wo, prob, q, kv, dmid, bg, dq, dkv, rows):
    attend_back(1, g, mid, (p0, p1, p2, p3), lnp, wm, wo, prob, q, kv, dmid, bg, dq, dkv, rows)


def attend_back_first_kernel(
    g, mid, p0, p1, p2, p3, lnp, wm, wo, prob, q, kv, dmid, bg, dq, dkv, rows
):
    attend_back(0, g, mid, (p0, p1, p2, p3), lnp, wm, wo, prob, q, kv, dmid, bg, dq, dkv, rows)


def add_into(msg, at, gm, gr):
    for i in range(8):
        for j in range(2):
            both = gm[i, j].astype(F32) + gr[i, j].astype(F32)
            msg[2 * i + j, 0:128, at : at + gm.shape[3]] = both.astype(BF)


def add_kernel(gm, gr, msg):
    add_into(msg, 0, gm, gr)


def join_kernel(fm, fr, am, ar, msg):
    add_into(msg, 0, fm, fr)
    add_into(msg, 512, am, ar)


def mark_kernel(rows, out):
    out[...] = rows[0:1, 0:128]


def project_back_kernel(dkv, dq, wm, wo, dproj, part, sums):
    pairs = jnp.sum(dkv[...].astype(F32), axis=0).astype(BF)
    acc = None
    for k, side, yh in heads():
        tile = jnp.concatenate([pairs[:, k * 128 : k * 128 + 128], dq[k]], axis=1)
        dproj[k] = tile
        sums[k : k + 1, :] = jnp.sum(tile.astype(F32), axis=0, keepdims=True)
        term = nt(tile, attn_tile((wm, wo)[side], yh))
        acc = term if acc is None else acc + term
    part[...] = acc.astype(BF)


def grad_attn_kernel(n1, bg, att, dproj, mine, other):
    for k, side, yh in heads():
        out = (mine, other)[side]
        first = tn(n1[...], dproj[k])
        second = tn(bg[...], att[k])
        out[:, yh, :, 0:128] = first[:, :128].astype(BF).reshape(8, 128, 128)
        out[:, yh, :, 128:] = (first[:, 128:] + second).astype(BF).reshape(8, 128, 128)


def hand_down_kernel(x, dmid, p0, p1, p2, p3, lnp, pre, wm, wo, dx, dpre, part, rows):
    back, gg, gs = layer_norm_back(
        x[...].astype(F32), ln_row(lnp, 1, 0, 0), total((p0, p1, p2, p3))
    )
    g = (dmid[...] + back).astype(BF)
    dx[...] = g
    rows[0:1, :] = gg
    rows[1:2, :] = gs
    feed_back(g, pre, wm, wo, dpre, part)


def last_kernel(
    core, dx1, x, dmid, p0, p1, p2, p3, lnp, gm, gr,
    r0, o0, a0, u0, h1, r1, o1, a1, u1, keep, send, msg,
):
    back, gg, gs = layer_norm_back(
        x[...].astype(F32), ln_row(lnp, 0, 0, 0), total((p0, p1, p2, p3))
    )
    by_section(core, (dmid[...] + back).astype(BF), dx1[...], keep, send)
    lines = []
    for first, rows, ob, a, u in (
        ((gg, gs), r0, o0, a0, u0),
        ((h1[0:1, :], h1[1:2, :]), r1, o1, a1, u1),
    ):
        lines.append(
            (
                a[...],
                u[...],
                (
                    (first[0], rows[0:1, :]),
                    (first[1], rows[1:2, :]),
                    (rows[2:3, :], ob[...]),
                ),
            )
        )
    for d in range(8):
        cols = slice(d * 128, d * 128 + 128)
        for yh in range(2):
            block = []
            for a, u, pairs in lines:
                block += [a[yh : yh + 1], a[2 + yh : 3 + yh], u[yh : yh + 1], u[2 + yh : 3 + yh]]
                block += [jnp.concatenate([f[:, cols], s[:, cols]], axis=1) for f, s in pairs]
            block.append(jnp.zeros((2, 256), F32))
            g = 2 * d + yh
            msg[g, 0:128, :] = (gm[d, yh].astype(F32) + gr[d, yh].astype(F32)).astype(BF)
            msg[g, 128:144, :] = jnp.concatenate(block).astype(BF)


def settle_kernel(core, l0, l1, keep, send, attn):
    first = core[0] == 0
    for j in range(2):
        cols = slice(j * 256, j * 256 + 256)
        a = jnp.sum(l0[:, :, cols].astype(F32), axis=0)
        b = jnp.sum(l1[:, :, cols].astype(F32), axis=0)
        keep[:, cols] = jnp.where(first, a, b)
        send[:, cols] = jnp.where(first, b, a)
    attn[...] = jnp.sum(l0[:, :, 512:768].astype(F32), axis=0)


def settle_tail_kernel(core, tail, attn, keep, send):
    first = core[0] == 0
    t = jnp.sum(tail[...].astype(F32), axis=0)
    a, b = t[0:128], attn[...]
    small = t[128:144]
    pad = jnp.zeros((1, 256), F32)
    c, d = jnp.concatenate([small[0:7], pad]), jnp.concatenate([small[7:14], pad])
    keep[0:128, :] = jnp.where(first, a, b)
    send[0:128, :] = jnp.where(first, b, a)
    keep[128:136, :] = jnp.where(first, c, d)
    send[128:136, :] = jnp.where(first, d, c)


def unpack_kernel(
    core, fk, fg, ak, ag, qkv, out, up, down, gain, shift, inb, outb, upb
):
    first = core[0] == 0

    def ordered(k, g):
        return jnp.where(first, k, g), jnp.where(first, g, k)

    a = ordered(ak[0:128, :], ag[0:128, :])
    for i, at in enumerate((128, 0, 64)):
        qkv[i] = jnp.concatenate([t[:, at : at + 64] for t in a], axis=1)
    out[...] = jnp.concatenate([t[:, 192:256] for t in a], axis=1).T
    ups = ordered(fk[:, 0:256], fg[:, 0:256])
    downs = ordered(fk[:, 256:512], fg[:, 256:512])
    for j in range(2):
        up[:, j * 256 : j * 256 + 256] = ups[j]
        down[j * 256 : j * 256 + 256, :] = downs[j].T
    s0, s1 = ordered(ak[128:136, :], ag[128:136, :])
    for row, ref in ((4, gain), (5, shift), (6, outb)):
        t = s0[row : row + 1] + s1[row : row + 1]
        ref[0:1, :] = t[:, 0:128]
        ref[1:2, :] = t[:, 128:256]
    sides = [s0[0:1] + s1[1:2], s0[1:2] + s1[0:1]]
    inb[0:1, :] = jnp.concatenate([t[:, 128:192] for t in sides], axis=1)
    inb[1:2, :] = jnp.concatenate([t[:, 64:128] for t in sides], axis=1)
    upb[...] = jnp.concatenate([s0[2:3] + s1[3:4], s0[3:4] + s1[2:3]], axis=1)


def swap_cores(v):
    return lax.ppermute(v, "s", [(0, 1), (1, 0)])


def all_parts(part):
    got = [lax.ppermute(part, "x", [(i, i ^ k) for i in range(4)]) for k in (1, 3, 2)]
    return [part, got[0], got[2], got[1]]


def exchange(v, axes=CHIPS):
    return lax.all_to_all(v, axes, 0, 0, tiled=True)


def by_layer(mine, first, second):
    return jnp.where(mine == 0, first, second)


def other_half(v):
    return lax.ppermute(v, "yh", [(0, 1), (1, 0)])


def local(inputs, cotangent, wqkv, wout, wup, wdown, gain, shift, inb, outb, upb):
    s, yh = lax.axis_index("s"), lax.axis_index("yh")
    first = (lax.axis_index(CHIPS) * ROWS).astype(jnp.int32).reshape(1)

    def own_rows(v):
        return lax.dynamic_slice(v, (s, 0, yh * ROWS, 0), (1, 1, ROWS, D)).reshape(ROWS, D)

    x, cot = own_rows(inputs), own_rows(cotangent)
    core = (s.astype(jnp.int32).reshape(1), None, None)
    weights = [
        jnp.moveaxis(wqkv[0], 1, 0), wout[0], wup[0], wdown[0],
        gain[0], shift[0], inb[0], outb[0], upb,
    ]
    keep, send = pl.pallas_call(
        pack_kernel,
        out_shape=[sds(144, 768), sds(144, 768)],
        in_specs=[pl.BlockSpec(memory_space=pltpu.SMEM)]
        + [pl.BlockSpec(memory_space=pl.ANY)] * 9,
        out_specs=[pl.BlockSpec(memory_space=pltpu.VMEM)] * 2,
        scratch_shapes=[pltpu.VMEM(w.shape, BF) for w in weights]
        + [pltpu.SemaphoreType.DMA((9,))],
        compiler_params=pltpu.CompilerParams(vmem_limit_bytes=48 * 1024 * 1024),
    )(core[0], *[pltpu.with_memory_space_constraint(w, pltpu.HBM) for w in weights])
    msg, piece0, piece1 = call(
        spread_kernel,
        [message(16, 272, 256), sds(128, 512), sds(128, 512)],
        [core, keep, swap_cores(send)],
    )
    u = exchange(msg).reshape(8, 2, 272, 256)
    uo = swap_cores(u)
    am = [(u, (8, 2, 128, 256), (0, 0, l, 0)) for l in range(2)]
    ao = [(uo, (8, 2, 128, 256), (0, 0, l, 0)) for l in range(2)]
    kinds = dict(n1=kept(ROWS, D), q=kept(4, ROWS, 128))
    n10, q0, msg, lnp, bias = call(
        first_kernel,
        [kinds["n1"], kinds["q"], message(16, 192, 512), kept(2, 16, D, dtype=F32), kept(2, 16, 256, dtype=F32)],
        [x, (u, (8, 2, 16, 256), (0, 0, 16, 0)), am[0], ao[0], piece0],
    )
    got0 = exchange(msg)
    kv0 = (got0, (16, ROWS, 512), (0, 2, 0))
    f0 = (got0.reshape(8, 2, 192, 512), (8, 2, 128, 512), (0, 0, 0, 0))
    f0o = (swap_cores(got0).reshape(8, 2, 192, 512), (8, 2, 128, 512), (0, 0, 0, 0))
    attend_outs = [sds(ROWS, D), kept(4, ROWS, D, dtype=F32), kept(4, ROWS, 128)]
    feed_outs = [
        sds(ROWS, D), kept(ROWS, D, dtype=F32), kept(ROWS, D),
        kept(4, ROWS, 256, dtype=F32), kept(4, ROWS, 256),
    ]
    part, prob0, att0, copies = call(
        attend_spread_kernel,
        attend_outs + [message(16, 128, 512)],
        [(first, None, None), q0, kv0, am[0], ao[0], piece1],
    )
    f1 = exchange(copies)
    part, mid0, n20, pre0, act0 = call(
        feed_kernel, feed_outs, [x, *all_parts(part), lnp, bias, f0, f0o]
    )
    y0, n11, q1, msg, f1 = call(
        next_kernel,
        [sds(ROWS, D), kinds["n1"], kinds["q"], message(16, ROWS, 512)],
        [mid0, *all_parts(part), lnp, bias, am[1], ao[1]],
        through=[f1],
    )
    f1 = f1.reshape(8, 2, 128, 512)
    f1o = swap_cores(f1)
    kv1 = exchange(msg)
    part, prob1, att1 = call(attend_kernel, attend_outs, [(first, None, None), q1, kv1, am[1], ao[1]])
    last_part, mid1, n21, pre1, act1, dpre1, back = call(
        turn_kernel,
        feed_outs + [kept(4, ROWS, 256), sds(ROWS, D)],
        [y0, *all_parts(part), lnp, bias, f1, f1o, cot],
    )
    backs = all_parts(back)
    grad_ffn_outs = [
        kept(8, 2, 128, 512), sds(8, 2, 128, 512), kept(4, 256, dtype=F32), kept(1, D, dtype=F32)
    ]
    back_outs = [kept(ROWS, D, dtype=F32), kept(ROWS, D), kept(4, ROWS, 128)]
    rows_out = kept(8, D, dtype=F32)
    dmid1, bg1, dq1, dkv, rows1, last_part = call(
        attend_back_kernel,
        back_outs + [message(16, ROWS, 512), rows_out],
        [cot, mid1, *backs, lnp, am[1], ao[1], prob1, q1, kv1],
        through=[last_part],
    )
    dkv = exchange(dkv)
    gfm1, gfo1, gub1, ob11 = call(
        grad_ffn_kernel, grad_ffn_outs, [n21, cot, dpre1, act1], after=rows1
    )
    gfr1 = swap_cores(gfo1)
    keep, send = call(
        finish_kernel,
        [sds(ROWS, D), sds(ROWS, D)],
        [core, y0, mid1, *all_parts(last_part), lnp],
    )
    (acts,) = call(pair_kernel, [sds(2, ROWS, D)], [core, keep, swap_cores(send)], us=1)
    project_outs = [kept(4, ROWS, 256), sds(ROWS, D), kept(4, 256, dtype=F32)]
    dproj1, part, gib1, acts = call(
        project_back_kernel, project_outs, [dkv, dq1, am[1], ao[1]], through=[acts]
    )
    far = other_half(acts)
    backs = all_parts(part)
    grad_attn_outs = [kept(8, 2, 128, 256), sds(8, 2, 128, 256)]
    (l1,) = call(add_kernel, [message(16, 128, 512)], [gfm1, gfr1])
    dx1, dpre0, part, head1, l1, far = call(
        hand_down_kernel,
        [sds(ROWS, D), kept(4, ROWS, 256), sds(ROWS, D), rows_out],
        [y0, dmid1, *backs, lnp, pre0, f0, f0o],
        through=[l1, far],
    )
    l1 = exchange(l1)
    backs = all_parts(part)
    dmid0, bg0, dq0, dkv, rows0 = call(
        attend_back_first_kernel,
        back_outs + [message(16, ROWS, 512), rows_out],
        [dx1, mid0, *backs, lnp, am[0], ao[0], prob0, q0, kv0],
    )
    _, dkv, l1 = call(mark_kernel, [sds(1, 128, dtype=F32)], [rows0], through=[dkv, l1])
    dkv = exchange(dkv)
    gfm0, gfo0, gub0, ob10 = call(
        grad_ffn_kernel, grad_ffn_outs, [n20, dx1, dpre0, act0], after=rows0
    )
    gfr0 = swap_cores(gfo0)
    gam1, gao1 = call(
        grad_attn_kernel, grad_attn_outs, [n11, bg1, att1, dproj1], after=rows0
    )
    gar1 = swap_cores(gao1)
    (l0,) = call(join_kernel, [message(16, 128, 768)], [gfm0, gfr0, gam1, gar1])
    dproj0, part, gib0, l0 = call(
        project_back_kernel, project_outs, [dkv, dq0, am[0], ao[0]], through=[l0]
    )
    l0 = exchange(l0)
    backs = all_parts(part)
    gam0, gao0 = call(grad_attn_kernel, grad_attn_outs, [n10, bg0, att0, dproj0])
    gar0 = swap_cores(gao0)
    half = (yh.astype(jnp.int32).reshape(1), None, None)
    (acts,) = call(line_up_kernel, [sds(2, 2 * ROWS, D)], [half, acts, far], us=1)
    keep, send, msg, acts = call(
        last_kernel,
        [sds(ROWS, D), sds(ROWS, D), message(16, 144, 256)],
        [core, dx1, x, dmid0, *backs, lnp, gam0, gar0, rows0, ob10, gib0, gub0, head1, rows1, ob11, gib1, gub1],
        through=[acts],
    )
    tail = exchange(msg)
    (grads,) = call(pair_kernel, [sds(2, ROWS, D)], [core, keep, swap_cores(send)], us=1)
    (grads,) = call(line_up_kernel, [sds(2, 2 * ROWS, D)], [half, grads, other_half(grads)], us=1)
    f = functools.partial(sds, dtype=F32)
    fk, send, at1 = call(settle_kernel, [f(128, 512), f(128, 512), f(128, 256)], [core, l0, l1])
    fg = swap_cores(send)
    ak, send = call(settle_tail_kernel, [f(136, 256), f(136, 256)], [core, tail, at1])
    gq, go, gu, gd, gg, gs, gi, gb, gub = call(
        unpack_kernel,
        [f(3, 128, 128), f(128, 128), f(128, 512), f(512, 128), f(2, 128), f(2, 128), f(2, 128), f(2, 128), f(1, 512)],
        [core, fk, fg, ak, swap_cores(send)],
    )
    return (
        acts[None, :, None], grads[None, :, None], jnp.moveaxis(gq, 0, 1)[None], go[None], gu[None], gd[None],
        gg[None], gs[None], gi[None], gb[None], gub,
    )


def solution(mesh):
    parts = Mesh(mesh.devices.reshape(2, 4, 2, 2, 4), ("s", "z", "yl", "yh", "x"))
    dp, tp = ("z", "yl"), ("yh", "x")
    return jax.shard_map(
        local,
        mesh=parts,
        in_specs=(
            P(None, None, dp, None),
            P(None, None, dp, None),
            P("s", dp, None, tp),
            P("s", tp, dp),
            P("s", dp, tp),
            P("s", tp, dp),
            P("s", None, dp),
            P("s", None, dp),
            P("s", None, tp),
            P("s", None, dp),
            P("s", tp),
        ),
        out_specs=(
            P("s", None, None, dp, None),
            P("s", None, None, dp, None),
            P("s", dp, None, tp),
            P("s", tp, dp),
            P("s", dp, tp),
            P("s", tp, dp),
            P("s", None, dp),
            P("s", None, dp),
            P("s", None, tp),
            P("s", None, dp),
            P("s", tp),
        ),
        check_vma=False,
    )
```

```python
import functools
import math

import jax
import jax.numpy as jnp
from jax import lax
from jax.experimental import pallas as pl
from jax.experimental.pallas import tpu as pltpu
from jax.sharding import Mesh, PartitionSpec as P

EPSILON = 1e-05
MASKED = -1e30
SCALE = 1.0 / math.sqrt(64)
BF = jnp.bfloat16
F32 = jnp.float32
CHIPS = ("z", "yl", "yh")
ROWS = 64
D = 1024


def sds(*shape, dtype=BF):
    return jax.ShapeDtypeStruct(shape, dtype)


def kept(*shape, dtype=BF):
    return ("kept", pltpu.HBM(shape, dtype))


def message(*shape):
    return pltpu.HBM(shape, BF)


def call(kernel, outs, ins, us=3, through=(), after=None):
    n, m, k = len(ins), len(outs), len(through)
    e = n + (after is not None)
    held = [i for i, o in enumerate(outs) if isinstance(o, tuple)]
    outs = [o[1] if isinstance(o, tuple) else o for o in outs]
    specs, arrays = [], []
    for item in ins:
        if isinstance(item, tuple):
            array, block, index = item
            if block is None:
                specs.append(pl.BlockSpec(memory_space=pltpu.SMEM))
            else:
                specs.append(
                    pl.BlockSpec(
                        block,
                        functools.partial(lambda at, i: at, index),
                        pipeline_mode=pl.Buffered(1),
                    )
                )
        else:
            array = item
            specs.append(
                pl.BlockSpec(
                    array.shape,
                    functools.partial(lambda n, i: (0,) * n, array.ndim),
                    pipeline_mode=pl.Buffered(1),
                )
            )
        arrays.append(array)
    if after is not None:
        specs.append(pl.BlockSpec(memory_space=pl.ANY))
        arrays.append(after)
    out_specs = [
        pl.BlockSpec(o.shape, functools.partial(lambda n, i: (0,) * n, len(o.shape)))
        for o in outs
    ]

    def body(*refs):
        kernel(*refs[:n], *refs[e + k : e + k + m])

    results = pl.pallas_call(
        body,
        grid=(1,),
        out_shape=list(outs) + [pltpu.HBM(t.shape, t.dtype) for t in through],
        in_specs=specs + [pl.BlockSpec(memory_space=pl.ANY)] * k,
        out_specs=out_specs + [pl.BlockSpec(memory_space=pl.ANY)] * k,
        input_output_aliases={e + i: m + i for i in range(k)},
        compiler_params=pltpu.CompilerParams(vmem_limit_bytes=48 * 1024 * 1024),
        cost_estimate=pl.CostEstimate(
            flops=0, bytes_accessed=us * 3_000_000, transcendentals=0
        ),
    )(*arrays, *[pltpu.with_memory_space_constraint(t, pltpu.HBM) for t in through])
    return [
        pltpu.with_memory_space_constraint(r, pltpu.HBM) if i in held else r
        for i, r in enumerate(results)
    ]


def nn(a, b):
    return jnp.dot(a, b, preferred_element_type=F32)


def nt(a, b):
    return lax.dot_general(a, b, (((1,), (1,)), ((), ())), preferred_element_type=F32)


def tn(a, b):
    return lax.dot_general(a, b, (((0,), (0,)), ((), ())), preferred_element_type=F32)


def heads():
    return [(k, side, yh) for k, (side, yh) in enumerate([(0, 0), (0, 1), (1, 0), (1, 1)])]


def attn_tile(ref, yh):
    return ref[:, yh, 0:128, :].reshape(D, 256)


def ffn_tile(ref, yh, part):
    return ref[:, yh, 0:128, part * 256 : part * 256 + 256].reshape(D, 256)


def low_half(v):
    lane = lax.broadcasted_iota(jnp.int32, v.shape, 1)
    return jnp.where(lane < 64, v, 0.0)


def high_half(v):
    lane = lax.broadcasted_iota(jnp.int32, v.shape, 1)
    return jnp.where(lane >= 64, v, 0.0)


def mean_of(v):
    return jnp.sum(v, axis=-1, keepdims=True) * (1.0 / D)


def normal(v):
    centred = v - mean_of(v)
    inverse = lax.rsqrt(mean_of(centred * centred) + EPSILON)
    return centred * inverse, inverse


def layer_norm(v, gain, shift):
    return normal(v)[0] * gain + shift


def layer_norm_back(v, gain, grad):
    xhat, inverse = normal(v)
    d = grad * gain
    back = inverse * (d - mean_of(d) - xhat * mean_of(d * xhat))
    return (
        back,
        jnp.sum(grad * xhat, axis=0, keepdims=True),
        jnp.sum(grad, axis=0, keepdims=True),
    )


def gelu(u):
    return 0.5 * u * (1.0 + jnp.tanh(0.7978845608028654 * (u + 0.044715 * u * u * u)))


def gelu_slope(u):
    t = jnp.tanh(0.7978845608028654 * (u + 0.044715 * u * u * u))
    return 0.5 * (1.0 + t) + 0.5 * u * (1.0 - t * t) * (
        0.7978845608028654 * (1.0 + 3.0 * 0.044715 * u * u)
    )


def total(parts):
    a, b, c, d = [p[...].astype(F32) for p in parts]
    return (a + b) + (c + d)


def ln_row(lnp, layer, which, kind):
    return lnp[which, layer * 8 + 4 + kind : layer * 8 + 5 + kind, :]


def project(x, lnp, bias, wm, wo, layer, n1, q, kv):
    normed = layer_norm(x, ln_row(lnp, layer, 0, 0), ln_row(lnp, layer, 0, 1)).astype(BF)
    n1[...] = normed
    for k, side, yh in heads():
        tile = nn(normed, attn_tile((wm, wo)[side], yh))
        tile = tile + bias[yh, layer * 8 + side : layer * 8 + side + 1, :]
        q[k] = low_half(tile[:, 128:]).astype(BF)
        pair = tile[:, :128].astype(BF)
        for g in range(16):
            kv[g, kv.shape[1] - ROWS :, k * 128 : k * 128 + 128] = pair


def pack_kernel(core, *refs):
    sources, (keep, send), held, sem = refs[:9], refs[9:11], refs[11:20], refs[20]
    copies = [
        pltpu.make_async_copy(a, b, sem.at[i]) for i, (a, b) in enumerate(zip(sources, held))
    ]
    for c in copies:
        c.start()
    for c in copies:
        c.wait()
    pack(core, *held, keep, send)


def pack(core, qkv, out, up, down, gain, shift, inb, outb, upb, keep, send):
    wt = out[...].astype(F32).T
    dt = down[...].astype(F32).T
    inb_, gain_, shift_, outb_ = [r[...].astype(F32) for r in (inb, gain, shift, outb)]
    upb_ = upb[...].astype(F32)
    zero = jnp.zeros((1, 64), F32)
    def flat(v):
        return jnp.concatenate([v[0:1], v[1:2]], axis=1)
    rows = []
    for j in range(2):
        cols = slice(j * 64, j * 64 + 64)
        rows.append(jnp.concatenate([zero, inb_[1:2, cols], inb_[0:1, cols], zero], axis=1))
    ups = [upb_[:, :256], upb_[:, 256:]]
    rest = [flat(gain_), flat(shift_), flat(outb_), jnp.zeros((9, 256), F32)]
    halves = []
    for j in range(2):
        cols = slice(j * 64, j * 64 + 64)
        wide = slice(j * 256, j * 256 + 256)
        halves.append(
            (
                up[:, wide].astype(F32),
                dt[:, wide],
                jnp.concatenate([qkv[i, :, cols].astype(F32) for i in (1, 2, 0)] + [wt[:, cols]], axis=1),
                jnp.concatenate([rows[j], rows[1 - j], ups[j], ups[1 - j], *rest]),
            )
        )
    first = core[0] == 0
    for ref, pair in ((keep, halves), (send, halves[::-1])):
        values = [jnp.where(first, a, b).astype(BF) for a, b in zip(*pair)]
        ref[0:128, 0:256] = values[0]
        ref[0:128, 256:512] = values[1]
        ref[0:128, 512:768] = values[2]
        ref[128:144, 512:768] = values[3]


def spread_kernel(core, keep, got, msg, ffn0, ffn1):
    first = core[0] == 0
    k, o = keep[...], got[...]
    lower, upper = jnp.where(first, k, o), jnp.where(first, o, k)
    small = jnp.concatenate(
        [v[128:144, 512:768].astype(F32)[0:8] for v in (lower, upper)]
    ).astype(BF)
    tiles = lower[0:128, 512:768], upper[0:128, 512:768]
    for g in range(16):
        msg[g, 0:128, :] = tiles[0]
        msg[g, 128:256, :] = tiles[1]
        msg[g, 256:272, :] = small
    ffn0[...] = lower[0:128, 0:512]
    ffn1[...] = upper[0:128, 0:512]


def first_kernel(x, params, wm, wo, piece, n1, q, msg, lnp, bias):
    for layer in range(2):
        part = slice(layer * 8, layer * 8 + 8)
        blocks = [params[d, 0].astype(F32)[part] for d in range(8)]
        for half in range(2):
            cols = slice(half * 128, half * 128 + 128)
            lnp[half, part, :] = jnp.concatenate([b[:, cols] for b in blocks], axis=1)
        for yh in range(2):
            bias[yh, part, :] = params[0, yh].astype(F32)[part]
    project(x[...].astype(F32), lnp, bias, wm, wo, 0, n1, q, msg)
    rest = piece[...]
    for g in range(16):
        msg[g, 0:128, :] = rest


def next_kernel(mid, p0, p1, p2, p3, lnp, bias, wm, wo, y, n1, q, msg):
    out = (mid[...] + (total((p0, p1, p2, p3)) + ln_row(lnp, 0, 1, 2))).astype(BF)
    y[...] = out
    project(out.astype(F32), lnp, bias, wm, wo, 1, n1, q, msg)


def attend_spread_kernel(first, q, kv, wm, wo, piece, part, prob, att, copies):
    attend_kernel(first, q, kv, wm, wo, part, prob, att)
    rest = piece[...]
    for g in range(16):
        copies[g] = rest


def attend_kernel(first, q, kv, wm, wo, part, prob, att):
    length = 16 * ROWS
    qpos = first[0] + lax.broadcasted_iota(jnp.int32, (ROWS, length), 0)
    kpos = lax.broadcasted_iota(jnp.int32, (ROWS, length), 1)
    allowed = kpos <= qpos
    acc = None
    for k, side, yh in heads():
        pair = kv[:, :, k * 128 : k * 128 + 128].reshape(length, 128)
        scores = jnp.where(allowed, nt(q[k], pair) * SCALE, MASKED)
        e = jnp.exp(scores - jnp.max(scores, axis=-1, keepdims=True))
        p = e / jnp.sum(e, axis=-1, keepdims=True)
        prob[k] = p
        mixed = high_half(nn(p.astype(BF), pair)).astype(BF)
        att[k] = mixed
        term = nt(mixed, attn_tile((wm, wo)[side], yh)[:, 128:])
        acc = term if acc is None else acc + term
    part[...] = acc.astype(BF)


def feed(x, parts, lnp, bias, wm, wo, layer, part, mid, n2, pre, act):
    middle = x[...].astype(F32) + (total(parts) + ln_row(lnp, layer, 0, 2))
    mid[...] = middle
    normed = layer_norm(middle, ln_row(lnp, layer, 1, 0), ln_row(lnp, layer, 1, 1)).astype(BF)
    n2[...] = normed
    acc = None
    for k, side, yh in heads():
        w = (wm, wo)[side]
        u = nn(normed, ffn_tile(w, yh, 0))
        u = u + bias[yh, layer * 8 + 2 + side : layer * 8 + 3 + side, :]
        pre[k] = u
        a = gelu(u).astype(BF)
        act[k] = a
        term = nt(a, ffn_tile(w, yh, 1))
        acc = term if acc is None else acc + term
    part[...] = acc.astype(BF)


def feed_back(g, pre, wm, wo, dpre, part):
    acc = None
    for k, side, yh in heads():
        w = (wm, wo)[side]
        d = (nn(g, ffn_tile(w, yh, 1)) * gelu_slope(pre[k])).astype(BF)
        dpre[k] = d
        term = nt(d, ffn_tile(w, yh, 0))
        acc = term if acc is None else acc + term
    part[...] = acc.astype(BF)


def feed_kernel(x, p0, p1, p2, p3, lnp, bias, wm, wo, part, mid, n2, pre, act):
    feed(x, (p0, p1, p2, p3), lnp, bias, wm, wo, 0, part, mid, n2, pre, act)


def turn_kernel(x, p0, p1, p2, p3, lnp, bias, wm, wo, g, part, mid, n2, pre, act, dpre, back):
    feed(x, (p0, p1, p2, p3), lnp, bias, wm, wo, 1, part, mid, n2, pre, act)
    feed_back(g[...], pre, wm, wo, dpre, back)


def by_section(core, a, b, keep, send):
    first = core[0] == 0
    keep[...] = jnp.where(first, a, b)
    send[...] = jnp.where(first, b, a)


def finish_kernel(core, y0, mid, p0, p1, p2, p3, lnp, keep, send):
    y1 = (mid[...] + (total((p0, p1, p2, p3)) + ln_row(lnp, 1, 1, 2))).astype(BF)
    by_section(core, y0[...], y1, keep, send)


def pair_kernel(core, keep, got, rows):
    first = core[0] == 0
    k, g = keep[...], got[...]
    rows[0] = jnp.where(first, k, g)
    rows[1] = jnp.where(first, g, k)


def line_up_kernel(half, rows, far, out):
    first = half[0] == 0
    k, g = rows[...], far[...]
    out[:, 0:ROWS, :] = jnp.where(first, k, g)
    out[:, ROWS:, :] = jnp.where(first, g, k)


def grad_ffn_kernel(n2, g, dpre, act, mine, other, sums, row):
    for k, side, yh in heads():
        out = (mine, other)[side]
        out[:, yh, :, 0:256] = tn(n2[...], dpre[k]).astype(BF).reshape(8, 128, 256)
        out[:, yh, :, 256:512] = tn(g[...], act[k]).astype(BF).reshape(8, 128, 256)
        sums[k : k + 1, :] = jnp.sum(dpre[k].astype(F32), axis=0, keepdims=True)
    row[...] = jnp.sum(g[...].astype(F32), axis=0, keepdims=True)


def attend_back(layer, g, mid, parts, lnp, wm, wo, prob, q, kv, dmid, bg, dq, dkv, rows):
    back, gg, gs = layer_norm_back(mid[...], ln_row(lnp, layer, 1, 0), total(parts))
    dm = g[...].astype(F32) + back
    dmid[...] = dm
    low = dm.astype(BF)
    bg[...] = low
    rows[0:1, :] = gg
    rows[1:2, :] = gs
    rows[2:3, :] = jnp.sum(low.astype(F32), axis=0, keepdims=True)
    at = dkv.shape[1] - ROWS
    for k, side, yh in heads():
        pair = kv[:, :, k * 128 : k * 128 + 128].reshape(16 * ROWS, 128)
        da = high_half(nn(low, attn_tile((wm, wo)[side], yh)[:, 128:])).astype(BF)
        p = prob[k]
        dp = nt(da, pair)
        ds = (p * (dp - jnp.sum(p * dp, axis=-1, keepdims=True))).astype(BF)
        dq[k] = low_half(nn(ds, pair) * SCALE).astype(BF)
        both = tn(ds, q[k]) * SCALE + tn(p.astype(BF), da)
        dkv[:, at:, k * 128 : k * 128 + 128] = both.astype(BF).reshape(16, ROWS, 128)


def attend_back_kernel(g, mid, p0, p1, p2, p3, lnp, wm, wo, prob, q, kv, dmid, bg, dq, dkv, rows):
    attend_back(1, g, mid, (p0, p1, p2, p3), lnp, wm, wo, prob, q, kv, dmid, bg, dq, dkv, rows)


def attend_back_first_kernel(
    g, mid, p0, p1, p2, p3, lnp, wm, wo, prob, q, kv, dmid, bg, dq, dkv, rows
):
    attend_back(0, g, mid, (p0, p1, p2, p3), lnp, wm, wo, prob, q, kv, dmid, bg, dq, dkv, rows)


def add_into(msg, at, gm, gr):
    for i in range(8):
        for j in range(2):
            msg[2 * i + j, 0:128, at : at + gm.shape[3]] = gm[i, j] + gr[i, j]


def add_kernel(gm, gr, msg):
    add_into(msg, 0, gm, gr)


def join_kernel(fm, fr, am, ar, msg):
    add_into(msg, 0, fm, fr)
    add_into(msg, 512, am, ar)


def mark_kernel(rows, out):
    out[...] = rows[0:1, 0:128]


def project_back_kernel(dkv, dq, wm, wo, dproj, part, sums):
    pairs = jnp.sum(dkv[...].astype(F32), axis=0).astype(BF)
    acc = None
    for k, side, yh in heads():
        tile = jnp.concatenate([pairs[:, k * 128 : k * 128 + 128], dq[k]], axis=1)
        dproj[k] = tile
        sums[k : k + 1, :] = jnp.sum(tile.astype(F32), axis=0, keepdims=True)
        term = nt(tile, attn_tile((wm, wo)[side], yh))
        acc = term if acc is None else acc + term
    part[...] = acc.astype(BF)


def grad_attn_kernel(n1, bg, att, dproj, mine, other):
    for k, side, yh in heads():
        out = (mine, other)[side]
        first = tn(n1[...], dproj[k])
        second = tn(bg[...], att[k])
        out[:, yh, :, 0:128] = first[:, :128].astype(BF).reshape(8, 128, 128)
        out[:, yh, :, 128:] = (first[:, 128:] + second).astype(BF).reshape(8, 128, 128)


def hand_down_kernel(x, dmid, p0, p1, p2, p3, lnp, pre, wm, wo, dx, dpre, part, rows):
    back, gg, gs = layer_norm_back(
        x[...].astype(F32), ln_row(lnp, 1, 0, 0), total((p0, p1, p2, p3))
    )
    g = (dmid[...] + back).astype(BF)
    dx[...] = g
    rows[0:1, :] = gg
    rows[1:2, :] = gs
    feed_back(g, pre, wm, wo, dpre, part)


def last_kernel(
    core, dx1, x, dmid, p0, p1, p2, p3, lnp, gm, gr,
    r0, o0, a0, u0, h1, r1, o1, a1, u1, keep, send, msg,
):
    back, gg, gs = layer_norm_back(
        x[...].astype(F32), ln_row(lnp, 0, 0, 0), total((p0, p1, p2, p3))
    )
    by_section(core, (dmid[...] + back).astype(BF), dx1[...], keep, send)
    lines = []
    for first, rows, ob, a, u in (
        ((gg, gs), r0, o0, a0, u0),
        ((h1[0:1, :], h1[1:2, :]), r1, o1, a1, u1),
    ):
        lines.append(
            (
                a[...],
                u[...],
                (
                    (first[0], rows[0:1, :]),
                    (first[1], rows[1:2, :]),
                    (rows[2:3, :], ob[...]),
                ),
            )
        )
    for d in range(8):
        cols = slice(d * 128, d * 128 + 128)
        for yh in range(2):
            block = []
            for a, u, pairs in lines:
                block += [a[yh : yh + 1], a[2 + yh : 3 + yh], u[yh : yh + 1], u[2 + yh : 3 + yh]]
                block += [jnp.concatenate([f[:, cols], s[:, cols]], axis=1) for f, s in pairs]
            block.append(jnp.zeros((2, 256), F32))
            g = 2 * d + yh
            msg[g, 0:128, :] = (gm[d, yh].astype(F32) + gr[d, yh].astype(F32)).astype(BF)
            msg[g, 128:144, :] = jnp.concatenate(block).astype(BF)


def settle_kernel(core, l0, l1, keep, send, attn):
    first = core[0] == 0
    for j in range(2):
        cols = slice(j * 256, j * 256 + 256)
        a = jnp.sum(l0[:, :, cols].astype(F32), axis=0)
        b = jnp.sum(l1[:, :, cols].astype(F32), axis=0)
        keep[:, cols] = jnp.where(first, a, b)
        send[:, cols] = jnp.where(first, b, a)
    attn[...] = jnp.sum(l0[:, :, 512:768].astype(F32), axis=0)


def settle_tail_kernel(core, tail, attn, keep, send):
    first = core[0] == 0
    t = jnp.sum(tail[...].astype(F32), axis=0)
    a, b = t[0:128], attn[...]
    small = t[128:144]
    pad = jnp.zeros((1, 256), F32)
    c, d = jnp.concatenate([small[0:7], pad]), jnp.concatenate([small[7:14], pad])
    keep[0:128, :] = jnp.where(first, a, b)
    send[0:128, :] = jnp.where(first, b, a)
    keep[128:136, :] = jnp.where(first, c, d)
    send[128:136, :] = jnp.where(first, d, c)


def unpack_kernel(
    core, fk, fg, ak, ag, qkv, out, up, down, gain, shift, inb, outb, upb
):
    first = core[0] == 0

    def ordered(k, g):
        return jnp.where(first, k, g), jnp.where(first, g, k)

    a = ordered(ak[0:128, :], ag[0:128, :])
    for i, at in enumerate((128, 0, 64)):
        qkv[i] = jnp.concatenate([t[:, at : at + 64] for t in a], axis=1)
    out[...] = jnp.concatenate([t[:, 192:256] for t in a], axis=1).T
    ups = ordered(fk[:, 0:256], fg[:, 0:256])
    downs = ordered(fk[:, 256:512], fg[:, 256:512])
    for j in range(2):
        up[:, j * 256 : j * 256 + 256] = ups[j]
        down[j * 256 : j * 256 + 256, :] = downs[j].T
    s0, s1 = ordered(ak[128:136, :], ag[128:136, :])
    for row, ref in ((4, gain), (5, shift), (6, outb)):
        t = s0[row : row + 1] + s1[row : row + 1]
        ref[0:1, :] = t[:, 0:128]
        ref[1:2, :] = t[:, 128:256]
    sides = [s0[0:1] + s1[1:2], s0[1:2] + s1[0:1]]
    inb[0:1, :] = jnp.concatenate([t[:, 128:192] for t in sides], axis=1)
    inb[1:2, :] = jnp.concatenate([t[:, 64:128] for t in sides], axis=1)
    upb[...] = jnp.concatenate([s0[2:3] + s1[3:4], s0[3:4] + s1[2:3]], axis=1)


def swap_cores(v):
    return lax.ppermute(v, "s", [(0, 1), (1, 0)])


def all_parts(part):
    got = [lax.ppermute(part, "x", [(i, i ^ k) for i in range(4)]) for k in (1, 3, 2)]
    return [part, got[0], got[2], got[1]]


def exchange(v, axes=CHIPS):
    return lax.all_to_all(v, axes, 0, 0, tiled=True)


def by_layer(mine, first, second):
    return jnp.where(mine == 0, first, second)


def other_half(v):
    return lax.ppermute(v, "yh", [(0, 1), (1, 0)])


def local(inputs, cotangent, wqkv, wout, wup, wdown, gain, shift, inb, outb, upb):
    s, yh = lax.axis_index("s"), lax.axis_index("yh")
    first = (lax.axis_index(CHIPS) * ROWS).astype(jnp.int32).reshape(1)

    def own_rows(v):
        return lax.dynamic_slice(v, (s, 0, yh * ROWS, 0), (1, 1, ROWS, D)).reshape(ROWS, D)

    x, cot = own_rows(inputs), own_rows(cotangent)
    core = (s.astype(jnp.int32).reshape(1), None, None)
    weights = [
        jnp.moveaxis(wqkv[0], 1, 0), wout[0], wup[0], wdown[0],
        gain[0], shift[0], inb[0], outb[0], upb,
    ]
    keep, send = pl.pallas_call(
        pack_kernel,
        out_shape=[sds(144, 768), sds(144, 768)],
        in_specs=[pl.BlockSpec(memory_space=pltpu.SMEM)]
        + [pl.BlockSpec(memory_space=pl.ANY)] * 9,
        out_specs=[pl.BlockSpec(memory_space=pltpu.VMEM)] * 2,
        scratch_shapes=[pltpu.VMEM(w.shape, BF) for w in weights]
        + [pltpu.SemaphoreType.DMA((9,))],
        compiler_params=pltpu.CompilerParams(vmem_limit_bytes=48 * 1024 * 1024),
    )(core[0], *[pltpu.with_memory_space_constraint(w, pltpu.HBM) for w in weights])
    msg, piece0, piece1 = call(
        spread_kernel,
        [message(16, 272, 256), sds(128, 512), sds(128, 512)],
        [core, keep, swap_cores(send)],
    )
    u = exchange(msg).reshape(8, 2, 272, 256)
    uo = swap_cores(u)
    am = [(u, (8, 2, 128, 256), (0, 0, l, 0)) for l in range(2)]
    ao = [(uo, (8, 2, 128, 256), (0, 0, l, 0)) for l in range(2)]
    kinds = dict(n1=kept(ROWS, D), q=kept(4, ROWS, 128))
    n10, q0, msg, lnp, bias = call(
        first_kernel,
        [kinds["n1"], kinds["q"], message(16, 192, 512), kept(2, 16, D, dtype=F32), kept(2, 16, 256, dtype=F32)],
        [x, (u, (8, 2, 16, 256), (0, 0, 16, 0)), am[0], ao[0], piece0],
    )
    got0 = exchange(msg)
    kv0 = (got0, (16, ROWS, 512), (0, 2, 0))
    f0 = (got0.reshape(8, 2, 192, 512), (8, 2, 128, 512), (0, 0, 0, 0))
    f0o = (swap_cores(got0).reshape(8, 2, 192, 512), (8, 2, 128, 512), (0, 0, 0, 0))
    attend_outs = [sds(ROWS, D), kept(4, ROWS, D, dtype=F32), kept(4, ROWS, 128)]
    feed_outs = [
        sds(ROWS, D), kept(ROWS, D, dtype=F32), kept(ROWS, D),
        kept(4, ROWS, 256, dtype=F32), kept(4, ROWS, 256),
    ]
    part, prob0, att0, copies = call(
        attend_spread_kernel,
        attend_outs + [message(16, 128, 512)],
        [(first, None, None), q0, kv0, am[0], ao[0], piece1],
    )
    f1 = exchange(copies)
    part, mid0, n20, pre0, act0 = call(
        feed_kernel, feed_outs, [x, *all_parts(part), lnp, bias, f0, f0o]
    )
    y0, n11, q1, msg, f1 = call(
        next_kernel,
        [sds(ROWS, D), kinds["n1"], kinds["q"], message(16, ROWS, 512)],
        [mid0, *all_parts(part), lnp, bias, am[1], ao[1]],
        through=[f1],
    )
    f1 = f1.reshape(8, 2, 128, 512)
    f1o = swap_cores(f1)
    kv1 = exchange(msg)
    part, prob1, att1 = call(attend_kernel, attend_outs, [(first, None, None), q1, kv1, am[1], ao[1]])
    last_part, mid1, n21, pre1, act1, dpre1, back = call(
        turn_kernel,
        [message(ROWS, D), *feed_outs[1:], kept(4, ROWS, 256), sds(ROWS, D)],
        [y0, *all_parts(part), lnp, bias, f1, f1o, cot],
    )
    backs = all_parts(back)
    grad_ffn_outs = [
        kept(8, 2, 128, 512), sds(8, 2, 128, 512), kept(4, 256, dtype=F32), kept(1, D, dtype=F32)
    ]
    back_outs = [kept(ROWS, D, dtype=F32), kept(ROWS, D), kept(4, ROWS, 128)]
    rows_out = kept(8, D, dtype=F32)
    dmid1, bg1, dq1, dkv, rows1, last_part = call(
        attend_back_kernel,
        back_outs + [message(16, ROWS, 512), rows_out],
        [cot, mid1, *backs, lnp, am[1], ao[1], prob1, q1, kv1],
        through=[last_part],
    )
    dkv = exchange(dkv)
    gfm1, gfo1, gub1, ob11 = call(
        grad_ffn_kernel, grad_ffn_outs, [n21, cot, dpre1, act1], after=rows1
    )
    gfr1 = swap_cores(gfo1)
    keep, send = call(
        finish_kernel,
        [sds(ROWS, D), sds(ROWS, D)],
        [core, y0, mid1, *all_parts(last_part), lnp],
    )
    (acts,) = call(pair_kernel, [message(2, ROWS, D)], [core, keep, swap_cores(send)], us=1)
    project_outs = [kept(4, ROWS, 256), sds(ROWS, D), kept(4, 256, dtype=F32)]
    dproj1, part, gib1, acts = call(
        project_back_kernel, project_outs, [dkv, dq1, am[1], ao[1]], through=[acts]
    )
    far = other_half(acts)
    backs = all_parts(part)
    grad_attn_outs = [kept(8, 2, 128, 256), sds(8, 2, 128, 256)]
    (l1,) = call(add_kernel, [message(16, 128, 512)], [gfm1, gfr1])
    dx1, dpre0, part, head1, l1 = call(
        hand_down_kernel,
        [kept(ROWS, D), kept(4, ROWS, 256), sds(ROWS, D), rows_out],
        [y0, dmid1, *backs, lnp, pre0, f0, f0o],
        through=[l1],
        after=far,
    )
    l1 = exchange(l1)
    backs = all_parts(part)
    dmid0, bg0, dq0, dkv, rows0 = call(
        attend_back_first_kernel,
        back_outs + [message(16, ROWS, 512), rows_out],
        [dx1, mid0, *backs, lnp, am[0], ao[0], prob0, q0, kv0],
    )
    _, dkv, l1 = call(mark_kernel, [sds(1, 128, dtype=F32)], [rows0], through=[dkv, l1])
    dkv = exchange(dkv)
    gfm0, gfo0, gub0, ob10 = call(
        grad_ffn_kernel, grad_ffn_outs, [n20, dx1, dpre0, act0], after=rows0
    )
    gfr0 = swap_cores(gfo0)
    gam1, gao1 = call(
        grad_attn_kernel, grad_attn_outs, [n11, bg1, att1, dproj1], after=rows0
    )
    gar1 = swap_cores(gao1)
    (l0,) = call(join_kernel, [message(16, 128, 768)], [gfm0, gfr0, gam1, gar1])
    dproj0, part, gib0, l0 = call(
        project_back_kernel, project_outs, [dkv, dq0, am[0], ao[0]], through=[l0]
    )
    l0 = exchange(l0)
    backs = all_parts(part)
    gam0, gao0 = call(grad_attn_kernel, grad_attn_outs, [n10, bg0, att0, dproj0])
    gar0 = swap_cores(gao0)
    half = (yh.astype(jnp.int32).reshape(1), None, None)
    (acts,) = call(line_up_kernel, [sds(2, 2 * ROWS, D)], [half, acts, far], us=1)
    keep, send, msg, acts = call(
        last_kernel,
        [sds(ROWS, D), sds(ROWS, D), message(16, 144, 256)],
        [core, dx1, x, dmid0, *backs, lnp, gam0, gar0, rows0, ob10, gib0, gub0, head1, rows1, ob11, gib1, gub1],
        through=[acts],
    )
    tail = exchange(msg)
    (grads,) = call(pair_kernel, [sds(2, ROWS, D)], [core, keep, swap_cores(send)], us=1)
    (grads,) = call(line_up_kernel, [sds(2, 2 * ROWS, D)], [half, grads, other_half(grads)], us=1)
    f = functools.partial(sds, dtype=F32)
    fk, send, at1 = call(
        settle_kernel, [f(128, 512), f(128, 512), f(128, 256)], [core, *[pltpu.with_memory_space_constraint(v, pltpu.HBM) for v in (l0, l1)]],
    )
    fg = swap_cores(send)
    ak, send = call(settle_tail_kernel, [f(136, 256), f(136, 256)], [core, tail, at1])
    gq, go, gu, gd, gg, gs, gi, gb, gub = call(
        unpack_kernel,
        [f(3, 128, 128), f(128, 128), f(128, 512), f(512, 128), f(2, 128), f(2, 128), f(2, 128), f(2, 128), f(1, 512)],
        [core, fk, fg, ak, swap_cores(send)],
    )
    return (
        acts[None, :, None], grads[None, :, None], jnp.moveaxis(gq, 0, 1)[None], go[None], gu[None], gd[None],
        gg[None], gs[None], gi[None], gb[None], gub,
    )


def solution(mesh):
    parts = Mesh(mesh.devices.reshape(2, 4, 2, 2, 4), ("s", "z", "yl", "yh", "x"))
    dp, tp = ("z", "yl"), ("yh", "x")
    return jax.shard_map(
        local,
        mesh=parts,
        in_specs=(
            P(None, None, dp, None),
            P(None, None, dp, None),
            P("s", dp, None, tp),
            P("s", tp, dp),
            P("s", dp, tp),
            P("s", tp, dp),
            P("s", None, dp),
            P("s", None, dp),
            P("s", None, tp),
            P("s", None, dp),
            P("s", tp),
        ),
        out_specs=(
            P("s", None, None, dp, None),
            P("s", None, None, dp, None),
            P("s", dp, None, tp),
            P("s", tp, dp),
            P("s", dp, tp),
            P("s", tp, dp),
            P("s", None, dp),
            P("s", None, dp),
            P("s", None, tp),
            P("s", None, dp),
            P("s", tp),
        ),
        check_vma=False,
    )
```

```python
import functools
import math

import jax
import jax.numpy as jnp
from jax import lax
from jax.experimental import pallas as pl
from jax.experimental.pallas import tpu as pltpu
from jax.sharding import Mesh, PartitionSpec as P

EPSILON = 1e-05
MASKED = -1e30
SCALE = 1.0 / math.sqrt(64)
BF = jnp.bfloat16
F32 = jnp.float32
CHIPS = ("z", "yl", "yh")
ROWS = 64
D = 1024


def sds(*shape, dtype=BF):
    return jax.ShapeDtypeStruct(shape, dtype)


def kept(*shape, dtype=BF):
    return ("kept", pltpu.HBM(shape, dtype))


def message(*shape):
    return pltpu.HBM(shape, BF)


def fan(rows, columns):
    return ("fan", pltpu.HBM((16, rows, columns), BF))


class Source:
    def __init__(self, copies, held):
        self.copies, self.held = copies, held
        self.shape, self.dtype = held.shape, held.dtype

    def __getitem__(self, at):
        key = at[1] if isinstance(at, tuple) and len(at) > 1 else at
        if isinstance(key, int) and key in self.copies:
            self.copies.pop(key).wait()
        elif not isinstance(key, int) or None in self.copies:
            self.settle()
        return self.held[at]

    def settle(self):
        for key in list(self.copies):
            self.copies.pop(key).wait()


class Sink:
    def __init__(self, place, held, next_sem, copies):
        self.place, self.held, self.next_sem = place, held, next_sem
        self.copies, self.sent, self.shape = copies, [], held.shape

    def __setitem__(self, at, value):
        self.held[at] = value

    def __getitem__(self, at):
        return self.held[at]

    def send(self, at=None):
        source = self.held if at is None else self.held.at[at]
        for g in range(self.copies):
            if self.copies > 1:
                place = self.place.at[g] if at is None else self.place.at[g, at]
            else:
                place = self.place if at is None else self.place.at[at]
            copy = pltpu.make_async_copy(source, place, self.next_sem())
            copy.start()
            self.sent.append(copy)

    def settle(self):
        for copy in self.sent:
            copy.wait()


def call_early(kernel, outs, ins, us=3, through=(), after=None, more=0):
    m, k = len(outs), len(through)
    kinds = [o[0] if isinstance(o, tuple) else "" for o in outs]
    outs = [o[1] if isinstance(o, tuple) else o for o in outs]
    specs, arrays, scratch, windows = [], [], [], []
    for item in ins:
        array, block, index = item if isinstance(item, tuple) else (item, item.shape, None)
        arrays.append(array)
        if block is None:
            specs.append(pl.BlockSpec(memory_space=pltpu.SMEM))
            windows.append(None)
            continue
        if index is None and jax.typeof(array).memory_space is not pltpu.HBM:
            specs.append(pl.BlockSpec(memory_space=pltpu.VMEM))
            windows.append(None)
            continue
        specs.append(pl.BlockSpec(memory_space=pl.ANY))
        index = index or (0,) * len(block)
        windows.append(tuple(slice(i * b, i * b + b) for i, b in zip(index, block)))
        scratch.append(pltpu.VMEM(block, array.dtype))
    out_specs = []
    for kind, o in zip(kinds, outs):
        if isinstance(o, jax.ShapeDtypeStruct):
            out_specs.append(pl.BlockSpec(memory_space=pltpu.VMEM))
            continue
        out_specs.append(pl.BlockSpec(memory_space=pl.ANY))
        scratch.append(pltpu.VMEM(o.shape[1:] if kind == "fan" else o.shape, o.dtype))
    sem_count = more + sum(16 if kind == "fan" else 1 for kind in kinds)
    for window, array in zip(windows, arrays):
        if window is not None:
            sem_count += 2 if len(window) == 4 else 4 if array.shape == (4, ROWS, D) else 1
    extra = list(through) + ([] if after is None else [after])
    n, e = len(ins), len(ins) + len(extra)

    def body(*refs):
        held, sems = list(refs[e + m + k : -1]), refs[-1]
        used = []

        def next_sem():
            used.append(None)
            return sems.at[len(used) - 1]

        operands = []
        for ref, window in zip(refs[:n], windows):
            if window is None:
                operands.append(ref)
                continue
            place = held.pop(0)
            if len(window) == 4:
                keys = {i: (slice(None), i) for i in range(2)}
            elif place.shape == (4, ROWS, D):
                keys = {i: (i,) for i in range(4)}
            else:
                keys = {None: ()}
            copies = {}
            for key, at in keys.items():
                if len(window) == 4:
                    source = ref.at[window[0], key, window[2], window[3]]
                elif key is None:
                    source = ref.at[window]
                else:
                    source = ref.at[key]
                copies[key] = pltpu.make_async_copy(
                    source, place.at[at] if at else place, next_sem()
                )
                copies[key].start()
            operands.append(Source(copies, place))
        sinks = [
            ref
            if isinstance(o, jax.ShapeDtypeStruct)
            else Sink(ref, held.pop(0), next_sem, 16 if kind == "fan" else 1)
            for kind, o, ref in zip(kinds, outs, refs[e : e + m])
        ]
        kernel(*operands, *sinks)
        sinks = [o for o in sinks if isinstance(o, Sink)]
        for o in operands:
            if isinstance(o, Source):
                o.settle()
        for o in sinks:
            if not o.sent:
                o.send()
        for o in sinks:
            o.settle()

    results = pl.pallas_call(
        body,
        out_shape=list(outs) + [pltpu.HBM(t.shape, t.dtype) for t in through],
        in_specs=specs + [pl.BlockSpec(memory_space=pl.ANY)] * len(extra),
        out_specs=out_specs + [pl.BlockSpec(memory_space=pl.ANY)] * k,
        input_output_aliases={n + i: m + i for i in range(k)},
        scratch_shapes=scratch + [pltpu.SemaphoreType.DMA((sem_count,))],
        compiler_params=pltpu.CompilerParams(vmem_limit_bytes=48 * 1024 * 1024),
        cost_estimate=pl.CostEstimate(
            flops=0, bytes_accessed=us * 3_000_000, transcendentals=0
        ),
    )(
        *arrays,
        *[pltpu.with_memory_space_constraint(t, pltpu.HBM) for t in through],
        *([] if after is None else [after]),
    )
    return [
        pltpu.with_memory_space_constraint(r, pltpu.HBM) if kind == "kept" else r
        for kind, r in zip(kinds + [""] * k, results)
    ]


def call(kernel, outs, ins, us=3, through=(), after=None):
    n, m, k = len(ins), len(outs), len(through)
    e = n + (after is not None)
    held = [i for i, o in enumerate(outs) if isinstance(o, tuple)]
    outs = [o[1] if isinstance(o, tuple) else o for o in outs]
    specs, arrays = [], []
    for item in ins:
        if isinstance(item, tuple):
            array, block, index = item
            if block is None:
                specs.append(pl.BlockSpec(memory_space=pltpu.SMEM))
            else:
                specs.append(
                    pl.BlockSpec(
                        block,
                        functools.partial(lambda at, i: at, index),
                        pipeline_mode=pl.Buffered(1),
                    )
                )
        else:
            array = item
            specs.append(
                pl.BlockSpec(
                    array.shape,
                    functools.partial(lambda n, i: (0,) * n, array.ndim),
                    pipeline_mode=pl.Buffered(1),
                )
            )
        arrays.append(array)
    if after is not None:
        specs.append(pl.BlockSpec(memory_space=pl.ANY))
        arrays.append(after)
    out_specs = [
        pl.BlockSpec(o.shape, functools.partial(lambda n, i: (0,) * n, len(o.shape)))
        for o in outs
    ]

    def body(*refs):
        kernel(*refs[:n], *refs[e + k : e + k + m])

    results = pl.pallas_call(
        body,
        grid=(1,),
        out_shape=list(outs) + [pltpu.HBM(t.shape, t.dtype) for t in through],
        in_specs=specs + [pl.BlockSpec(memory_space=pl.ANY)] * k,
        out_specs=out_specs + [pl.BlockSpec(memory_space=pl.ANY)] * k,
        input_output_aliases={e + i: m + i for i in range(k)},
        compiler_params=pltpu.CompilerParams(vmem_limit_bytes=48 * 1024 * 1024),
        cost_estimate=pl.CostEstimate(
            flops=0, bytes_accessed=us * 3_000_000, transcendentals=0
        ),
    )(*arrays, *[pltpu.with_memory_space_constraint(t, pltpu.HBM) for t in through])
    return [
        pltpu.with_memory_space_constraint(r, pltpu.HBM) if i in held else r
        for i, r in enumerate(results)
    ]


def send(ref, at=None):
    if isinstance(ref, Sink):
        ref.send(at)


def fill(msg, rows, columns, value):
    if isinstance(msg, Sink):
        msg[rows, columns] = value
    else:
        for g in range(16):
            msg[g, rows, columns] = value


def nn(a, b):
    return jnp.dot(a, b, preferred_element_type=F32)


def nt(a, b):
    return lax.dot_general(a, b, (((1,), (1,)), ((), ())), preferred_element_type=F32)


def tn(a, b):
    return lax.dot_general(a, b, (((0,), (0,)), ((), ())), preferred_element_type=F32)


def heads():
    return [(k, side, yh) for k, (side, yh) in enumerate([(0, 0), (0, 1), (1, 0), (1, 1)])]


def attn_tile(ref, yh):
    return ref[:, yh, 0:128, :].reshape(D, 256)


def out_tile(ref, yh):
    return ref[:, yh, :, :].reshape(D, 128)


def ffn_tile(ref, yh, part):
    return ref[:, yh, 0:128, part * 256 : part * 256 + 256].reshape(D, 256)


def low_half(v):
    lane = lax.broadcasted_iota(jnp.int32, v.shape, 1)
    return jnp.where(lane < 64, v, 0.0)


def high_half(v):
    lane = lax.broadcasted_iota(jnp.int32, v.shape, 1)
    return jnp.where(lane >= 64, v, 0.0)


def mean_of(v):
    return jnp.sum(v, axis=-1, keepdims=True) * (1.0 / D)


def normal(v):
    centred = v - mean_of(v)
    inverse = lax.rsqrt(mean_of(centred * centred) + EPSILON)
    return centred * inverse, inverse


def layer_norm(v, gain, shift):
    return normal(v)[0] * gain + shift


def layer_norm_back(v, gain, grad):
    xhat, inverse = normal(v)
    d = grad * gain
    back = inverse * (d - mean_of(d) - xhat * mean_of(d * xhat))
    return (
        back,
        jnp.sum(grad * xhat, axis=0, keepdims=True),
        jnp.sum(grad, axis=0, keepdims=True),
    )


def gelu(u):
    return 0.5 * u * (1.0 + jnp.tanh(0.7978845608028654 * (u + 0.044715 * u * u * u)))


def gelu_slope(u):
    t = jnp.tanh(0.7978845608028654 * (u + 0.044715 * u * u * u))
    return 0.5 * (1.0 + t) + 0.5 * u * (1.0 - t * t) * (
        0.7978845608028654 * (1.0 + 3.0 * 0.044715 * u * u)
    )


def total(parts):
    a, b, c, d = [p[...].astype(F32) for p in parts]
    return (a + b) + (c + d)


def ln_row(lnp, layer, which, kind):
    return lnp[which, layer * 8 + 4 + kind : layer * 8 + 5 + kind, :]


def project(x, lnp, bias, wm, wo, layer, n1, q, kv):
    normed = layer_norm(x, ln_row(lnp, layer, 0, 0), ln_row(lnp, layer, 0, 1)).astype(BF)
    n1[...] = normed
    send(n1)
    at = kv.shape[-2] - ROWS
    for k, side, yh in heads():
        tile = nn(normed, attn_tile((wm, wo)[side], yh))
        tile = tile + bias[yh, layer * 8 + side : layer * 8 + side + 1, :]
        q[k] = low_half(tile[:, 128:]).astype(BF)
        fill(kv, slice(at, at + ROWS), slice(k * 128, k * 128 + 128), tile[:, :128].astype(BF))
    send(kv, slice(at, at + ROWS))


def pack_kernel(core, *refs):
    sources, (keep, send), held, sem = refs[:9], refs[9:11], refs[11:20], refs[20]
    copies = [
        pltpu.make_async_copy(a, b, sem.at[i]) for i, (a, b) in enumerate(zip(sources, held))
    ]
    for c in copies:
        c.start()
    for c in copies:
        c.wait()
    pack(core, *held, keep, send)


def pack(core, qkv, out, up, down, gain, shift, inb, outb, upb, keep, send):
    wt = out[...].astype(F32).T
    dt = down[...].astype(F32).T
    inb_, gain_, shift_, outb_ = [r[...].astype(F32) for r in (inb, gain, shift, outb)]
    upb_ = upb[...].astype(F32)
    zero = jnp.zeros((1, 64), F32)
    def flat(v):
        return jnp.concatenate([v[0:1], v[1:2]], axis=1)
    rows = []
    for j in range(2):
        cols = slice(j * 64, j * 64 + 64)
        rows.append(jnp.concatenate([zero, inb_[1:2, cols], inb_[0:1, cols], zero], axis=1))
    ups = [upb_[:, :256], upb_[:, 256:]]
    rest = [flat(gain_), flat(shift_), flat(outb_), jnp.zeros((9, 256), F32)]
    halves = []
    for j in range(2):
        cols = slice(j * 64, j * 64 + 64)
        wide = slice(j * 256, j * 256 + 256)
        halves.append(
            (
                up[:, wide].astype(F32),
                dt[:, wide],
                jnp.concatenate([qkv[i, :, cols].astype(F32) for i in (1, 2, 0)] + [wt[:, cols]], axis=1),
                jnp.concatenate([rows[j], rows[1 - j], ups[j], ups[1 - j], *rest]),
            )
        )
    first = core[0] == 0
    for ref, pair in ((keep, halves), (send, halves[::-1])):
        values = [jnp.where(first, a, b).astype(BF) for a, b in zip(*pair)]
        ref[0:128, 0:256] = values[0]
        ref[0:128, 256:512] = values[1]
        ref[0:128, 512:768] = values[2]
        ref[128:144, 512:768] = values[3]


def spread_kernel(core, keep, got, msg, ffn0, ffn1):
    first = core[0] == 0
    k, o = keep[...], got[...]
    lower, upper = jnp.where(first, k, o), jnp.where(first, o, k)
    small = jnp.concatenate(
        [v[128:144, 512:768].astype(F32)[0:8] for v in (lower, upper)]
    ).astype(BF)
    tiles = lower[0:128, 512:768], upper[0:128, 512:768]
    msg[0:128, :] = tiles[0]
    msg[128:256, :] = tiles[1]
    msg[256:272, :] = small
    msg.send()
    ffn0[...] = lower[0:128, 0:512]
    ffn1[...] = upper[0:128, 0:512]


def first_kernel(x, params, wm, wo, piece, n1, q, msg, lnp, bias):
    for layer in range(2):
        part = slice(layer * 8, layer * 8 + 8)
        blocks = [params[d, 0].astype(F32)[part] for d in range(8)]
        for half in range(2):
            cols = slice(half * 128, half * 128 + 128)
            lnp[half, part, :] = jnp.concatenate([b[:, cols] for b in blocks], axis=1)
        for yh in range(2):
            bias[yh, part, :] = params[0, yh].astype(F32)[part]
    msg[0:128, :] = piece[...]
    msg.send(slice(0, 128))
    project(x[...].astype(F32), lnp, bias, wm, wo, 0, n1, q, msg)


def next_kernel(mid, p0, p1, p2, p3, lnp, bias, wm, wo, y, n1, q, msg):
    out = (mid[...] + (total((p0, p1, p2, p3)) + ln_row(lnp, 0, 1, 2))).astype(BF)
    y[...] = out
    project(out.astype(F32), lnp, bias, wm, wo, 1, n1, q, msg)


def attend_spread_kernel(first, q, kv, wm, wo, piece, part, prob, att, copies):
    copies[...] = piece[...]
    copies.send()
    attend_kernel(first, q, kv, wm, wo, part, prob, att)


def attend_kernel(first, q, kv, wm, wo, part, prob, att):
    length = 16 * ROWS
    qpos = first[0] + lax.broadcasted_iota(jnp.int32, (ROWS, length), 0)
    kpos = lax.broadcasted_iota(jnp.int32, (ROWS, length), 1)
    allowed = kpos <= qpos
    acc = None
    for k, side, yh in heads():
        pair = kv[:, :, k * 128 : k * 128 + 128].reshape(length, 128)
        scores = jnp.where(allowed, nt(q[k], pair) * SCALE, MASKED)
        e = jnp.exp(scores - jnp.max(scores, axis=-1, keepdims=True))
        p = e / jnp.sum(e, axis=-1, keepdims=True)
        prob[k] = p
        send(prob, k)
        mixed = high_half(nn(p.astype(BF), pair)).astype(BF)
        att[k] = mixed
        term = nt(mixed, out_tile((wm, wo)[side], yh))
        acc = term if acc is None else acc + term
    part[...] = acc.astype(BF)


def feed(x, parts, lnp, bias, wm, wo, layer, part, mid, n2, pre, act):
    middle = x[...].astype(F32) + (total(parts) + ln_row(lnp, layer, 0, 2))
    mid[...] = middle
    send(mid)
    normed = layer_norm(middle, ln_row(lnp, layer, 1, 0), ln_row(lnp, layer, 1, 1)).astype(BF)
    n2[...] = normed
    send(n2)
    acc = None
    for k, side, yh in heads():
        w = (wm, wo)[side]
        u = nn(normed, ffn_tile(w, yh, 0))
        u = u + bias[yh, layer * 8 + 2 + side : layer * 8 + 3 + side, :]
        pre[k] = u
        a = gelu(u).astype(BF)
        act[k] = a
        term = nt(a, ffn_tile(w, yh, 1))
        acc = term if acc is None else acc + term
    part[...] = acc.astype(BF)


def feed_back(g, pre, wm, wo, dpre, part):
    acc = None
    for k, side, yh in heads():
        w = (wm, wo)[side]
        d = (nn(g, ffn_tile(w, yh, 1)) * gelu_slope(pre[k])).astype(BF)
        dpre[k] = d
        term = nt(d, ffn_tile(w, yh, 0))
        acc = term if acc is None else acc + term
    part[...] = acc.astype(BF)


def feed_kernel(x, p0, p1, p2, p3, lnp, bias, wm, wo, part, mid, n2, pre, act):
    feed(x, (p0, p1, p2, p3), lnp, bias, wm, wo, 0, part, mid, n2, pre, act)


def turn_kernel(x, p0, p1, p2, p3, lnp, bias, wm, wo, g, part, mid, n2, pre, act, dpre, back):
    feed(x, (p0, p1, p2, p3), lnp, bias, wm, wo, 1, part, mid, n2, pre, act)
    feed_back(g[...], pre, wm, wo, dpre, back)


def by_section(core, a, b, keep, send):
    first = core[0] == 0
    keep[...] = jnp.where(first, a, b)
    send[...] = jnp.where(first, b, a)


def finish_kernel(core, y0, mid, p0, p1, p2, p3, lnp, keep, send):
    y1 = (mid[...] + (total((p0, p1, p2, p3)) + ln_row(lnp, 1, 1, 2))).astype(BF)
    by_section(core, y0[...], y1, keep, send)


def pair_kernel(core, keep, got, rows):
    first = core[0] == 0
    k, g = keep[...], got[...]
    rows[0] = jnp.where(first, k, g)
    rows[1] = jnp.where(first, g, k)


def line_up_kernel(half, rows, far, out):
    first = half[0] == 0
    k, g = rows[...], far[...]
    out[:, 0:ROWS, :] = jnp.where(first, k, g)
    out[:, ROWS:, :] = jnp.where(first, g, k)


def grad_ffn_kernel(n2, g, dpre, act, mine, other, sums, row):
    first, second = n2[...].T, g[...].T
    for k, side, yh in heads():
        out = (mine, other)[side]
        out[:, yh, :, 0:256] = nn(first, dpre[k]).astype(BF).reshape(8, 128, 256)
        out[:, yh, :, 256:512] = nn(second, act[k]).astype(BF).reshape(8, 128, 256)
        sums[k : k + 1, :] = jnp.sum(dpre[k].astype(F32), axis=0, keepdims=True)
    row[...] = jnp.sum(g[...].astype(F32), axis=0, keepdims=True)


def attend_back(layer, g, mid, parts, lnp, wm, wo, prob, q, kv, dmid, bg, dq, dkv, rows):
    back, gg, gs = layer_norm_back(mid[...], ln_row(lnp, layer, 1, 0), total(parts))
    dm = g[...].astype(F32) + back
    dmid[...] = dm
    send(dmid)
    low = dm.astype(BF)
    bg[...] = low
    send(bg)
    rows[0:1, :] = gg
    rows[1:2, :] = gs
    rows[2:3, :] = jnp.sum(low.astype(F32), axis=0, keepdims=True)
    for k, side, yh in heads():
        pair = kv[:, :, k * 128 : k * 128 + 128].reshape(16 * ROWS, 128)
        da = high_half(nn(low, out_tile((wm, wo)[side], yh))).astype(BF)
        p = prob[k]
        dp = nt(da, pair)
        ds = (p * (dp - jnp.sum(p * dp, axis=-1, keepdims=True))).astype(BF)
        dq[k] = low_half(nn(ds, pair) * SCALE).astype(BF)
        both = tn(ds, q[k]) * SCALE + tn(p.astype(BF), da)
        dkv[:, :, k * 128 : k * 128 + 128] = both.astype(BF).reshape(16, ROWS, 128)


def attend_back_kernel(g, mid, p0, p1, p2, p3, lnp, wm, wo, prob, q, kv, dmid, bg, dq, dkv, rows):
    attend_back(1, g, mid, (p0, p1, p2, p3), lnp, wm, wo, prob, q, kv, dmid, bg, dq, dkv, rows)


def attend_back_first_kernel(
    g, mid, p0, p1, p2, p3, lnp, wm, wo, prob, q, kv, dmid, bg, dq, dkv, rows
):
    attend_back(0, g, mid, (p0, p1, p2, p3), lnp, wm, wo, prob, q, kv, dmid, bg, dq, dkv, rows)


def add_into(msg, at, gm, gr):
    for i in range(8):
        for j in range(2):
            msg[2 * i + j, 0:128, at : at + gm.shape[3]] = gm[i, j] + gr[i, j]


def add_kernel(gm, gr, msg):
    msg[...] = (gm[...] + gr[...]).reshape(4, 128, 512)


def add_in_steps(gm, gr):
    block = pl.BlockSpec((2, 2, 128, 512), lambda i: (i, 0, 0, 0))
    return pl.pallas_call(
        add_kernel,
        grid=(4,),
        out_shape=message(16, 128, 512),
        in_specs=[block, block],
        out_specs=pl.BlockSpec((4, 128, 512), lambda i: (i, 0, 0)),
        compiler_params=pltpu.CompilerParams(vmem_limit_bytes=16 * 1024 * 1024),
        cost_estimate=pl.CostEstimate(flops=0, bytes_accessed=9_000_000, transcendentals=0),
    )(gm, gr)


def join_kernel(fm, fr, am, ar, msg):
    add_into(msg, 0, fm, fr)
    add_into(msg, 512, am, ar)


def mark_kernel(rows, out):
    out[...] = rows[0:1, 0:128]


def project_back_kernel(dkv, dq, wm, wo, dproj, part, sums):
    pairs = jnp.sum(dkv[...].astype(F32), axis=0).astype(BF)
    acc = None
    for k, side, yh in heads():
        tile = jnp.concatenate([pairs[:, k * 128 : k * 128 + 128], dq[k]], axis=1)
        dproj[k] = tile
        sums[k : k + 1, :] = jnp.sum(tile.astype(F32), axis=0, keepdims=True)
        term = nt(tile, attn_tile((wm, wo)[side], yh))
        acc = term if acc is None else acc + term
    part[...] = acc.astype(BF)


def grad_attn_kernel(n1, bg, att, dproj, mine, other):
    left, right = n1[...].T, bg[...].T
    for k, side, yh in heads():
        out = (mine, other)[side]
        first = nn(left, dproj[k])
        second = nn(right, att[k])
        out[:, yh, :, 0:128] = first[:, :128].astype(BF).reshape(8, 128, 128)
        out[:, yh, :, 128:] = (first[:, 128:] + second).astype(BF).reshape(8, 128, 128)


def hand_down_kernel(x, dmid, p0, p1, p2, p3, lnp, pre, wm, wo, dx, dpre, part, rows):
    back, gg, gs = layer_norm_back(
        x[...].astype(F32), ln_row(lnp, 1, 0, 0), total((p0, p1, p2, p3))
    )
    g = (dmid[...] + back).astype(BF)
    dx[...] = g
    rows[0:1, :] = gg
    rows[1:2, :] = gs
    feed_back(g, pre, wm, wo, dpre, part)


def last_kernel(
    core, dx1, x, dmid, p0, p1, p2, p3, lnp, gm, gr,
    r0, o0, a0, u0, h1, r1, o1, a1, u1, keep, send, msg,
):
    back, gg, gs = layer_norm_back(
        x[...].astype(F32), ln_row(lnp, 0, 0, 0), total((p0, p1, p2, p3))
    )
    by_section(core, (dmid[...] + back).astype(BF), dx1[...], keep, send)
    lines = []
    for first, rows, ob, a, u in (
        ((gg, gs), r0, o0, a0, u0),
        ((h1[0:1, :], h1[1:2, :]), r1, o1, a1, u1),
    ):
        lines.append(
            (
                a[...],
                u[...],
                (
                    (first[0], rows[0:1, :]),
                    (first[1], rows[1:2, :]),
                    (rows[2:3, :], ob[...]),
                ),
            )
        )
    for d in range(8):
        cols = slice(d * 128, d * 128 + 128)
        for yh in range(2):
            block = []
            for a, u, pairs in lines:
                block += [a[yh : yh + 1], a[2 + yh : 3 + yh], u[yh : yh + 1], u[2 + yh : 3 + yh]]
                block += [jnp.concatenate([f[:, cols], s[:, cols]], axis=1) for f, s in pairs]
            block.append(jnp.zeros((2, 256), F32))
            g = 2 * d + yh
            msg[g, 0:128, :] = (gm[d, yh].astype(F32) + gr[d, yh].astype(F32)).astype(BF)
            msg[g, 128:144, :] = jnp.concatenate(block).astype(BF)


def settle_kernel(core, l0, l1, keep, send, attn):
    first = core[0] == 0
    for j in range(2):
        cols = slice(j * 256, j * 256 + 256)
        a = jnp.sum(l0[:, :, cols].astype(F32), axis=0)
        b = jnp.sum(l1[:, :, cols].astype(F32), axis=0)
        keep[:, cols] = jnp.where(first, a, b)
        send[:, cols] = jnp.where(first, b, a)
    attn[...] = jnp.sum(l0[:, :, 512:768].astype(F32), axis=0)


def settle_tail_kernel(core, tail, attn, keep, send):
    first = core[0] == 0
    t = jnp.sum(tail[...].astype(F32), axis=0)
    a, b = t[0:128], attn[...]
    small = t[128:144]
    pad = jnp.zeros((1, 256), F32)
    c, d = jnp.concatenate([small[0:7], pad]), jnp.concatenate([small[7:14], pad])
    keep[0:128, :] = jnp.where(first, a, b)
    send[0:128, :] = jnp.where(first, b, a)
    keep[128:136, :] = jnp.where(first, c, d)
    send[128:136, :] = jnp.where(first, d, c)


def unpack_kernel(
    core, fk, fg, ak, ag, qkv, out, up, down, gain, shift, inb, outb, upb
):
    first = core[0] == 0

    def ordered(k, g):
        return jnp.where(first, k, g), jnp.where(first, g, k)

    a = ordered(ak[0:128, :], ag[0:128, :])
    for i, at in enumerate((128, 0, 64)):
        qkv[i] = jnp.concatenate([t[:, at : at + 64] for t in a], axis=1)
    out[...] = jnp.concatenate([t[:, 192:256] for t in a], axis=1).T
    ups = ordered(fk[:, 0:256], fg[:, 0:256])
    downs = ordered(fk[:, 256:512], fg[:, 256:512])
    for j in range(2):
        up[:, j * 256 : j * 256 + 256] = ups[j]
        down[j * 256 : j * 256 + 256, :] = downs[j].T
    s0, s1 = ordered(ak[128:136, :], ag[128:136, :])
    for row, ref in ((4, gain), (5, shift), (6, outb)):
        t = s0[row : row + 1] + s1[row : row + 1]
        ref[0:1, :] = t[:, 0:128]
        ref[1:2, :] = t[:, 128:256]
    sides = [s0[0:1] + s1[1:2], s0[1:2] + s1[0:1]]
    inb[0:1, :] = jnp.concatenate([t[:, 128:192] for t in sides], axis=1)
    inb[1:2, :] = jnp.concatenate([t[:, 64:128] for t in sides], axis=1)
    upb[...] = jnp.concatenate([s0[2:3] + s1[3:4], s0[3:4] + s1[2:3]], axis=1)


def swap_cores(v):
    return lax.ppermute(v, "s", [(0, 1), (1, 0)])


def all_parts(part):
    got = [lax.ppermute(part, "x", [(i, i ^ k) for i in range(4)]) for k in (1, 3, 2)]
    return [part, got[0], got[2], got[1]]


def exchange(v, axes=CHIPS):
    return lax.all_to_all(v, axes, 0, 0, tiled=True)


def by_layer(mine, first, second):
    return jnp.where(mine == 0, first, second)


def other_half(v):
    return lax.ppermute(v, "yh", [(0, 1), (1, 0)])


def local(inputs, cotangent, wqkv, wout, wup, wdown, gain, shift, inb, outb, upb):
    s, yh = lax.axis_index("s"), lax.axis_index("yh")
    first = (lax.axis_index(CHIPS) * ROWS).astype(jnp.int32).reshape(1)

    def own_rows(v):
        return lax.dynamic_slice(v, (s, 0, yh * ROWS, 0), (1, 1, ROWS, D)).reshape(ROWS, D)

    x, cot = own_rows(inputs), own_rows(cotangent)
    core = (s.astype(jnp.int32).reshape(1), None, None)
    weights = [
        jnp.moveaxis(wqkv[0], 1, 0), wout[0], wup[0], wdown[0],
        gain[0], shift[0], inb[0], outb[0], upb,
    ]
    keep, send = pl.pallas_call(
        pack_kernel,
        out_shape=[sds(144, 768), sds(144, 768)],
        in_specs=[pl.BlockSpec(memory_space=pltpu.SMEM)]
        + [pl.BlockSpec(memory_space=pl.ANY)] * 9,
        out_specs=[pl.BlockSpec(memory_space=pltpu.VMEM)] * 2,
        scratch_shapes=[pltpu.VMEM(w.shape, BF) for w in weights]
        + [pltpu.SemaphoreType.DMA((9,))],
        compiler_params=pltpu.CompilerParams(vmem_limit_bytes=48 * 1024 * 1024),
    )(core[0], *[pltpu.with_memory_space_constraint(w, pltpu.HBM) for w in weights])
    msg, piece0, piece1 = call_early(
        spread_kernel,
        [fan(272, 256), sds(128, 512), sds(128, 512)],
        [core, keep, swap_cores(send)],
    )
    u = exchange(msg).reshape(8, 2, 272, 256)
    uo = swap_cores(u)
    am = [(u, (8, 2, 128, 256), (0, 0, l, 0)) for l in range(2)]
    ao = [(uo, (8, 2, 128, 256), (0, 0, l, 0)) for l in range(2)]
    outm = [(u, (8, 2, 128, 128), (0, 0, l, 1)) for l in range(2)]
    outo = [(uo, (8, 2, 128, 128), (0, 0, l, 1)) for l in range(2)]
    kinds = dict(n1=kept(ROWS, D), q=kept(4, ROWS, 128))
    n10, q0, msg, lnp, bias = call_early(
        first_kernel,
        [kinds["n1"], kinds["q"], fan(192, 512), kept(2, 16, D, dtype=F32), kept(2, 16, 256, dtype=F32)],
        [x, (u, (8, 2, 16, 256), (0, 0, 16, 0)), am[0], ao[0], piece0],
        more=16,
    )
    got0 = exchange(msg)
    kv0 = (got0, (16, ROWS, 512), (0, 2, 0))
    f0 = (got0.reshape(8, 2, 192, 512), (8, 2, 128, 512), (0, 0, 0, 0))
    f0o = (swap_cores(got0).reshape(8, 2, 192, 512), (8, 2, 128, 512), (0, 0, 0, 0))
    attend_outs = [sds(ROWS, D), kept(4, ROWS, D, dtype=F32), kept(4, ROWS, 128)]
    feed_outs = [
        sds(ROWS, D), kept(ROWS, D, dtype=F32), kept(ROWS, D),
        kept(4, ROWS, 256, dtype=F32), kept(4, ROWS, 256),
    ]
    part, prob0, att0, copies = call_early(
        attend_spread_kernel,
        attend_outs + [fan(128, 512)],
        [(first, None, None), q0, kv0, outm[0], outo[0], piece1],
        more=3,
    )
    f1 = exchange(copies)
    part, mid0, n20, pre0, act0 = call_early(
        feed_kernel, feed_outs, [x, *all_parts(part), lnp, bias, f0, f0o]
    )
    y0, n11, q1, msg, f1 = call(
        next_kernel,
        [sds(ROWS, D), kinds["n1"], kinds["q"], message(16, ROWS, 512)],
        [mid0, *all_parts(part), lnp, bias, am[1], ao[1]],
        through=[f1],
    )
    f1 = f1.reshape(8, 2, 128, 512)
    f1o = swap_cores(f1)
    kv1 = exchange(msg)
    part, prob1, att1 = call_early(attend_kernel, attend_outs, [(first, None, None), q1, kv1, outm[1], outo[1]], more=3)
    last_part, mid1, n21, pre1, act1, dpre1, back = call(
        turn_kernel,
        [message(ROWS, D), *feed_outs[1:], kept(4, ROWS, 256), sds(ROWS, D)],
        [y0, *all_parts(part), lnp, bias, f1, f1o, cot],
    )
    backs = all_parts(back)
    grad_ffn_outs = [
        kept(8, 2, 128, 512), sds(8, 2, 128, 512), kept(4, 256, dtype=F32), kept(1, D, dtype=F32)
    ]
    back_outs = [kept(ROWS, D, dtype=F32), kept(ROWS, D), kept(4, ROWS, 128)]
    rows_out = kept(8, D, dtype=F32)
    dmid1, bg1, dq1, dkv, rows1, last_part = call(
        attend_back_kernel,
        back_outs + [message(16, ROWS, 512), rows_out],
        [cot, mid1, *backs, lnp, outm[1], outo[1], prob1, q1, kv1],
        through=[last_part],
    )
    dkv = exchange(dkv)
    gfm1, gfo1, gub1, ob11 = call(
        grad_ffn_kernel, grad_ffn_outs, [n21, cot, dpre1, act1], after=rows1
    )
    gfr1 = swap_cores(gfo1)
    keep, send = call(
        finish_kernel,
        [sds(ROWS, D), sds(ROWS, D)],
        [core, y0, mid1, *all_parts(last_part), lnp],
    )
    (acts,) = call(pair_kernel, [message(2, ROWS, D)], [core, keep, swap_cores(send)], us=1)
    project_outs = [kept(4, ROWS, 256), sds(ROWS, D), kept(4, 256, dtype=F32)]
    dproj1, part, gib1, acts = call(
        project_back_kernel, project_outs, [dkv, dq1, am[1], ao[1]], through=[acts]
    )
    far = other_half(acts)
    backs = all_parts(part)
    grad_attn_outs = [kept(8, 2, 128, 256), sds(8, 2, 128, 256)]
    l1 = add_in_steps(gfm1, gfr1)
    dx1, dpre0, part, head1, l1 = call_early(
        hand_down_kernel,
        [kept(ROWS, D), kept(4, ROWS, 256), sds(ROWS, D), rows_out],
        [y0, dmid1, *backs, lnp, pre0, f0, f0o],
        through=[l1],
        after=far,
    )
    l1 = exchange(l1)
    backs = all_parts(part)
    dmid0, bg0, dq0, dkv, rows0 = call(
        attend_back_first_kernel,
        back_outs + [message(16, ROWS, 512), rows_out],
        [dx1, mid0, *backs, lnp, outm[0], outo[0], prob0, q0, kv0],
    )
    _, dkv, l1 = call(mark_kernel, [sds(1, 128, dtype=F32)], [rows0], through=[dkv, l1])
    dkv = exchange(dkv)
    gfm0, gfo0, gub0, ob10 = call(
        grad_ffn_kernel, grad_ffn_outs, [n20, dx1, dpre0, act0], after=rows0
    )
    gfr0 = swap_cores(gfo0)
    gam1, gao1 = call(
        grad_attn_kernel, grad_attn_outs, [n11, bg1, att1, dproj1], after=rows0
    )
    gar1 = swap_cores(gao1)
    (l0,) = call(join_kernel, [message(16, 128, 768)], [gfm0, gfr0, gam1, gar1])
    dproj0, part, gib0, l0 = call(
        project_back_kernel, project_outs, [dkv, dq0, am[0], ao[0]], through=[l0]
    )
    l0 = exchange(l0)
    backs = all_parts(part)
    gam0, gao0 = call(grad_attn_kernel, grad_attn_outs, [n10, bg0, att0, dproj0])
    gar0 = swap_cores(gao0)
    half = (yh.astype(jnp.int32).reshape(1), None, None)
    (acts,) = call(line_up_kernel, [sds(2, 2 * ROWS, D)], [half, acts, far], us=1)
    keep, send, msg, acts = call(
        last_kernel,
        [sds(ROWS, D), sds(ROWS, D), message(16, 144, 256)],
        [core, dx1, x, dmid0, *backs, lnp, gam0, gar0, rows0, ob10, gib0, gub0, head1, rows1, ob11, gib1, gub1],
        through=[acts],
    )
    tail = exchange(msg)
    (grads,) = call(pair_kernel, [sds(2, ROWS, D)], [core, keep, swap_cores(send)], us=1)
    (grads,) = call(line_up_kernel, [sds(2, 2 * ROWS, D)], [half, grads, other_half(grads)], us=1)
    f = functools.partial(sds, dtype=F32)
    fk, send, at1 = call(
        settle_kernel, [f(128, 512), f(128, 512), f(128, 256)], [core, *[pltpu.with_memory_space_constraint(v, pltpu.HBM) for v in (l0, l1)]],
    )
    fg = swap_cores(send)
    ak, send = call(settle_tail_kernel, [f(136, 256), f(136, 256)], [core, tail, at1])
    gq, go, gu, gd, gg, gs, gi, gb, gub = call(
        unpack_kernel,
        [f(3, 128, 128), f(128, 128), f(128, 512), f(512, 128), f(2, 128), f(2, 128), f(2, 128), f(2, 128), f(1, 512)],
        [core, fk, fg, ak, swap_cores(send)],
    )
    return (
        acts[None, :, None], grads[None, :, None], jnp.moveaxis(gq, 0, 1)[None], go[None], gu[None], gd[None],
        gg[None], gs[None], gi[None], gb[None], gub,
    )


def solution(mesh):
    parts = Mesh(mesh.devices.reshape(2, 4, 2, 2, 4), ("s", "z", "yl", "yh", "x"))
    dp, tp = ("z", "yl"), ("yh", "x")
    return jax.shard_map(
        local,
        mesh=parts,
        in_specs=(
            P(None, None, dp, None),
            P(None, None, dp, None),
            P("s", dp, None, tp),
            P("s", tp, dp),
            P("s", dp, tp),
            P("s", tp, dp),
            P("s", None, dp),
            P("s", None, dp),
            P("s", None, tp),
            P("s", None, dp),
            P("s", tp),
        ),
        out_specs=(
            P("s", None, None, dp, None),
            P("s", None, None, dp, None),
            P("s", dp, None, tp),
            P("s", tp, dp),
            P("s", dp, tp),
            P("s", tp, dp),
            P("s", None, dp),
            P("s", None, dp),
            P("s", None, tp),
            P("s", None, dp),
            P("s", tp),
        ),
        check_vma=False,
    )
```
